32 devices in a mesh: gy: 8 (over z, core), gx: 4 (over y, x).
Axes of the slice: x: 2, y: 2, z: 4, core: 2. Of those that a mesh axis runs over, the one named last changes fastest.
Arguments:
- level_in: bfloat16 [64, 256, 128], P('gy', 'gx'), may hold values from -6 to 6
- w_level: bfloat16 [3, 3, 128, 128], replicated, may hold values from -0.1875 to 0.1875
- w_down: bfloat16 [2, 2, 128, 256], replicated, may hold values from -0.25 to 0.25
- w_neck: bfloat16 [3, 3, 256, 256], replicated, may hold values from -0.125 to 0.125
- cotangent: bfloat16 [32, 128, 256], P('gy', None, 'gx'), may hold values from -6 to 6
Outputs:
- neck_out: bfloat16 [32, 128, 256], P('gy', None, 'gx')
- grad_input: bfloat16 [64, 256, 128], P('gy', 'gx')
- grad_level: bfloat16 [3, 3, 128, 128], replicated
- grad_down: bfloat16 [2, 2, 128, 256], replicated
- grad_neck: bfloat16 [3, 3, 256, 256], replicated
The draws below stay inside these ranges and needn't reach their ends.
All inputs are finite; a program needn't handle non-finite values.
Results may differ from the reference program's by a relative error of at most 0.012.
Values may be sent and summed in bfloat16 or wider, within the bound.
No kernel may reach another device: no remote copies, remote signals or barrier semaphores. Data moves between devices by JAX's collectives and lax.ppermute only.
A program may use at most 64 MiB of HBM per device.

```python
import math
import jax
import jax.numpy as jnp

C4 = 128
CB = 256
H4 = 64
W4 = 256
HB = 32
WB = 128


def block_scale(key, shape, pieces, low, largest):
    gain, own = 1.0, jax.random.fold_in(key, 6)
    for dim, shards_of in pieces:
        steps = jnp.exp(jax.random.uniform(jax.random.fold_in(own, dim), (shards_of,), jnp.float32, low / len(pieces), largest / len(pieces)))
        gain = gain * jnp.repeat(steps, shape[dim] // shards_of).reshape([-1 if axis == dim else 1 for axis in range(len(shape))])
    return gain


def bell_draw(key, dims, width, reach, pieces=(), dtype=jnp.bfloat16):
    values = width * jax.random.normal(key, dims, jnp.float32)
    if pieces:
        values = values * block_scale(key, dims, pieces, -0.22, 0.18)
    return jnp.clip(values, -reach, reach).astype(dtype)


def setup_inputs(seed: int = 0) -> dict:
    key_list = jax.random.split(jax.random.key(seed), 6)
    level_in = bell_draw(key_list[0], (H4, W4, C4), 1.0, 6.0, ((0, 8), (1, 4)))
    w_level = bell_draw(key_list[1], (3, 3, C4, C4), (9 * C4) ** -0.5, 0.1875)
    w_down = bell_draw(key_list[2], (2, 2, C4, CB), (4 * C4) ** -0.5, 0.25)
    w_neck = bell_draw(key_list[3], (3, 3, CB, CB), (9 * CB) ** -0.5, 0.125)
    cotangent = bell_draw(key_list[4], (HB, WB, CB), 1.0, 6.0, ((0, 8), (2, 4)))
    return dict(level_in=level_in, w_level=w_level, w_down=w_down, w_neck=w_neck, cotangent=cotangent)


def slope_of(value):
    gate = jax.nn.sigmoid(value)
    return gate + value * gate * (1.0 - gate)

def conv_same(field_in, weights):
    height = field_in.shape[0]
    col_count = field_in.shape[1]
    padded = jnp.pad(field_in.astype(jnp.float32), ((1, 1), (1, 1), (0, 0)))
    kernel = weights.astype(jnp.float32)
    result = jnp.zeros((height, col_count, weights.shape[3]), jnp.float32)
    for offset_y in range(3):
        for offset_x in range(3):
            window = padded[offset_y:offset_y + height, offset_x:offset_x + col_count]
            result = result + jnp.einsum('hwc,cd->hwd', window, kernel[offset_y, offset_x])
    return result

def weight_terms(field_in, grads):
    height = field_in.shape[0]
    col_count = field_in.shape[1]
    padded = jnp.pad(field_in.astype(jnp.float32), ((1, 1), (1, 1), (0, 0)))
    grad_float = grads.astype(jnp.float32)
    kernel_rows = []
    for offset_y in range(3):
        kernel_row = []
        for offset_x in range(3):
            window = padded[offset_y:offset_y + height, offset_x:offset_x + col_count]
            kernel_row.append(jnp.einsum('hwc,hwd->cd', window, grad_float))
        kernel_rows.append(jnp.stack(kernel_row))
    return jnp.stack(kernel_rows)

def reference(level_in, w_level, w_down, w_neck, cotangent):
    level_pre = conv_same(level_in, w_level)
    level_act = (level_in.astype(jnp.float32) + jax.nn.silu(level_pre)).astype(jnp.bfloat16)
    level_grid = level_act.astype(jnp.float32).reshape(HB, 2, WB, 2, C4)
    neck_in = jnp.einsum('hpwqc,pqcd->hwd', level_grid, w_down.astype(jnp.float32)).astype(jnp.bfloat16)
    neck_pre = conv_same(neck_in, w_neck)
    neck_out = (neck_in.astype(jnp.float32) + jax.nn.silu(neck_pre)).astype(jnp.bfloat16)
    cot_float = cotangent.astype(jnp.float32)
    neck_gate = (cot_float * slope_of(neck_pre)).astype(jnp.bfloat16)
    flip_neck = jnp.transpose(w_neck[::-1, ::-1], (0, 1, 3, 2))
    neck_grad = (cot_float + conv_same(neck_gate, flip_neck)).astype(jnp.bfloat16)
    neck_scale = 1.0 / math.sqrt(HB * WB)
    grad_neck = (weight_terms(neck_in, neck_gate) * neck_scale).astype(jnp.bfloat16)
    level_back = jnp.einsum('hwd,pqcd->hpwqc', neck_grad.astype(jnp.float32), w_down.astype(jnp.float32)).reshape(H4, W4, C4)
    grad_down = (jnp.einsum('hpwqc,hwd->pqcd', level_grid, neck_grad.astype(jnp.float32)) * neck_scale).astype(jnp.bfloat16)
    level_gate = (level_back * slope_of(level_pre)).astype(jnp.bfloat16)
    flip_level = jnp.transpose(w_level[::-1, ::-1], (0, 1, 3, 2))
    grad_input = (level_back + conv_same(level_gate, flip_level)).astype(jnp.bfloat16)
    grad_level = (weight_terms(level_in, level_gate) * (1.0 / math.sqrt(H4 * W4))).astype(jnp.bfloat16)
    return (neck_out, grad_input, grad_level, grad_down, grad_neck)
```

```python
import functools
import math

import jax
import jax.numpy as jnp
from jax import lax
from jax.experimental import pallas as pl
from jax.experimental.pallas import tpu as pltpu
from jax.sharding import PartitionSpec as P

BF, F32 = jnp.bfloat16, jnp.float32
HALO = 7
SIDE = 8
VMEM = pl.BlockSpec(memory_space=pltpu.VMEM)


def call(body, out_shapes, args, scratch=(), limit=32):
    return pl.pallas_call(
        body,
        out_shape=out_shapes,
        in_specs=[VMEM] * len(args),
        out_specs=jax.tree.map(lambda _: VMEM, out_shapes),
        scratch_shapes=list(scratch),
        compiler_params=pltpu.CompilerParams(vmem_limit_bytes=limit * 1024 * 1024),
    )(*args)


def shape(dims, dtype=BF):
    return jax.ShapeDtypeStruct(dims, dtype)


def placing(owner, width, total):
    lane = lax.broadcasted_iota(jnp.int32, (128, total), 0)
    channel = lax.broadcasted_iota(jnp.int32, (128, total), 1)
    return jnp.where((lane < width) & (channel == lane + owner * width), 1.0, 0.0).astype(BF)


def dot(a, b, dims=((1,), (0,))):
    return lax.dot_general(a, b, (dims, ((), ())), preferred_element_type=F32)


def strip_piece(padded, tile, half_cols):
    start = pl.multiple_of(tile * half_cols, 8)
    piece = padded[:, pl.ds(start, half_cols + 2 * SIDE), :]
    return jnp.concatenate([piece[:, SIDE:], piece[:, :SIDE]], axis=1).astype(BF)


def pad_strip(cot_ref, padded):
    width = cot_ref.shape[2]
    padded[...] = jnp.zeros(padded.shape, F32)
    padded[:, SIDE : SIDE + cot_ref.shape[1], 0:width] = cot_ref[...].astype(F32)


def pack_cols(count, half_cols, level_ref, cot_ref, *refs):
    outs, padded = refs[:-1], refs[-1]
    me = lax.axis_index("gx")
    pad_strip(cot_ref, padded)
    level = level_ref[...].astype(F32)
    first, last = level[:, :SIDE], level[:, level.shape[1] - SIDE :]
    for turn in range(1, count):
        other = me ^ turn
        piece = strip_piece(padded, other, half_cols)
        cut = piece.shape[0] * piece.shape[1]
        outs[turn - 1][0:cut] = piece.reshape(cut, 128)
        edge = jnp.where(other == me + 1, last, first)
        outs[turn - 1][cut:] = edge.reshape(-1, 128).astype(BF)


def pack_rows(count, half_cols, level_ref, cot_ref, *refs):
    got = refs[: count - 1]
    wide_ref, cot_out, up_ref, down_ref, padded = refs[count - 1 :]
    me = lax.axis_index("gx")
    rows, cols = level_ref.shape[0], level_ref.shape[1]
    half_rows, width = cot_ref.shape[0], cot_ref.shape[2]
    total = cot_out.shape[2]
    pad_strip(cot_ref, padded)
    piece = strip_piece(padded, me, half_cols)
    pitch = piece.shape[1]
    cut = half_rows * pitch
    cot = dot(piece.reshape(cut, 128), placing(me, width, total))
    right = jnp.zeros((rows * SIDE, 128), F32)
    left = jnp.zeros((rows * SIDE, 128), F32)
    for turn in range(1, count):
        other = me ^ turn
        ref = got[turn - 1]
        cot = cot + dot(ref[0:cut], placing(other, width, total))
        edge = ref[cut:].astype(F32)
        right = jnp.where(other == me + 1, edge, right)
        left = jnp.where(other == me - 1, edge, left)
    right, left = right.reshape(rows, SIDE, 128), left.reshape(rows, SIDE, 128)
    cot = cot.astype(BF).reshape(half_rows, pitch, total)
    cot_out[...] = cot
    level = level_ref[...]
    gap = jnp.zeros((rows, 2 * pitch - cols - 2 * SIDE, 128), F32)
    wide_ref[:, :cols] = level
    wide_ref[:, cols:] = jnp.concatenate([right, gap, left], axis=1).astype(BF)
    edges = jnp.concatenate([right, left], axis=1).astype(BF)
    band = jnp.concatenate([level, edges], axis=1)
    cells = HALO * (cols + 2 * SIDE)
    for ref, low, neck in ((up_ref, 0, 0), (down_ref, rows - HALO, half_rows - 2)):
        ref[0:cells] = band[low : low + HALO].reshape(cells, 128)
        side = cot[neck : neck + 2].reshape(2 * pitch, total)
        ref[cells : cells + 2 * pitch] = side[:, :128]
        ref[cells + 2 * pitch :] = side[:, 128:]


def sigmoid_slope(value):
    gate = jax.nn.sigmoid(value)
    return gate, gate + value * gate * (1.0 - gate)


def shifted(value):
    size = value.shape[1]
    return pltpu.roll(value, 1, 1), pltpu.roll(value, size - 1, 1)


def paired(value):
    return jnp.concatenate(
        [pltpu.roll(value[:, :, 128:], 1, 1), pltpu.roll(value[:, :, :128], value.shape[1] - 1, 1)],
        axis=2,
    ).astype(BF)


def flat(value):
    return value.reshape(-1, value.shape[-1])


def main(
    sizes,
    wide_ref, cot_ref, above_ref, below_ref, wl_ref, wlt_ref, wd_ref, wdt_ref, wn_ref, wnt_ref,
    keep_ref, send_ref, pieces_ref, grad_ref,
    field, pair, side, wfwd, wbwd, act, slope, neck, gate, cot_all, ngrad, lback, lgate, lside, spread, store,
):
    rows, half_rows, half_cols, width, count, level_scale, neck_scale = sizes
    cols = 2 * half_cols
    pitch = wide_ref.shape[1] // 2
    total = cot_ref.shape[2]
    me, row = lax.axis_index("gx"), lax.axis_index("gy")
    row_end, col_end = lax.axis_size("gy") * half_rows, lax.axis_size("gx") * half_cols

    cells = HALO * (cols + 2 * SIDE)
    for ref, low in ((above_ref, 0), (below_ref, HALO + rows)):
        band = ref[0:cells].reshape(HALO, cols + 2 * SIDE, 128).astype(F32)
        field[low : low + HALO, 0 : cols + SIDE] = band[:, : cols + SIDE]
        field[low : low + HALO, cols + SIDE : 2 * pitch - SIDE] = jnp.zeros(
            (HALO, 2 * pitch - cols - 2 * SIDE, 128), F32
        )
        field[low : low + HALO, 2 * pitch - SIDE :] = band[:, cols + SIDE :]
        low_neck = 0 if low == 0 else 2 + half_rows
        cot_all[low_neck : low_neck + 2, :, :128] = ref[cells : cells + 2 * pitch].reshape(2, pitch, 128)
        cot_all[low_neck : low_neck + 2, :, 128:] = ref[cells + 2 * pitch :].reshape(2, pitch, 128)
    field[HALO : HALO + rows] = wide_ref[...].astype(F32)
    cot_all[2 : 2 + half_rows] = cot_ref[...]
    even = field[:, pl.ds(0, pitch, stride=2), :]
    odd = field[:, pl.ds(1, pitch, stride=2), :]
    both = jnp.concatenate([even, odd], axis=2)
    pair[...] = both.astype(BF)
    side[...] = paired(both)

    zero = jnp.zeros((128, 128), BF)
    for ky in range(3):
        w = [wl_ref[3 * ky + kx] for kx in range(3)]
        t = [wlt_ref[3 * ky + kx] for kx in range(3)]
        base = 512 * ky
        for ref, blocks in (
            (wfwd, (w[1], w[0], w[2], w[1], w[0], zero, zero, w[2])),
            (wbwd, (t[1], t[2], t[0], t[1], t[2], zero, zero, t[0])),
        ):
            for spot, block in enumerate(blocks):
                low = base + 128 * (spot // 2)
                ref[low : low + 128, 128 * (spot % 2) : 128 * (spot % 2) + 128] = block

    act_rows = act.shape[0]
    step = act_rows // 2
    for low in range(0, act_rows, step):
        taken = [
            flat(ref[low + ky : low + ky + step]) for ky in range(3) for ref in (pair, side)
        ]
        pre = dot(jnp.concatenate(taken, axis=1), wfwd[...])
        sig, slp = sigmoid_slope(pre)
        own = flat(pair[low + 1 : low + 1 + step]).astype(F32)
        act[low : low + step] = (own + pre * sig).astype(BF).reshape(step, pitch, 256)
        slope[low : low + step] = slp.reshape(step, pitch, 256)

    def inside(value, first_row):
        r = lax.broadcasted_iota(jnp.int32, value.shape, 0) + (row * half_rows + first_row)
        c = lax.broadcasted_iota(jnp.int32, value.shape, 1)
        c = jnp.where(c < half_cols + SIDE, c, c - pitch) + me * half_cols
        ok = (r >= 0) & (r < row_end) & (c >= 0) & (c < col_end)
        return jnp.where(ok, value, 0.0)

    neck_rows = act_rows // 2
    grid = act[...].reshape(neck_rows, 2, pitch, 256)
    both = jnp.concatenate([flat(grid[:, 0]), flat(grid[:, 1])], axis=1)
    value = dot(both, wd_ref[...]).reshape(neck_rows, pitch, total)
    value = inside(value, -3).astype(BF)
    before, behind = shifted(value.astype(F32))
    neck[0], neck[1], neck[2] = before.astype(BF), value, behind.astype(BF)

    gate_rows = neck_rows - 2
    taken = [flat(neck[kx, ky : ky + gate_rows]) for ky in range(3) for kx in range(3)]
    pre = dot(jnp.concatenate(taken, axis=1), wn_ref[...])
    sig, slp = sigmoid_slope(pre)
    own = flat(neck[1, 1 : 1 + gate_rows]).astype(F32)
    out = (own + pre * sig).astype(BF).reshape(gate_rows, pitch, total)
    out = out[2 : 2 + half_rows, :half_cols].reshape(half_rows * half_cols, total)
    for turn in range(count):
        pieces_ref[turn] = dot(out, placing(me ^ turn, width, total), ((1,), (1,))).astype(BF)
    value = (flat(cot_all[...]).astype(F32) * slp).astype(BF).reshape(gate_rows, pitch, total)
    before, behind = shifted(value.astype(F32))
    gate[0], gate[1], gate[2] = before.astype(BF), value, behind.astype(BF)

    grad_rows = gate_rows - 2
    taken = [
        flat(gate[2 - kx, 2 - ky : 2 - ky + grad_rows]) for ky in range(3) for kx in range(3)
    ]
    back = dot(jnp.concatenate(taken, axis=1), wnt_ref[...])
    value = flat(cot_all[1 : 1 + grad_rows]).astype(F32) + back
    value = inside(value.reshape(grad_rows, pitch, total), -1)
    ngrad[...] = value.astype(BF)

    value = dot(flat(ngrad[...]), wdt_ref[...]).reshape(grad_rows, pitch, 512)
    for p in range(2):
        for i in range(grad_rows):
            lback[2 * i + p] = value[i, :, 256 * p : 256 * p + 256]
    value = lback[...] * slope[4 : 4 + 2 * grad_rows]
    value = value.astype(BF)
    lgate[...] = value
    lside[...] = paired(value.astype(F32))

    taken = [
        flat(ref[3 - ky : 3 - ky + rows, :half_cols]) for ky in range(3) for ref in (lgate, lside)
    ]
    value = dot(jnp.concatenate(taken, axis=1), wbwd[...]).reshape(rows, half_cols, 256)
    value = value + lback[2 : 2 + rows, :half_cols]
    spread[:, pl.ds(0, half_cols, stride=2), :] = value[:, :, :128]
    spread[:, pl.ds(1, half_cols, stride=2), :] = value[:, :, 128:]
    grad_ref[...] = spread[...].astype(BF)

    half = keep_ref.shape[0]
    taken = [
        flat(neck[kx, 2 + ky : 2 + ky + half_rows, :half_cols]) for ky in range(3) for kx in range(3)
    ]
    own = flat(gate[1, 2 : 2 + half_rows, :half_cols])
    place = 0
    for lhs in taken:
        value = (dot(lhs, own, ((0,), (0,))) * neck_scale).astype(BF)
        store[place : place + 256] = value[:, :128]
        store[place + 256 : place + 512] = value[:, 128:]
        place += 512
    own = flat(ngrad[1 : 1 + half_rows, :half_cols])
    grid = act[6 : 6 + rows].reshape(half_rows, 2, pitch, 256)
    for p in range(2):
        lhs = flat(grid[:, p, :half_cols])
        value = (dot(lhs, own, ((0,), (0,))) * neck_scale).astype(BF)
        for q in range(2):
            for h in range(2):
                store[place : place + 128] = value[128 * q : 128 * q + 128, 128 * h : 128 * h + 128]
                place += 128
    own = flat(lgate[2 : 2 + rows, :half_cols])
    for ky in range(3):
        m = dot(flat(pair[6 + ky : 6 + ky + rows, :half_cols]), own, ((0,), (0,)))
        s = dot(flat(side[6 + ky : 6 + ky + rows, :half_cols]), own, ((0,), (0,)))
        for value in (
            m[:128, 128:] + s[:128, :128],
            m[:128, :128] + m[128:, 128:],
            m[128:, :128] + s[128:, 128:],
        ):
            store[place : place + 128] = (value * level_scale).astype(BF)
            place += 128
    store[place:] = jnp.zeros((2 * half - place, 128), BF)
    core = row & 1
    keep_ref[...] = store[pl.ds(pl.multiple_of(core * half, 16), half), :]
    send_ref[...] = store[pl.ds(pl.multiple_of((1 - core) * half, 16), half), :]


def add_cores(count, keep_ref, got_ref, pieces_ref, own_ref, *outs):
    me = lax.axis_index("gx")
    part = own_ref.shape[0]
    for turn in range(count):
        here = pl.ds(pl.multiple_of((me ^ turn) * part, 16), part)
        value = keep_ref[here, :].astype(F32) + got_ref[here, :].astype(F32)
        if turn == 0:
            own_ref[...] = value
        else:
            outs[turn - 1][0:part] = value.astype(BF)
            outs[turn - 1][part:] = pieces_ref[turn]


def add_cols(count, z_count, own_ref, pieces_ref, *refs):
    got = refs[: count - 1]
    neck_ref, first_ref = refs[count - 1 : count + 1]
    outs = refs[count + 1 : -1]
    total = refs[-1]
    me, z = lax.axis_index("gx"), lax.axis_index("gy") // 2
    part = own_ref.shape[0]
    rows, width = neck_ref.shape[0], neck_ref.shape[2]
    cols = neck_ref.shape[1] // count
    value = own_ref[...]
    for ref in got:
        value = value + ref[0:part].astype(F32)
    total[...] = value
    unit = part // z_count
    for turn in range(z_count):
        value = total[pl.ds(pl.multiple_of((z ^ turn) * unit, 16), unit), :]
        if turn == 0:
            first_ref[...] = value
        else:
            outs[turn - 1][...] = value.astype(BF)
    for turn in range(count):
        piece = pieces_ref[0] if turn == 0 else got[turn - 1][part:]
        here = pl.ds(pl.multiple_of((me ^ turn) * cols, 16), cols)
        neck_ref[:, here, :] = piece.reshape(rows, cols, 128)[:, :, :width]


def add_rows(first_ref, *refs):
    value = first_ref[...]
    for ref in refs[:-1]:
        value = value + ref[...].astype(F32)
    refs[-1][...] = value.astype(BF)


def finish(count, z_count, *refs):
    ours, theirs = refs[:count], refs[count : 2 * count]
    level_ref, down_ref, neck_ref, store = refs[2 * count :]
    me, row = lax.axis_index("gx"), lax.axis_index("gy")
    z, core = row // 2, row & 1
    unit = ours[0].shape[0] // z_count
    for flip, group in ((0, ours), (1, theirs)):
        for turn in range(count):
            for lap in range(z_count):
                place = (((core ^ flip) * count + (me ^ turn)) * z_count + (z ^ lap)) * unit
                store[pl.ds(pl.multiple_of(place, 16), unit), :] = group[turn][
                    unit * lap : unit * lap + unit
                ]
    place = 0
    for ref in (neck_ref, down_ref):
        deep = ref.shape[1]
        for i in range(ref.shape[0]):
            for h in range(2):
                ref[i, :, 128 * h : 128 * h + 128] = store[place : place + deep]
                place += deep
    for i in range(level_ref.shape[0]):
        level_ref[i] = store[place : place + 128]
        place += 128


def local(level_in, w_level, w_down, w_neck, cotangent):
    rows, cols, _ = level_in.shape
    half_rows, half_cols = rows // 2, cols // 2
    total = w_neck.shape[3]
    width = cotangent.shape[2]
    count, gy_count = lax.axis_size("gx"), lax.axis_size("gy")
    z_count = gy_count // 2
    pitch = half_cols + 2 * SIDE
    axes = ("gy", "gx")
    spots = [(y, x) for y in range(gy_count) for x in range(count)]

    def permute(value, target):
        pairs = [(y * count + x, target(y, x)) for y, x in spots]
        return lax.ppermute(value, axes, [(a, b) for a, b in pairs if b is not None])

    def by_col(value, turn):
        return permute(value, lambda y, x: y * count + (x ^ turn))

    def by_z(value, turn):
        return permute(value, lambda y, x: (y ^ (2 * turn)) * count + x)

    def by_core(value):
        return permute(value, lambda y, x: (y ^ 1) * count + x)

    def to_above(value):
        return permute(value, lambda y, x: (y - 1) * count + x if y > 0 else None)

    def to_below(value):
        return permute(value, lambda y, x: (y + 1) * count + x if y + 1 < gy_count else None)

    strip = pltpu.VMEM((half_rows, cotangent.shape[1] + 2 * SIDE, 128), F32)
    packed = shape((half_rows * pitch + rows * SIDE, 128))
    sent = call(
        functools.partial(pack_cols, count, half_cols),
        [packed] * (count - 1), (level_in, cotangent), [strip],
    )
    got = [by_col(value, turn + 1) for turn, value in enumerate(sent)]
    band = shape((HALO * (cols + 2 * SIDE) + 4 * pitch, 128))
    wide, cot, up, down = call(
        functools.partial(pack_rows, count, half_cols),
        [shape((rows, 2 * pitch, 128)), shape((half_rows, pitch, total)), band, band],
        (level_in, cotangent, *got), [strip],
    )
    below, above = to_above(up), to_below(down)

    wl = w_level.reshape(9, 128, 128)
    wlt = jnp.transpose(wl, (0, 2, 1))
    wd = w_down.reshape(512, total)
    wdt = wd.T
    wn = w_neck.reshape(9 * total, total)
    wnt = jnp.transpose(w_neck, (0, 1, 3, 2)).reshape(9 * total, total)
    pixels = rows * cols * count * gy_count
    grain = 2 * count * z_count
    used = 2 * 9 * total + 4 * 2 * 128 + 9 * 128
    unit = -(-used // (grain * 16)) * 16
    half = unit * grain // 2
    sizes = (
        rows, half_rows, half_cols, width, count,
        1.0 / math.sqrt(pixels), 1.0 / math.sqrt(pixels // 4),
    )
    far = rows + 2 * HALO
    keep, send, pieces, grad_input = call(
        functools.partial(main, sizes),
        [shape((half, 128)), shape((half, 128)), shape((count, half_rows * half_cols, 128)), shape(level_in.shape)],
        (wide, cot, above, below, wl, wlt, wd, wdt, wn, wnt),
        [
            pltpu.VMEM((far, 2 * pitch, 128), F32),
            pltpu.VMEM((far, pitch, 256), BF),
            pltpu.VMEM((far, pitch, 256), BF),
            pltpu.VMEM((1536, 256), BF),
            pltpu.VMEM((1536, 256), BF),
            pltpu.VMEM((far - 2, pitch, 256), BF),
            pltpu.VMEM((far - 2, pitch, 256), F32),
            pltpu.VMEM((3, half_rows + 6, pitch, total), BF),
            pltpu.VMEM((3, half_rows + 4, pitch, total), BF),
            pltpu.VMEM((half_rows + 4, pitch, total), BF),
            pltpu.VMEM((half_rows + 2, pitch, total), BF),
            pltpu.VMEM((rows + 4, pitch, 256), F32),
            pltpu.VMEM((rows + 4, pitch, 256), BF),
            pltpu.VMEM((rows + 4, pitch, 256), BF),
            pltpu.VMEM((rows, cols, 128), F32),
            pltpu.VMEM((2 * half, 128), BF),
        ],
        limit=48,
    )

    part = half // count
    tiles = half_rows * half_cols
    own, *sent = call(
        functools.partial(add_cores, count),
        [shape((part, 128), F32)] + [shape((part + tiles, 128))] * (count - 1),
        (keep, by_core(send), pieces),
    )
    got = [by_col(value, turn + 1) for turn, value in enumerate(sent)]
    neck_out, own, *sent = call(
        functools.partial(add_cols, count, z_count),
        [shape(cotangent.shape), shape((unit, 128), F32)] + [shape((unit, 128))] * (z_count - 1),
        (own, pieces, *got),
        [pltpu.VMEM((part, 128), F32)],
    )
    got = [by_z(value, turn + 1) for turn, value in enumerate(sent)]
    own = call(add_rows, shape((unit, 128)), (own, *got))
    own = jnp.concatenate([own] + [by_z(own, turn) for turn in range(1, z_count)])
    ours = [own] + [by_col(own, turn) for turn in range(1, count)]
    theirs = [by_core(value) for value in ours]
    grad_level, grad_down, grad_neck = call(
        functools.partial(finish, count, z_count),
        [shape((9, 128, 128)), shape((4, 128, total)), shape((9, total, total))],
        (*ours, *theirs),
        [pltpu.VMEM((2 * half, 128), BF)],
    )
    return (
        neck_out,
        grad_input,
        grad_level.reshape(w_level.shape),
        grad_down.reshape(w_down.shape),
        grad_neck.reshape(w_neck.shape),
    )


def solution(mesh):
    return jax.shard_map(
        local,
        mesh=mesh,
        in_specs=(P("gy", "gx", None), P(), P(), P(), P("gy", None, "gx")),
        out_specs=(P("gy", None, "gx"), P("gy", "gx", None), P(), P(), P()),
        check_vma=False,
    )
```

```python
import functools
import math

import jax
import jax.numpy as jnp
from jax import lax
from jax.experimental import pallas as pl
from jax.experimental.pallas import tpu as pltpu
from jax.sharding import PartitionSpec as P

BF, F32 = jnp.bfloat16, jnp.float32
HALO = 7
SIDE = 8
VMEM = pl.BlockSpec(memory_space=pltpu.VMEM)


def call(body, out_shapes, args, scratch=(), limit=8, flops=10**9):
    return pl.pallas_call(
        body,
        out_shape=out_shapes,
        in_specs=[VMEM] * len(args),
        out_specs=jax.tree.map(lambda _: VMEM, out_shapes),
        scratch_shapes=list(scratch),
        cost_estimate=pl.CostEstimate(flops=flops, bytes_accessed=0, transcendentals=0),
        compiler_params=pltpu.CompilerParams(vmem_limit_bytes=limit * 1024 * 1024),
    )(*args)


def shape(dims, dtype=BF):
    return jax.ShapeDtypeStruct(dims, dtype)


def dot(a, b, dims=((1,), (0,))):
    return lax.dot_general(a, b, (dims, ((), ())), preferred_element_type=F32)


def picking(dims, rule):
    i, j = (lax.broadcasted_iota(jnp.int32, dims, axis) for axis in (0, 1))
    return jnp.where(rule(i, j), 1.0, 0.0).astype(BF)


def groups_of(rows, width):
    return -(-rows * width // 128)


def lanes_to_channels(row, owner, width, total):
    base = row * width % 128
    return picking(
        (128, total),
        lambda lane, channel: (lane >= base)
        & (lane < base + width)
        & (lane - base == channel - owner * width),
    )


def strip_rows(cot_ref):
    half_rows, width, cols = cot_ref.shape
    value = cot_ref[...].reshape(half_rows * width, cols)
    short = 128 * groups_of(half_rows, width) - half_rows * width
    if short:
        value = jnp.concatenate([value, jnp.zeros((short, cols), BF)], axis=0)
    return value


def strip_piece(value, tile, half_cols):
    pitch = half_cols + 2 * SIDE
    pick = picking(
        (pitch, value.shape[1]),
        lambda i, j: j == jnp.where(i < half_cols + SIDE, i, i - pitch) + tile * half_cols,
    )
    parts = [
        dot(pick, value[low : low + 128], ((1,), (1,))) for low in range(0, value.shape[0], 128)
    ]
    return jnp.concatenate(parts, axis=0).astype(BF)


def pack_cols(count, half_cols, level_ref, cot_ref, *outs):
    me = lax.axis_index("gx")
    strip = strip_rows(cot_ref)
    level = level_ref[...].astype(F32)
    first, last = level[:, :SIDE], level[:, level.shape[1] - SIDE :]
    for turn in range(1, count):
        other = me ^ turn
        piece = strip_piece(strip, other, half_cols)
        cut = piece.shape[0]
        outs[turn - 1][0:cut] = piece
        edge = jnp.where(other == me + 1, last, first)
        outs[turn - 1][cut:] = edge.reshape(-1, 128).astype(BF)


def pack_rows(count, half_cols, level_ref, cot_ref, *refs):
    got = refs[: count - 1]
    kept_ref, cross_ref, inner_ref = refs[count - 1 :]
    me, core = lax.axis_index("gx"), lax.axis_index("gy") & 1
    rows, cols = level_ref.shape[0], level_ref.shape[1]
    half_rows, width = cot_ref.shape[0], cot_ref.shape[1]
    total = count * width
    pitch = half_cols + 2 * SIDE
    cut = groups_of(half_rows, width) * pitch
    mine = strip_piece(strip_rows(cot_ref), me, half_cols)
    right = jnp.zeros((rows * SIDE, 128), F32)
    left = jnp.zeros((rows * SIDE, 128), F32)
    for turn in range(1, count):
        edge = got[turn - 1][cut:].astype(F32)
        right = jnp.where(me ^ turn == me + 1, edge, right)
        left = jnp.where(me ^ turn == me - 1, edge, left)
    right, left = right.reshape(rows, SIDE, 128), left.reshape(rows, SIDE, 128)
    level = level_ref[...]
    gap = jnp.zeros((rows, 2 * pitch - cols - 2 * SIDE, 128), F32)
    edges = jnp.concatenate([right, gap, left], axis=1).astype(BF)
    wide = jnp.concatenate([level, edges], axis=1).reshape(2 * rows * pitch, 128)
    kept_ref[0 : 2 * rows * pitch] = wide
    cot = []
    for row in range(half_rows):
        low = row * width // 128 * pitch
        value = jnp.zeros((pitch, total), F32)
        for turn in range(count):
            part = mine[low : low + pitch] if turn == 0 else got[turn - 1][low : low + pitch]
            value = value + dot(part, lanes_to_channels(row, me ^ turn, width, total))
        value = value.astype(BF)
        cot.append(value)
        low = 2 * (rows + row) * pitch
        kept_ref[low : low + pitch] = value[:, :128]
        kept_ref[low + pitch : low + 2 * pitch] = value[:, 128:]
    edges = jnp.concatenate([right, left], axis=1).astype(BF)
    band = jnp.concatenate([level, edges], axis=1)
    cells = HALO * (cols + 2 * SIDE)
    for low, neck, is_cross in ((0, 0, core == 0), (rows - HALO, half_rows - 2, core == 1)):
        for ref, here in ((cross_ref, is_cross), (inner_ref, jnp.logical_not(is_cross))):

            @pl.when(here)
            def _(ref=ref, low=low, neck=neck):
                ref[0:cells] = band[low : low + HALO].reshape(cells, 128)
                for i in range(2):
                    spot = cells + 2 * pitch * i
                    ref[spot : spot + pitch] = cot[neck + i][:, :128]
                    ref[spot + pitch : spot + 2 * pitch] = cot[neck + i][:, 128:]


def turn_weights(wl_ref, wd_ref, wn_ref, wfwd_ref, wbwd_ref, wdt_ref, wnt_ref):
    zero = jnp.zeros((128, 128), BF)
    for ky in range(3):
        w = [wl_ref[3 * ky + kx] for kx in range(3)]
        t = [value.T for value in w]
        for ref, blocks in (
            (wfwd_ref, (w[1], w[0], w[2], w[1], w[0], zero, zero, w[2])),
            (wbwd_ref, (t[1], t[2], t[0], t[1], t[2], zero, zero, t[0])),
        ):
            for spot, block in enumerate(blocks):
                low = 512 * ky + 128 * (spot // 2)
                ref[low : low + 128, 128 * (spot % 2) : 128 * (spot % 2) + 128] = block
    for p in range(2):
        wdt_ref[:, 256 * p : 256 * p + 256] = wd_ref[256 * p : 256 * p + 256].T
    for k in range(9):
        total = wn_ref.shape[1]
        wnt_ref[total * k : total * k + total] = wn_ref[total * k : total * k + total].T


def sigmoid_slope(value):
    gate = jax.nn.sigmoid(value)
    return gate, gate + value * gate * (1.0 - gate)


def shifted(value):
    size = value.shape[1]
    return pltpu.roll(value, 1, 1), pltpu.roll(value, size - 1, 1)


def paired(value):
    return jnp.concatenate(
        [pltpu.roll(value[:, :, 128:], 1, 1), pltpu.roll(value[:, :, :128], value.shape[1] - 1, 1)],
        axis=2,
    ).astype(BF)


def flat(value):
    return value.reshape(-1, value.shape[-1])


def main(
    sizes,
    kept_ref, cross_ref, inner_ref, wfwd, wbwd, wd_ref, wdt_ref, wn_ref, wnt_ref,
    keep_ref, send_ref, pieces_ref, grad_ref,
    field, pair, side, act, slope, neck, gate, cot_all, ngrad, lback, lgate, lside, spread, store,
):
    rows, half_rows, half_cols, width, count, level_scale, neck_scale = sizes
    cols = 2 * half_cols
    pitch = half_cols + 2 * SIDE
    total = wd_ref.shape[1]
    me, row = lax.axis_index("gx"), lax.axis_index("gy")
    row_end, col_end = lax.axis_size("gy") * half_rows, lax.axis_size("gx") * half_cols
    core = row & 1

    cells = HALO * (cols + 2 * SIDE)

    def take(ref, low, low_neck):
        band = ref[0:cells].reshape(HALO, cols + 2 * SIDE, 128).astype(F32)
        field[low : low + HALO, 0 : cols + SIDE] = band[:, : cols + SIDE]
        field[low : low + HALO, cols + SIDE : 2 * pitch - SIDE] = jnp.zeros(
            (HALO, 2 * pitch - cols - 2 * SIDE, 128), F32
        )
        field[low : low + HALO, 2 * pitch - SIDE :] = band[:, cols + SIDE :]
        for i in range(2):
            spot = cells + 2 * pitch * i
            cot_all[low_neck + i, :, :128] = ref[spot : spot + pitch]
            cot_all[low_neck + i, :, 128:] = ref[spot + pitch : spot + 2 * pitch]

    @pl.when(core == 0)
    def _():
        take(cross_ref, 0, 0)
        take(inner_ref, HALO + rows, 2 + half_rows)

    @pl.when(core == 1)
    def _():
        take(inner_ref, 0, 0)
        take(cross_ref, HALO + rows, 2 + half_rows)

    own = kept_ref[0 : 2 * rows * pitch].reshape(rows, 2 * pitch, 128)
    field[HALO : HALO + rows] = own.astype(F32)
    for row_in in range(half_rows):
        low = 2 * (rows + row_in) * pitch
        cot_all[2 + row_in, :, :128] = kept_ref[low : low + pitch]
        cot_all[2 + row_in, :, 128:] = kept_ref[low + pitch : low + 2 * pitch]
    even = field[:, pl.ds(0, pitch, stride=2), :]
    odd = field[:, pl.ds(1, pitch, stride=2), :]
    both = jnp.concatenate([even, odd], axis=2)
    pair[...] = both.astype(BF)
    side[...] = paired(both)

    act_rows = act.shape[0]
    step = act_rows // 2
    for low in range(0, act_rows, step):
        taken = [
            flat(ref[low + ky : low + ky + step]) for ky in range(3) for ref in (pair, side)
        ]
        pre = dot(jnp.concatenate(taken, axis=1), wfwd[...])
        sig, slp = sigmoid_slope(pre)
        own = flat(pair[low + 1 : low + 1 + step]).astype(F32)
        act[low : low + step] = (own + pre * sig).astype(BF).reshape(step, pitch, 256)
        slope[low : low + step] = slp.reshape(step, pitch, 256)

    def inside(value, first_row):
        r = lax.broadcasted_iota(jnp.int32, value.shape, 0) + (row * half_rows + first_row)
        c = lax.broadcasted_iota(jnp.int32, value.shape, 1)
        c = jnp.where(c < half_cols + SIDE, c, c - pitch) + me * half_cols
        ok = (r >= 0) & (r < row_end) & (c >= 0) & (c < col_end)
        return jnp.where(ok, value, 0.0)

    neck_rows = act_rows // 2
    grid = act[...].reshape(neck_rows, 2, pitch, 256)
    both = jnp.concatenate([flat(grid[:, 0]), flat(grid[:, 1])], axis=1)
    value = dot(both, wd_ref[...]).reshape(neck_rows, pitch, total)
    value = inside(value, -3).astype(BF)
    before, behind = shifted(value.astype(F32))
    neck[0], neck[1], neck[2] = before.astype(BF), value, behind.astype(BF)

    gate_rows = neck_rows - 2
    taken = [flat(neck[kx, ky : ky + gate_rows]) for ky in range(3) for kx in range(3)]
    pre = dot(jnp.concatenate(taken, axis=1), wn_ref[...])
    sig, slp = sigmoid_slope(pre)
    own = flat(neck[1, 1 : 1 + gate_rows]).astype(F32)
    out = (own + pre * sig).astype(BF).reshape(gate_rows, pitch, total)
    out = out[2 : 2 + half_rows, :half_cols].reshape(half_rows * half_cols, total)
    for turn in range(count):
        for low in range(0, half_rows, max(1, 128 // width)):
            piece = jnp.zeros((half_cols, 128), F32)
            for r in range(low, min(half_rows, low + 128 // width)):
                pick = lanes_to_channels(r, me ^ turn, width, total)
                piece = piece + dot(out[half_cols * r : half_cols * r + half_cols], pick, ((1,), (1,)))
            group = low * width // 128
            pieces_ref[turn, half_cols * group : half_cols * group + half_cols] = piece.astype(BF)
    value = (flat(cot_all[...]).astype(F32) * slp).astype(BF).reshape(gate_rows, pitch, total)
    before, behind = shifted(value.astype(F32))
    gate[0], gate[1], gate[2] = before.astype(BF), value, behind.astype(BF)

    grad_rows = gate_rows - 2
    taken = [
        flat(gate[2 - kx, 2 - ky : 2 - ky + grad_rows]) for ky in range(3) for kx in range(3)
    ]
    back = dot(jnp.concatenate(taken, axis=1), wnt_ref[...])
    value = flat(cot_all[1 : 1 + grad_rows]).astype(F32) + back
    value = inside(value.reshape(grad_rows, pitch, total), -1)
    ngrad[...] = value.astype(BF)

    value = dot(flat(ngrad[...]), wdt_ref[...]).reshape(grad_rows, pitch, 512)
    for p in range(2):
        for i in range(grad_rows):
            lback[2 * i + p] = value[i, :, 256 * p : 256 * p + 256]
    value = lback[...] * slope[4 : 4 + 2 * grad_rows]
    value = value.astype(BF)
    lgate[...] = value
    lside[...] = paired(value.astype(F32))

    taken = [
        flat(ref[3 - ky : 3 - ky + rows, :half_cols]) for ky in range(3) for ref in (lgate, lside)
    ]
    value = dot(jnp.concatenate(taken, axis=1), wbwd[...]).reshape(rows, half_cols, 256)
    value = value + lback[2 : 2 + rows, :half_cols]
    spread[:, pl.ds(0, half_cols, stride=2), :] = value[:, :, :128]
    spread[:, pl.ds(1, half_cols, stride=2), :] = value[:, :, 128:]
    grad_ref[...] = spread[...].astype(BF)

    half = keep_ref.shape[0]
    taken = [
        flat(neck[kx, 2 + ky : 2 + ky + half_rows, :half_cols]) for ky in range(3) for kx in range(3)
    ]
    own = flat(gate[1, 2 : 2 + half_rows, :half_cols])
    place = 0
    for lhs in taken:
        value = (dot(lhs, own, ((0,), (0,))) * neck_scale).astype(BF)
        store[place : place + 256] = value[:, :128]
        store[place + 256 : place + 512] = value[:, 128:]
        place += 512
    own = flat(ngrad[1 : 1 + half_rows, :half_cols])
    grid = act[6 : 6 + rows].reshape(half_rows, 2, pitch, 256)
    for p in range(2):
        lhs = flat(grid[:, p, :half_cols])
        value = (dot(lhs, own, ((0,), (0,))) * neck_scale).astype(BF)
        for q in range(2):
            for h in range(2):
                store[place : place + 128] = value[128 * q : 128 * q + 128, 128 * h : 128 * h + 128]
                place += 128
    own = flat(lgate[2 : 2 + rows, :half_cols])
    for ky in range(3):
        m = dot(flat(pair[6 + ky : 6 + ky + rows, :half_cols]), own, ((0,), (0,)))
        s = dot(flat(side[6 + ky : 6 + ky + rows, :half_cols]), own, ((0,), (0,)))
        for value in (
            m[:128, 128:] + s[:128, :128],
            m[:128, :128] + m[128:, 128:],
            m[128:, :128] + s[128:, 128:],
        ):
            store[place : place + 128] = (value * level_scale).astype(BF)
            place += 128
    if place < 2 * half:
        store[place:] = jnp.zeros((2 * half - place, 128), BF)
    keep_ref[...] = store[pl.ds(pl.multiple_of(core * half, 16), half), :]
    send_ref[...] = store[pl.ds(pl.multiple_of((1 - core) * half, 16), half), :]


def add_cores(count, keep_ref, got_ref, pieces_ref, own_ref, *outs):
    me = lax.axis_index("gx")
    part = own_ref.shape[0]
    for turn in range(count):
        here = pl.ds(pl.multiple_of((me ^ turn) * part, 16), part)
        value = keep_ref[here, :].astype(F32) + got_ref[here, :].astype(F32)
        if turn == 0:
            own_ref[...] = value
        else:
            outs[turn - 1][0:part] = value.astype(BF)
            outs[turn - 1][part:] = pieces_ref[turn]


def add_cols(count, z_count, own_ref, *refs):
    got = refs[: count - 1]
    first_ref, outs, total = refs[count - 1], refs[count:-1], refs[-1]
    z = lax.axis_index("gy") // 2
    part, unit = own_ref.shape[0], first_ref.shape[0]
    value = own_ref[...]
    for ref in got:
        value = value + ref[0:part].astype(F32)
    total[0:part] = value
    if part < total.shape[0]:
        total[part:] = jnp.zeros((total.shape[0] - part, 128), F32)
    for turn in range(z_count):
        value = total[pl.ds(pl.multiple_of((z ^ turn) * unit, 16), unit), :]
        if turn == 0:
            first_ref[...] = value
        else:
            outs[turn - 1][...] = value.astype(BF)


def place_neck(count, part, pieces_ref, *refs):
    got, neck_ref = refs[:-1], refs[-1]
    me = lax.axis_index("gx")
    half_rows, width, cols = neck_ref.shape
    half_cols = cols // count
    for group in range(groups_of(half_rows, width)):
        value = jnp.zeros((128, cols), F32)
        here = slice(half_cols * group, half_cols * group + half_cols)
        for turn in range(count):
            piece = pieces_ref[0, here] if turn == 0 else got[turn - 1][part:][here]
            pick = picking((half_cols, cols), lambda i, j, t=turn: j == i + (me ^ t) * half_cols)
            value = value + dot(piece, pick, ((0,), (0,)))
        per = min(half_rows, 128 // width)
        value = value[: per * width].astype(BF).reshape(per, width, cols)
        neck_ref[group * per : group * per + per] = value


def add_rows(first_ref, *refs):
    value = first_ref[...]
    for ref in refs[:-1]:
        value = value + ref[...].astype(F32)
    refs[-1][...] = value.astype(BF)


def join(z_count, *refs):
    pieces, (out_ref, store) = refs[:z_count], refs[z_count:]
    z = lax.axis_index("gy") // 2
    unit = pieces[0].shape[0]
    for turn in range(z_count):
        store[pl.ds(pl.multiple_of((z ^ turn) * unit, 16), unit), :] = pieces[turn][...]
    out_ref[...] = store[0 : out_ref.shape[0]]


def finish(count, *refs):
    ours, theirs = refs[:count], refs[count : 2 * count]
    level_ref, down_ref, neck_ref, store = refs[2 * count :]
    me, row = lax.axis_index("gx"), lax.axis_index("gy")
    part = ours[0].shape[0]
    for flip, group in ((0, ours), (1, theirs)):
        for turn in range(count):
            place = (((row & 1) ^ flip) * count + (me ^ turn)) * part
            store[pl.ds(pl.multiple_of(place, 16), part), :] = group[turn][...]
    place = 0
    for ref in (neck_ref, down_ref):
        deep = ref.shape[1]
        for i in range(ref.shape[0]):
            for h in range(2):
                ref[i, :, 128 * h : 128 * h + 128] = store[place : place + deep]
                place += deep
    for i in range(level_ref.shape[0]):
        level_ref[i] = store[place : place + 128]
        place += 128


def local(level_in, w_level, w_down, w_neck, cotangent):
    rows, cols, _ = level_in.shape
    half_rows, half_cols = rows // 2, cols // 2
    total = w_neck.shape[3]
    count, gy_count = lax.axis_size("gx"), lax.axis_size("gy")
    z_count = gy_count // 2
    pitch = half_cols + 2 * SIDE
    axes = ("gy", "gx")
    spots = [(y, x) for y in range(gy_count) for x in range(count)]

    def permute(value, target):
        pairs = [(y * count + x, target(y, x)) for y, x in spots]
        return lax.ppermute(value, axes, [(a, b) for a, b in pairs if b is not None])

    def by_col(value, turn):
        return permute(value, lambda y, x: y * count + (x ^ turn))

    def by_z(value, turn):
        return permute(value, lambda y, x: (y ^ (2 * turn)) * count + x)

    def by_core(value):
        return permute(value, lambda y, x: (y ^ 1) * count + x)

    def by_seam(value):
        def target(y, x):
            other = y + 1 if y % 2 else y - 1
            return other * count + x if 0 <= other < gy_count else None

        return permute(value, target)

    strip = jnp.swapaxes(cotangent, 1, 2)
    width = strip.shape[1]
    packed = shape((groups_of(half_rows, width) * pitch + rows * SIDE, 128))
    sent = call(
        functools.partial(pack_cols, count, half_cols), [packed] * (count - 1), (level_in, strip)
    )
    got = [by_col(value, turn + 1) for turn, value in enumerate(sent)]
    band = shape((HALO * (cols + 2 * SIDE) + 4 * pitch, 128))
    kept, cross, inner = call(
        functools.partial(pack_rows, count, half_cols),
        [shape((3 * rows * pitch, 128)), band, band],
        (level_in, strip, *got),
    )
    cross, inner = by_seam(cross), by_core(inner)

    wl = w_level.reshape(9, 128, 128)
    wd = w_down.reshape(512, total)
    wn = w_neck.reshape(9 * total, total)
    wfwd, wbwd, wdt, wnt = call(
        turn_weights,
        [shape((1536, 256)), shape((1536, 256)), shape((total, 512)), shape(wn.shape)],
        (wl, wd, wn),
    )
    pixels = rows * cols * count * gy_count
    used = 2 * 9 * total + 4 * 2 * 128 + 9 * 128
    part = -(-used // (2 * count * 16)) * 16
    half = part * count
    unit = -(-part // (z_count * 16)) * 16
    tiles = groups_of(half_rows, width) * half_cols
    sizes = (
        rows, half_rows, half_cols, width, count,
        1.0 / math.sqrt(pixels), 1.0 / math.sqrt(pixels // 4),
    )
    far = rows + 2 * HALO
    keep, send, pieces, grad_input = call(
        functools.partial(main, sizes),
        [shape((half, 128)), shape((half, 128)), shape((count, tiles, 128)), shape(level_in.shape)],
        (kept, cross, inner, wfwd, wbwd, wd, wdt, wn, wnt),
        [
            pltpu.VMEM((far, 2 * pitch, 128), F32),
            pltpu.VMEM((far, pitch, 256), BF),
            pltpu.VMEM((far, pitch, 256), BF),
            pltpu.VMEM((far - 2, pitch, 256), BF),
            pltpu.VMEM((far - 2, pitch, 256), F32),
            pltpu.VMEM((3, half_rows + 6, pitch, total), BF),
            pltpu.VMEM((3, half_rows + 4, pitch, total), BF),
            pltpu.VMEM((half_rows + 4, pitch, total), BF),
            pltpu.VMEM((half_rows + 2, pitch, total), BF),
            pltpu.VMEM((rows + 4, pitch, 256), F32),
            pltpu.VMEM((rows + 4, pitch, 256), BF),
            pltpu.VMEM((rows + 4, pitch, 256), BF),
            pltpu.VMEM((rows, cols, 128), F32),
            pltpu.VMEM((2 * half, 128), BF),
        ],
        limit=20,
        flops=6 * 10**9,
    )

    own, *sent = call(
        functools.partial(add_cores, count),
        [shape((part, 128), F32)] + [shape((part + tiles, 128))] * (count - 1),
        (keep, by_core(send), pieces),
    )
    got = [by_col(value, turn + 1) for turn, value in enumerate(sent)]
    own, *sent = call(
        functools.partial(add_cols, count, z_count),
        [shape((unit, 128), F32)] + [shape((unit, 128))] * (z_count - 1),
        (own, *got),
        [pltpu.VMEM((unit * z_count, 128), F32)],
    )
    neck_out = call(functools.partial(place_neck, count, part), shape(strip.shape), (pieces, *got))
    got = [by_z(value, turn + 1) for turn, value in enumerate(sent)]
    own = call(add_rows, shape((unit, 128)), (own, *got))
    own = call(
        functools.partial(join, z_count),
        shape((part, 128)),
        [own] + [by_z(own, turn) for turn in range(1, z_count)],
        [pltpu.VMEM((unit * z_count, 128), BF)],
    )
    ours = [own] + [by_col(own, turn) for turn in range(1, count)]
    theirs = [by_core(value) for value in ours]
    grad_level, grad_down, grad_neck = call(
        functools.partial(finish, count),
        [shape((9, 128, 128)), shape((4, 128, total)), shape((9, total, total))],
        (*ours, *theirs),
        [pltpu.VMEM((2 * half, 128), BF)],
    )
    return (
        jnp.swapaxes(neck_out, 1, 2),
        grad_input,
        grad_level.reshape(w_level.shape),
        grad_down.reshape(w_down.shape),
        grad_neck.reshape(w_neck.shape),
    )


def solution(mesh):
    return jax.shard_map(
        local,
        mesh=mesh,
        in_specs=(P("gy", "gx", None), P(), P(), P(), P("gy", None, "gx")),
        out_specs=(P("gy", None, "gx"), P("gy", "gx", None), P(), P(), P()),
        check_vma=False,
    )
```

```python
import functools
import math

import jax
import jax.numpy as jnp
from jax import lax
from jax.experimental import pallas as pl
from jax.experimental.pallas import tpu as pltpu
from jax.sharding import PartitionSpec as P

BF, F32 = jnp.bfloat16, jnp.float32
HALO = 7
SIDE = 8
VMEM = pl.BlockSpec(memory_space=pltpu.VMEM)


def call(body, out_shapes, args, scratch=(), limit=8, flops=10**9):
    return pl.pallas_call(
        body,
        out_shape=out_shapes,
        in_specs=[VMEM] * len(args),
        out_specs=jax.tree.map(lambda _: VMEM, out_shapes),
        scratch_shapes=list(scratch),
        cost_estimate=pl.CostEstimate(flops=flops, bytes_accessed=0, transcendentals=0),
        compiler_params=pltpu.CompilerParams(vmem_limit_bytes=limit * 1024 * 1024),
    )(*args)


def shape(dims, dtype=BF):
    return jax.ShapeDtypeStruct(dims, dtype)


def dot(a, b, dims=((1,), (0,))):
    return lax.dot_general(a, b, (dims, ((), ())), preferred_element_type=F32)


def picking(dims, rule):
    i, j = (lax.broadcasted_iota(jnp.int32, dims, axis) for axis in (0, 1))
    return jnp.where(rule(i, j), 1.0, 0.0).astype(BF)


def groups_of(rows, width):
    return -(-rows * width // 128)


def lanes_to_channels(row, owner, width, total):
    base = row * width % 128
    return picking(
        (128, total),
        lambda lane, channel: (lane >= base)
        & (lane < base + width)
        & (lane - base == channel - owner * width),
    )


def strip_rows(cot_ref):
    half_rows, width, cols = cot_ref.shape
    value = cot_ref[...].reshape(half_rows * width, cols)
    short = 128 * groups_of(half_rows, width) - half_rows * width
    if short:
        value = jnp.concatenate([value, jnp.zeros((short, cols), BF)], axis=0)
    return value


def strip_piece(value, tile, half_cols):
    pitch = half_cols + 2 * SIDE
    pick = picking(
        (pitch, value.shape[1]),
        lambda i, j: j == jnp.where(i < half_cols + SIDE, i, i - pitch) + tile * half_cols,
    )
    parts = [
        dot(pick, value[low : low + 128], ((1,), (1,))) for low in range(0, value.shape[0], 128)
    ]
    return jnp.concatenate(parts, axis=0).astype(BF)


def pack_cols(count, half_cols, level_ref, cot_ref, *outs):
    me = lax.axis_index("gx")
    strip = strip_rows(cot_ref)
    level = level_ref[...].astype(F32)
    first, last = level[:, :SIDE], level[:, level.shape[1] - SIDE :]
    for turn in range(1, count):
        other = me ^ turn
        piece = strip_piece(strip, other, half_cols)
        cut = piece.shape[0]
        outs[turn - 1][0:cut] = piece
        edge = jnp.where(other == me + 1, last, first)
        outs[turn - 1][cut:] = edge.reshape(-1, 128).astype(BF)


def pack_rows(count, half_cols, level_ref, cot_ref, *refs):
    got = refs[: count - 1]
    kept_ref, cross_ref, inner_ref = refs[count - 1 :]
    me, core = lax.axis_index("gx"), lax.axis_index("gy") & 1
    rows, cols = level_ref.shape[0], level_ref.shape[1]
    half_rows, width = cot_ref.shape[0], cot_ref.shape[1]
    total = count * width
    pitch = half_cols + 2 * SIDE
    cut = groups_of(half_rows, width) * pitch
    mine = strip_piece(strip_rows(cot_ref), me, half_cols)
    right = jnp.zeros((rows * SIDE, 128), F32)
    left = jnp.zeros((rows * SIDE, 128), F32)
    for turn in range(1, count):
        edge = got[turn - 1][cut:].astype(F32)
        right = jnp.where(me ^ turn == me + 1, edge, right)
        left = jnp.where(me ^ turn == me - 1, edge, left)
    right, left = right.reshape(rows, SIDE, 128), left.reshape(rows, SIDE, 128)
    level = level_ref[...]
    gap = jnp.zeros((rows, 2 * pitch - cols - 2 * SIDE, 128), F32)
    edges = jnp.concatenate([right, gap, left], axis=1).astype(BF)
    wide = jnp.concatenate([level, edges], axis=1).reshape(2 * rows * pitch, 128)
    kept_ref[0 : 2 * rows * pitch] = wide
    cot = []
    for row in range(half_rows):
        low = row * width // 128 * pitch
        value = jnp.zeros((pitch, total), F32)
        for turn in range(count):
            part = mine[low : low + pitch] if turn == 0 else got[turn - 1][low : low + pitch]
            value = value + dot(part, lanes_to_channels(row, me ^ turn, width, total))
        value = value.astype(BF)
        cot.append(value)
        low = 2 * (rows + row) * pitch
        kept_ref[low : low + pitch] = value[:, :128]
        kept_ref[low + pitch : low + 2 * pitch] = value[:, 128:]
    edges = jnp.concatenate([right, left], axis=1).astype(BF)
    band = jnp.concatenate([level, edges], axis=1)
    cells = HALO * (cols + 2 * SIDE)
    for low, neck, is_cross in ((0, 0, core == 0), (rows - HALO, half_rows - 2, core == 1)):
        for ref, here in ((cross_ref, is_cross), (inner_ref, jnp.logical_not(is_cross))):

            @pl.when(here)
            def _(ref=ref, low=low, neck=neck):
                ref[0:cells] = band[low : low + HALO].reshape(cells, 128)
                for i in range(2):
                    spot = cells + 2 * pitch * i
                    ref[spot : spot + pitch] = cot[neck + i][:, :128]
                    ref[spot + pitch : spot + 2 * pitch] = cot[neck + i][:, 128:]


def turn_weights(wl_ref, wd_ref, wn_ref, wfwd_ref, wbwd_ref, wdt_ref, wnt_ref):
    zero = jnp.zeros((128, 128), BF)
    for ky in range(3):
        w = [wl_ref[3 * ky + kx] for kx in range(3)]
        t = [value.T for value in w]
        for ref, blocks in (
            (wfwd_ref, (w[1], w[0], w[2], w[1], w[0], zero, zero, w[2])),
            (wbwd_ref, (t[1], t[2], t[0], t[1], t[2], zero, zero, t[0])),
        ):
            for spot, block in enumerate(blocks):
                low = 512 * ky + 128 * (spot // 2)
                ref[low : low + 128, 128 * (spot % 2) : 128 * (spot % 2) + 128] = block
    for p in range(2):
        wdt_ref[:, 256 * p : 256 * p + 256] = wd_ref[256 * p : 256 * p + 256].T
    for k in range(9):
        total = wn_ref.shape[1]
        wnt_ref[total * k : total * k + total] = wn_ref[total * k : total * k + total].T


def sigmoid_slope(value):
    gate = jax.nn.sigmoid(value)
    return gate, gate + value * gate * (1.0 - gate)


def shifted(value):
    size = value.shape[1]
    return pltpu.roll(value, 1, 1), pltpu.roll(value, size - 1, 1)


def paired(value):
    return jnp.concatenate(
        [pltpu.roll(value[:, :, 128:], 1, 1), pltpu.roll(value[:, :, :128], value.shape[1] - 1, 1)],
        axis=2,
    ).astype(BF)


def dot_rows(a, b, step):
    return jnp.concatenate([dot(a[i : i + step], b) for i in range(0, a.shape[0], step)], axis=0)


def flat(value):
    return value.reshape(-1, value.shape[-1])


def main(
    sizes,
    kept_ref, cross_ref, inner_ref, wfwd, wbwd, wd_ref, wdt_ref, wn_ref, wnt_ref,
    sums_ref, send_ref, out_ref, grad_ref,
    field, pair, side, act, slope, neck, gate, cot_all, ngrad, lback, lgate, lside, spread,
):
    rows, half_rows, half_cols, _, _ = sizes
    cols = 2 * half_cols
    pitch = half_cols + 2 * SIDE
    total = wd_ref.shape[1]
    me, row = lax.axis_index("gx"), lax.axis_index("gy")
    row_end, col_end = lax.axis_size("gy") * half_rows, lax.axis_size("gx") * half_cols
    core = row & 1

    cells = HALO * (cols + 2 * SIDE)

    def take(ref, low, low_neck):
        band = ref[0:cells].reshape(HALO, cols + 2 * SIDE, 128).astype(F32)
        field[low : low + HALO, 0 : cols + SIDE] = band[:, : cols + SIDE]
        field[low : low + HALO, cols + SIDE : 2 * pitch - SIDE] = jnp.zeros(
            (HALO, 2 * pitch - cols - 2 * SIDE, 128), F32
        )
        field[low : low + HALO, 2 * pitch - SIDE :] = band[:, cols + SIDE :]
        for i in range(2):
            spot = cells + 2 * pitch * i
            cot_all[low_neck + i, :, :128] = ref[spot : spot + pitch]
            cot_all[low_neck + i, :, 128:] = ref[spot + pitch : spot + 2 * pitch]

    @pl.when(core == 0)
    def _():
        take(cross_ref, 0, 0)
        take(inner_ref, HALO + rows, 2 + half_rows)

    @pl.when(core == 1)
    def _():
        take(inner_ref, 0, 0)
        take(cross_ref, HALO + rows, 2 + half_rows)

    own = kept_ref[0 : 2 * rows * pitch].reshape(rows, 2 * pitch, 128)
    field[HALO : HALO + rows] = own.astype(F32)
    for row_in in range(half_rows):
        low = 2 * (rows + row_in) * pitch
        cot_all[2 + row_in, :, :128] = kept_ref[low : low + pitch]
        cot_all[2 + row_in, :, 128:] = kept_ref[low + pitch : low + 2 * pitch]
    even = field[:, pl.ds(0, pitch, stride=2), :]
    odd = field[:, pl.ds(1, pitch, stride=2), :]
    both = jnp.concatenate([even, odd], axis=2)
    pair[...] = both.astype(BF)
    side[...] = paired(both)

    act_rows = act.shape[0]
    step = act_rows // 2
    for low in range(0, act_rows, step):
        taken = [
            flat(ref[low + ky : low + ky + step]) for ky in range(3) for ref in (pair, side)
        ]
        pre = dot(jnp.concatenate(taken, axis=1), wfwd[...])
        sig, slp = sigmoid_slope(pre)
        own = flat(pair[low + 1 : low + 1 + step]).astype(F32)
        act[low : low + step] = (own + pre * sig).astype(BF).reshape(step, pitch, 256)
        slope[low : low + step] = slp.reshape(step, pitch, 256)

    def inside(value, first_row):
        r = lax.broadcasted_iota(jnp.int32, value.shape, 0) + (row * half_rows + first_row)
        c = lax.broadcasted_iota(jnp.int32, value.shape, 1)
        c = jnp.where(c < half_cols + SIDE, c, c - pitch) + me * half_cols
        ok = (r >= 0) & (r < row_end) & (c >= 0) & (c < col_end)
        return jnp.where(ok, value, 0.0)

    neck_rows = act_rows // 2
    grid = act[...].reshape(neck_rows, 2, pitch, 256)
    both = jnp.concatenate([flat(grid[:, 0]), flat(grid[:, 1])], axis=1)
    value = dot_rows(both, wd_ref[...], 5 * pitch).reshape(neck_rows, pitch, total)
    value = inside(value, -3).astype(BF)
    before, behind = shifted(value.astype(F32))
    neck[0], neck[1], neck[2] = before.astype(BF), value, behind.astype(BF)

    gate_rows = neck_rows - 2
    taken = [flat(neck[kx, ky : ky + gate_rows]) for ky in range(3) for kx in range(3)]
    pre = dot_rows(jnp.concatenate(taken, axis=1), wn_ref[...], 4 * pitch)
    sig, slp = sigmoid_slope(pre)
    own = flat(neck[1, 1 : 1 + gate_rows]).astype(F32)
    out = (own + pre * sig).astype(BF).reshape(gate_rows, pitch, total)
    out = out[2 : 2 + half_rows, :half_cols].reshape(half_rows * half_cols, total)
    out_ref[...] = out
    value = (flat(cot_all[...]).astype(F32) * slp).astype(BF).reshape(gate_rows, pitch, total)
    before, behind = shifted(value.astype(F32))
    gate[0], gate[1], gate[2] = before.astype(BF), value, behind.astype(BF)

    grad_rows = gate_rows - 2
    taken = [
        flat(gate[2 - kx, 2 - ky : 2 - ky + grad_rows]) for ky in range(3) for kx in range(3)
    ]
    back = dot_rows(jnp.concatenate(taken, axis=1), wnt_ref[...], 3 * pitch)
    value = flat(cot_all[1 : 1 + grad_rows]).astype(F32) + back
    value = inside(value.reshape(grad_rows, pitch, total), -1)
    ngrad[...] = value.astype(BF)

    value = dot_rows(flat(ngrad[...]), wdt_ref[...], 3 * pitch).reshape(grad_rows, pitch, 512)
    for p in range(2):
        for i in range(grad_rows):
            lback[2 * i + p] = value[i, :, 256 * p : 256 * p + 256]
    value = lback[...] * slope[4 : 4 + 2 * grad_rows]
    value = value.astype(BF)
    lgate[...] = value
    lside[...] = paired(value.astype(F32))

    taken = [
        flat(ref[3 - ky : 3 - ky + rows, :half_cols]) for ky in range(3) for ref in (lgate, lside)
    ]
    value = dot_rows(jnp.concatenate(taken, axis=1), wbwd[...], 4 * half_cols).reshape(rows, half_cols, 256)
    value = value + lback[2 : 2 + rows, :half_cols]
    spread[:, pl.ds(0, half_cols, stride=2), :] = value[:, :, :128]
    spread[:, pl.ds(1, half_cols, stride=2), :] = value[:, :, 128:]
    grad_ref[...] = spread[...].astype(BF)

    weight_sums(sizes, sums_ref, neck, gate, act, ngrad, pair, side, lgate)
    half = send_ref.shape[0]
    send_ref[...] = sums_ref[pl.ds(pl.multiple_of((1 - core) * half, 16), half), :]


def weight_sums(sizes, sums_ref, neck, gate, act, ngrad, pair, side, lgate):
    rows, half_rows, half_cols, level_scale, neck_scale = sizes
    pitch = act.shape[1]
    place = 0

    def put(value):
        nonlocal place
        sums_ref[place : place + value.shape[0]] = value
        place += value.shape[0]

    own = flat(gate[1, 2 : 2 + half_rows, :half_cols])
    for ky in range(3):
        for kx in range(3):
            lhs = flat(neck[kx, 2 + ky : 2 + ky + half_rows, :half_cols])
            value = (dot(lhs, own, ((0,), (0,))) * neck_scale).astype(BF)
            put(value[:, :128])
            put(value[:, 128:])
    own = flat(ngrad[1 : 1 + half_rows, :half_cols])
    grid = act[6 : 6 + rows].reshape(half_rows, 2, pitch, 256)
    for p in range(2):
        lhs = flat(grid[:, p, :half_cols])
        value = (dot(lhs, own, ((0,), (0,))) * neck_scale).astype(BF)
        for q in range(2):
            for h in range(2):
                put(value[128 * q : 128 * q + 128, 128 * h : 128 * h + 128])
    own = flat(lgate[2 : 2 + rows, :half_cols])
    for ky in range(3):
        m = dot(flat(pair[6 + ky : 6 + ky + rows, :half_cols]), own, ((0,), (0,)))
        s = dot(flat(side[6 + ky : 6 + ky + rows, :half_cols]), own, ((0,), (0,)))
        for value in (
            m[:128, 128:] + s[:128, :128],
            m[:128, :128] + m[128:, 128:],
            m[128:, :128] + s[128:, 128:],
        ):
            put((value * level_scale).astype(BF))
    if place < sums_ref.shape[0]:
        put(jnp.zeros((sums_ref.shape[0] - place, 128), BF))


def pack_neck(count, half_rows, width, out_ref, pieces_ref):
    me = lax.axis_index("gx")
    cells, total = out_ref.shape
    half_cols, per = cells // half_rows, 128 // width
    for turn in range(count):
        for low in range(0, half_rows, per):
            piece = jnp.zeros((half_cols, 128), F32)
            for r in range(low, min(half_rows, low + per)):
                pick = lanes_to_channels(r, me ^ turn, width, total)
                piece = piece + dot(out_ref[half_cols * r : half_cols * r + half_cols], pick, ((1,), (1,)))
            group = low // per
            pieces_ref[turn, half_cols * group : half_cols * group + half_cols] = piece.astype(BF)


def add_cores(count, sums_ref, got_ref, pieces_ref, own_ref, *outs):
    me, core = lax.axis_index("gx"), lax.axis_index("gy") & 1
    part = own_ref.shape[0]
    for turn in range(count):
        mine = pl.ds(pl.multiple_of((core * count + (me ^ turn)) * part, 16), part)
        theirs = pl.ds(pl.multiple_of((me ^ turn) * part, 16), part)
        value = sums_ref[mine, :].astype(F32) + got_ref[theirs, :].astype(F32)
        if turn == 0:
            own_ref[...] = value
        else:
            outs[turn - 1][0:part] = value.astype(BF)
            outs[turn - 1][part:] = pieces_ref[turn]


def add_cols(count, z_count, own_ref, *refs):
    got = refs[: count - 1]
    first_ref, outs, total = refs[count - 1], refs[count:-1], refs[-1]
    z = lax.axis_index("gy") // 2
    part, unit = own_ref.shape[0], first_ref.shape[0]
    value = own_ref[...]
    for ref in got:
        value = value + ref[0:part].astype(F32)
    total[0:part] = value
    if part < total.shape[0]:
        total[part:] = jnp.zeros((total.shape[0] - part, 128), F32)
    for turn in range(z_count):
        value = total[pl.ds(pl.multiple_of((z ^ turn) * unit, 16), unit), :]
        if turn == 0:
            first_ref[...] = value
        else:
            outs[turn - 1][...] = value.astype(BF)


def place_neck(count, part, pieces_ref, *refs):
    got, neck_ref = refs[:-1], refs[-1]
    me = lax.axis_index("gx")
    half_rows, width, cols = neck_ref.shape
    half_cols = cols // count
    for group in range(groups_of(half_rows, width)):
        value = jnp.zeros((128, cols), F32)
        here = slice(half_cols * group, half_cols * group + half_cols)
        for turn in range(count):
            piece = pieces_ref[0, here] if turn == 0 else got[turn - 1][part:][here]
            pick = picking((half_cols, cols), lambda i, j, t=turn: j == i + (me ^ t) * half_cols)
            value = value + dot(piece, pick, ((0,), (0,)))
        per = min(half_rows, 128 // width)
        value = value[: per * width].astype(BF).reshape(per, width, cols)
        neck_ref[group * per : group * per + per] = value


def add_rows(first_ref, *refs):
    value = first_ref[...]
    for ref in refs[:-1]:
        value = value + ref[...].astype(F32)
    refs[-1][...] = value.astype(BF)


def join(z_count, *refs):
    pieces, (out_ref, store) = refs[:z_count], refs[z_count:]
    z = lax.axis_index("gy") // 2
    unit = pieces[0].shape[0]
    for turn in range(z_count):
        store[pl.ds(pl.multiple_of((z ^ turn) * unit, 16), unit), :] = pieces[turn][...]
    out_ref[...] = store[0 : out_ref.shape[0]]


def finish(count, *refs):
    ours, theirs = refs[:count], refs[count : 2 * count]
    level_ref, down_ref, neck_ref, store = refs[2 * count :]
    me, row = lax.axis_index("gx"), lax.axis_index("gy")
    part = ours[0].shape[0]
    for flip, group in ((0, ours), (1, theirs)):
        for turn in range(count):
            place = (((row & 1) ^ flip) * count + (me ^ turn)) * part
            store[pl.ds(pl.multiple_of(place, 16), part), :] = group[turn][...]
    place = 0
    for ref in (neck_ref, down_ref):
        deep = ref.shape[1]
        for i in range(ref.shape[0]):
            for h in range(2):
                ref[i, :, 128 * h : 128 * h + 128] = store[place : place + deep]
                place += deep
    for i in range(level_ref.shape[0]):
        level_ref[i] = store[place : place + 128]
        place += 128


def local(level_in, w_level, w_down, w_neck, cotangent):
    rows, cols, _ = level_in.shape
    half_rows, half_cols = rows // 2, cols // 2
    total = w_neck.shape[3]
    count, gy_count = lax.axis_size("gx"), lax.axis_size("gy")
    z_count = gy_count // 2
    pitch = half_cols + 2 * SIDE
    axes = ("gy", "gx")
    spots = [(y, x) for y in range(gy_count) for x in range(count)]

    def permute(value, target):
        pairs = [(y * count + x, target(y, x)) for y, x in spots]
        return lax.ppermute(value, axes, [(a, b) for a, b in pairs if b is not None])

    def by_col(value, turn):
        return permute(value, lambda y, x: y * count + (x ^ turn))

    def by_z(value, turn):
        return permute(value, lambda y, x: (y ^ (2 * turn)) * count + x)

    def by_core(value):
        return permute(value, lambda y, x: (y ^ 1) * count + x)

    def by_seam(value):
        def target(y, x):
            other = y + 1 if y % 2 else y - 1
            return other * count + x if 0 <= other < gy_count else None

        return permute(value, target)

    strip = jnp.swapaxes(cotangent, 1, 2)
    width = strip.shape[1]
    packed = shape((groups_of(half_rows, width) * pitch + rows * SIDE, 128))
    sent = call(
        functools.partial(pack_cols, count, half_cols), [packed] * (count - 1), (level_in, strip)
    )
    got = [by_col(value, turn + 1) for turn, value in enumerate(sent)]
    band = shape((HALO * (cols + 2 * SIDE) + 4 * pitch, 128))
    kept, cross, inner = call(
        functools.partial(pack_rows, count, half_cols),
        [shape((3 * rows * pitch, 128)), band, band],
        (level_in, strip, *got),
    )
    cross, inner = by_seam(cross), by_core(inner)

    wl = w_level.reshape(9, 128, 128)
    wd = w_down.reshape(512, total)
    wn = w_neck.reshape(9 * total, total)
    wfwd, wbwd, wdt, wnt = call(
        turn_weights,
        [shape((1536, 256)), shape((1536, 256)), shape((total, 512)), shape(wn.shape)],
        (wl, wd, wn),
    )
    pixels = rows * cols * count * gy_count
    used = 2 * 9 * total + 4 * 2 * 128 + 9 * 128
    part = -(-used // (2 * count * 16)) * 16
    half = part * count
    unit = -(-part // (z_count * 16)) * 16
    tiles = groups_of(half_rows, width) * half_cols
    sizes = (
        rows, half_rows, half_cols,
        1.0 / math.sqrt(pixels), 1.0 / math.sqrt(pixels // 4),
    )
    far = rows + 2 * HALO
    sums, send, out, grad_input = call(
        functools.partial(main, sizes),
        [shape((2 * half, 128)), shape((half, 128)), shape((half_rows * half_cols, total)), shape(level_in.shape)],
        (kept, cross, inner, wfwd, wbwd, wd, wdt, wn, wnt),
        [
            pltpu.VMEM((far, 2 * pitch, 128), F32),
            pltpu.VMEM((far, pitch, 256), BF),
            pltpu.VMEM((far, pitch, 256), BF),
            pltpu.VMEM((far - 2, pitch, 256), BF),
            pltpu.VMEM((far - 2, pitch, 256), F32),
            pltpu.VMEM((3, half_rows + 6, pitch, total), BF),
            pltpu.VMEM((3, half_rows + 4, pitch, total), BF),
            pltpu.VMEM((half_rows + 4, pitch, total), BF),
            pltpu.VMEM((half_rows + 2, pitch, total), BF),
            pltpu.VMEM((rows + 4, pitch, 256), F32),
            pltpu.VMEM((rows + 4, pitch, 256), BF),
            pltpu.VMEM((rows + 4, pitch, 256), BF),
            pltpu.VMEM((rows, cols, 128), F32),
        ],
        limit=20,
        flops=6 * 10**9,
    )

    pieces = call(
        functools.partial(pack_neck, count, half_rows, width), shape((count, tiles, 128)), (out,)
    )
    own, *sent = call(
        functools.partial(add_cores, count),
        [shape((part, 128), F32)] + [shape((part + tiles, 128))] * (count - 1),
        (sums, by_core(send), pieces),
    )
    got = [by_col(value, turn + 1) for turn, value in enumerate(sent)]
    own, *sent = call(
        functools.partial(add_cols, count, z_count),
        [shape((unit, 128), F32)] + [shape((unit, 128))] * (z_count - 1),
        (own, *got),
        [pltpu.VMEM((unit * z_count, 128), F32)],
    )
    neck_out = call(functools.partial(place_neck, count, part), shape(strip.shape), (pieces, *got))
    got = [by_z(value, turn + 1) for turn, value in enumerate(sent)]
    own = call(add_rows, shape((unit, 128)), (own, *got))
    own = call(
        functools.partial(join, z_count),
        shape((part, 128)),
        [own] + [by_z(own, turn) for turn in range(1, z_count)],
        [pltpu.VMEM((unit * z_count, 128), BF)],
    )
    ours = [own] + [by_col(own, turn) for turn in range(1, count)]
    theirs = [by_core(value) for value in ours]
    grad_level, grad_down, grad_neck = call(
        functools.partial(finish, count),
        [shape((9, 128, 128)), shape((4, 128, total)), shape((9, total, total))],
        (*ours, *theirs),
        [pltpu.VMEM((2 * half, 128), BF)],
    )
    return (
        jnp.swapaxes(neck_out, 1, 2),
        grad_input,
        grad_level.reshape(w_level.shape),
        grad_down.reshape(w_down.shape),
        grad_neck.reshape(w_neck.shape),
    )


def solution(mesh):
    return jax.shard_map(
        local,
        mesh=mesh,
        in_specs=(P("gy", "gx", None), P(), P(), P(), P("gy", None, "gx")),
        out_specs=(P("gy", None, "gx"), P("gy", "gx", None), P(), P(), P()),
        check_vma=False,
    )
```

```python
import functools
import math

import jax
import jax.numpy as jnp
from jax import lax
from jax.experimental import pallas as pl
from jax.experimental.pallas import tpu as pltpu
from jax.sharding import PartitionSpec as P

BF, F32 = jnp.bfloat16, jnp.float32
HALO = 7
SIDE = 8
VMEM = pl.BlockSpec(memory_space=pltpu.VMEM)


def call(body, out_shapes, args, scratch=(), limit=8, flops=10**9):
    return pl.pallas_call(
        body,
        out_shape=out_shapes,
        in_specs=[VMEM] * len(args),
        out_specs=jax.tree.map(lambda _: VMEM, out_shapes),
        scratch_shapes=list(scratch),
        cost_estimate=pl.CostEstimate(flops=flops, bytes_accessed=0, transcendentals=0),
        compiler_params=pltpu.CompilerParams(vmem_limit_bytes=limit * 1024 * 1024),
    )(*args)


def shape(dims, dtype=BF):
    return jax.ShapeDtypeStruct(dims, dtype)


def dot(a, b, dims=((1,), (0,))):
    return lax.dot_general(a, b, (dims, ((), ())), preferred_element_type=F32)


def picking(dims, rule):
    i, j = (lax.broadcasted_iota(jnp.int32, dims, axis) for axis in (0, 1))
    return jnp.where(rule(i, j), 1.0, 0.0).astype(BF)


def groups_of(rows, width):
    return -(-rows * width // 128)


def lanes_to_channels(row, owner, width, total):
    base = row * width % 128
    return picking(
        (128, total),
        lambda lane, channel: (lane >= base)
        & (lane < base + width)
        & (lane - base == channel - owner * width),
    )


def strip_rows(cot_ref):
    half_rows, width, cols = cot_ref.shape
    value = cot_ref[...].reshape(half_rows * width, cols)
    short = 128 * groups_of(half_rows, width) - half_rows * width
    if short:
        value = jnp.concatenate([value, jnp.zeros((short, cols), BF)], axis=0)
    return value


def strip_piece(value, tile, half_cols):
    pitch = half_cols + 2 * SIDE
    pick = picking(
        (pitch, value.shape[1]),
        lambda i, j: j == jnp.where(i < half_cols + SIDE, i, i - pitch) + tile * half_cols,
    )
    parts = [
        dot(pick, value[low : low + 128], ((1,), (1,))) for low in range(0, value.shape[0], 128)
    ]
    return jnp.concatenate(parts, axis=0).astype(BF)


def begin(out_ref):
    out_ref[...] = jnp.zeros(out_ref.shape, BF)


def pack_cols(count, half_cols, level_ref, cot_ref, begin_ref, *outs):
    me = lax.axis_index("gx")
    strip = strip_rows(cot_ref)
    level = level_ref[...].astype(F32)
    first, last = level[:, :SIDE], level[:, level.shape[1] - SIDE :]
    for turn in range(1, count):
        other = me ^ turn
        piece = strip_piece(strip, other, half_cols)
        cut = piece.shape[0]
        outs[turn - 1][0:cut] = piece
        edge = jnp.where(other == me + 1, last, first)
        outs[turn - 1][cut:] = edge.reshape(-1, 128).astype(BF)


def pack_rows(count, half_cols, level_ref, cot_ref, *refs):
    got = refs[: count - 1]
    kept_ref, cross_ref, inner_ref = refs[count - 1 :]
    me, core = lax.axis_index("gx"), lax.axis_index("gy") & 1
    rows, cols = level_ref.shape[0], level_ref.shape[1]
    half_rows, width = cot_ref.shape[0], cot_ref.shape[1]
    total = count * width
    pitch = half_cols + 2 * SIDE
    cut = groups_of(half_rows, width) * pitch
    mine = strip_piece(strip_rows(cot_ref), me, half_cols)
    right = jnp.zeros((rows * SIDE, 128), F32)
    left = jnp.zeros((rows * SIDE, 128), F32)
    for turn in range(1, count):
        edge = got[turn - 1][cut:].astype(F32)
        right = jnp.where(me ^ turn == me + 1, edge, right)
        left = jnp.where(me ^ turn == me - 1, edge, left)
    right, left = right.reshape(rows, SIDE, 128), left.reshape(rows, SIDE, 128)
    level = level_ref[...]
    gap = jnp.zeros((rows, 2 * pitch - cols - 2 * SIDE, 128), F32)
    edges = jnp.concatenate([right, gap, left], axis=1).astype(BF)
    wide = jnp.concatenate([level, edges], axis=1).reshape(2 * rows * pitch, 128)
    kept_ref[0 : 2 * rows * pitch] = wide
    cot = []
    picks = {}
    for row in range(half_rows):
        low = row * width // 128 * pitch
        value = jnp.zeros((pitch, total), F32)
        for turn in range(count):
            part = mine[low : low + pitch] if turn == 0 else got[turn - 1][low : low + pitch]
            key = (row * width % 128, turn)
            if key not in picks:
                picks[key] = lanes_to_channels(row, me ^ turn, width, total)
            value = value + dot(part, picks[key])
        value = value.astype(BF)
        cot.append(value)
        low = 2 * (rows + row) * pitch
        kept_ref[low : low + pitch] = value[:, :128]
        kept_ref[low + pitch : low + 2 * pitch] = value[:, 128:]
    edges = jnp.concatenate([right, left], axis=1).astype(BF)
    band = jnp.concatenate([level, edges], axis=1)
    cells = HALO * (cols + 2 * SIDE)
    for low, neck, is_cross in ((0, 0, core == 0), (rows - HALO, half_rows - 2, core == 1)):
        for ref, here in ((cross_ref, is_cross), (inner_ref, jnp.logical_not(is_cross))):

            @pl.when(here)
            def _(ref=ref, low=low, neck=neck):
                ref[0:cells] = band[low : low + HALO].reshape(cells, 128)
                for i in range(2):
                    spot = cells + 2 * pitch * i
                    ref[spot : spot + pitch] = cot[neck + i][:, :128]
                    ref[spot + pitch : spot + 2 * pitch] = cot[neck + i][:, 128:]


def turn_weights(wl_ref, wd_ref, wn_ref, wfwd_ref, wbwd_ref, wdt_ref, wnt_ref):
    zero = jnp.zeros((128, 128), BF)
    for ky in range(3):
        w = [wl_ref[3 * ky + kx] for kx in range(3)]
        t = [value.T for value in w]
        for ref, blocks in (
            (wfwd_ref, (w[1], w[0], w[2], w[1], w[0], zero, zero, w[2])),
            (wbwd_ref, (t[1], t[2], t[0], t[1], t[2], zero, zero, t[0])),
        ):
            for spot, block in enumerate(blocks):
                low = 512 * ky + 128 * (spot // 2)
                ref[low : low + 128, 128 * (spot % 2) : 128 * (spot % 2) + 128] = block
    for p in range(2):
        wdt_ref[:, 256 * p : 256 * p + 256] = wd_ref[256 * p : 256 * p + 256].T
    for k in range(9):
        total = wn_ref.shape[1]
        wnt_ref[total * k : total * k + total] = wn_ref[total * k : total * k + total].T


def sigmoid_slope(value):
    gate = jax.nn.sigmoid(value)
    return gate, gate + value * gate * (1.0 - gate)


def shifted(value):
    size = value.shape[1]
    return pltpu.roll(value, 1, 1), pltpu.roll(value, size - 1, 1)


def paired(value):
    return jnp.concatenate(
        [pltpu.roll(value[:, :, 128:], 1, 1), pltpu.roll(value[:, :, :128], value.shape[1] - 1, 1)],
        axis=2,
    ).astype(BF)


def dot_rows(a, b, step):
    return jnp.concatenate([dot(a[i : i + step], b) for i in range(0, a.shape[0], step)], axis=0)


def flat(value):
    return value.reshape(-1, value.shape[-1])


def main(
    sizes,
    kept_ref, cross_ref, inner_ref, wfwd, wbwd, wd_ref, wdt_ref, wn_ref, wnt_ref,
    sums_ref, send_ref, out_ref, grad_ref,
    field, pair, side, act, slope, neck, gate, cot_all, ngrad, lback, lgate, lside, spread,
):
    rows, half_rows, half_cols, _, _ = sizes
    cols = 2 * half_cols
    pitch = half_cols + 2 * SIDE
    total = wd_ref.shape[1]
    me, row = lax.axis_index("gx"), lax.axis_index("gy")
    row_end, col_end = lax.axis_size("gy") * half_rows, lax.axis_size("gx") * half_cols
    core = row & 1

    cells = HALO * (cols + 2 * SIDE)

    def take(ref, low, low_neck):
        band = ref[0:cells].reshape(HALO, cols + 2 * SIDE, 128).astype(F32)
        field[low : low + HALO, 0 : cols + SIDE] = band[:, : cols + SIDE]
        field[low : low + HALO, cols + SIDE : 2 * pitch - SIDE] = jnp.zeros(
            (HALO, 2 * pitch - cols - 2 * SIDE, 128), F32
        )
        field[low : low + HALO, 2 * pitch - SIDE :] = band[:, cols + SIDE :]
        for i in range(2):
            spot = cells + 2 * pitch * i
            cot_all[low_neck + i, :, :128] = ref[spot : spot + pitch]
            cot_all[low_neck + i, :, 128:] = ref[spot + pitch : spot + 2 * pitch]

    @pl.when(core == 0)
    def _():
        take(cross_ref, 0, 0)
        take(inner_ref, HALO + rows, 2 + half_rows)

    @pl.when(core == 1)
    def _():
        take(inner_ref, 0, 0)
        take(cross_ref, HALO + rows, 2 + half_rows)

    own = kept_ref[0 : 2 * rows * pitch].reshape(rows, 2 * pitch, 128)
    field[HALO : HALO + rows] = own.astype(F32)
    for row_in in range(half_rows):
        low = 2 * (rows + row_in) * pitch
        cot_all[2 + row_in, :, :128] = kept_ref[low : low + pitch]
        cot_all[2 + row_in, :, 128:] = kept_ref[low + pitch : low + 2 * pitch]
    even = field[:, pl.ds(0, pitch, stride=2), :]
    odd = field[:, pl.ds(1, pitch, stride=2), :]
    both = jnp.concatenate([even, odd], axis=2)
    pair[...] = both.astype(BF)
    side[...] = paired(both)

    act_rows = act.shape[0]
    step = act_rows // 2
    for low in range(0, act_rows, step):
        taken = [
            flat(ref[low + ky : low + ky + step]) for ky in range(3) for ref in (pair, side)
        ]
        pre = dot_rows(jnp.concatenate(taken, axis=1), wfwd[...], step * pitch // 3)
        sig, slp = sigmoid_slope(pre)
        own = flat(pair[low + 1 : low + 1 + step]).astype(F32)
        act[low : low + step] = (own + pre * sig).astype(BF).reshape(step, pitch, 256)
        slope[low : low + step] = slp.reshape(step, pitch, 256)

    def inside(value, first_row):
        r = lax.broadcasted_iota(jnp.int32, value.shape, 0) + (row * half_rows + first_row)
        c = lax.broadcasted_iota(jnp.int32, value.shape, 1)
        c = jnp.where(c < half_cols + SIDE, c, c - pitch) + me * half_cols
        ok = (r >= 0) & (r < row_end) & (c >= 0) & (c < col_end)
        return jnp.where(ok, value, 0.0)

    neck_rows = act_rows // 2
    grid = act[...].reshape(neck_rows, 2, pitch, 256)
    both = jnp.concatenate([flat(grid[:, 0]), flat(grid[:, 1])], axis=1)
    value = dot_rows(both, wd_ref[...], 5 * pitch).reshape(neck_rows, pitch, total)
    value = inside(value, -3).astype(BF)
    before, behind = shifted(value.astype(F32))
    neck[0], neck[1], neck[2] = before.astype(BF), value, behind.astype(BF)

    gate_rows = neck_rows - 2
    taken = [flat(neck[kx, ky : ky + gate_rows]) for ky in range(3) for kx in range(3)]
    pre = dot_rows(jnp.concatenate(taken, axis=1), wn_ref[...], 4 * pitch)
    sig, slp = sigmoid_slope(pre)
    own = flat(neck[1, 1 : 1 + gate_rows]).astype(F32)
    out = (own + pre * sig).astype(BF).reshape(gate_rows, pitch, total)
    out = out[2 : 2 + half_rows, :half_cols].reshape(half_rows * half_cols, total)
    out_ref[...] = out
    value = (flat(cot_all[...]).astype(F32) * slp).astype(BF).reshape(gate_rows, pitch, total)
    before, behind = shifted(value.astype(F32))
    gate[0], gate[1], gate[2] = before.astype(BF), value, behind.astype(BF)

    grad_rows = gate_rows - 2
    taken = [
        flat(gate[2 - kx, 2 - ky : 2 - ky + grad_rows]) for ky in range(3) for kx in range(3)
    ]
    back = dot_rows(jnp.concatenate(taken, axis=1), wnt_ref[...], 3 * pitch)
    value = flat(cot_all[1 : 1 + grad_rows]).astype(F32) + back
    value = inside(value.reshape(grad_rows, pitch, total), -1)
    ngrad[...] = value.astype(BF)

    value = dot_rows(flat(ngrad[...]), wdt_ref[...], 3 * pitch).reshape(grad_rows, pitch, 512)
    for p in range(2):
        for i in range(grad_rows):
            lback[2 * i + p] = value[i, :, 256 * p : 256 * p + 256]
    value = lback[...] * slope[4 : 4 + 2 * grad_rows]
    value = value.astype(BF)
    lgate[...] = value
    lside[...] = paired(value.astype(F32))

    taken = [
        flat(ref[3 - ky : 3 - ky + rows, :half_cols]) for ky in range(3) for ref in (lgate, lside)
    ]
    value = dot_rows(jnp.concatenate(taken, axis=1), wbwd[...], 4 * half_cols).reshape(rows, half_cols, 256)
    value = value + lback[2 : 2 + rows, :half_cols]
    spread[:, pl.ds(0, half_cols, stride=2), :] = value[:, :, :128]
    spread[:, pl.ds(1, half_cols, stride=2), :] = value[:, :, 128:]
    grad_ref[...] = spread[...].astype(BF)

    weight_sums(sizes, sums_ref, neck, gate, act, ngrad, pair, side, lgate)
    half = send_ref.shape[0]
    send_ref[...] = sums_ref[pl.ds(pl.multiple_of((1 - core) * half, 16), half), :]


def weight_sums(sizes, sums_ref, neck, gate, act, ngrad, pair, side, lgate):
    rows, half_rows, half_cols, level_scale, neck_scale = sizes
    pitch = act.shape[1]
    place = 0

    def put(value):
        nonlocal place
        sums_ref[place : place + value.shape[0]] = value
        place += value.shape[0]

    own = flat(gate[1, 2 : 2 + half_rows, :half_cols])
    for ky in range(3):
        for kx in range(3):
            lhs = flat(neck[kx, 2 + ky : 2 + ky + half_rows, :half_cols])
            value = (dot(lhs, own, ((0,), (0,))) * neck_scale).astype(BF)
            put(value[:, :128])
            put(value[:, 128:])
    own = flat(ngrad[1 : 1 + half_rows, :half_cols])
    grid = act[6 : 6 + rows].reshape(half_rows, 2, pitch, 256)
    for p in range(2):
        lhs = flat(grid[:, p, :half_cols])
        value = (dot(lhs, own, ((0,), (0,))) * neck_scale).astype(BF)
        for q in range(2):
            for h in range(2):
                put(value[128 * q : 128 * q + 128, 128 * h : 128 * h + 128])
    own = flat(lgate[2 : 2 + rows, :half_cols])
    for ky in range(3):
        m = dot(flat(pair[6 + ky : 6 + ky + rows, :half_cols]), own, ((0,), (0,)))
        s = dot(flat(side[6 + ky : 6 + ky + rows, :half_cols]), own, ((0,), (0,)))
        for value in (
            m[:128, 128:] + s[:128, :128],
            m[:128, :128] + m[128:, 128:],
            m[128:, :128] + s[128:, 128:],
        ):
            put((value * level_scale).astype(BF))
    if place < sums_ref.shape[0]:
        put(jnp.zeros((sums_ref.shape[0] - place, 128), BF))


def pack_neck(count, half_rows, width, out_ref, pieces_ref):
    me = lax.axis_index("gx")
    cells, total = out_ref.shape
    half_cols, per = cells // half_rows, 128 // width
    for turn in range(count):
        for low in range(0, half_rows, per):
            piece = jnp.zeros((half_cols, 128), F32)
            for r in range(low, min(half_rows, low + per)):
                pick = lanes_to_channels(r, me ^ turn, width, total)
                piece = piece + dot(out_ref[half_cols * r : half_cols * r + half_cols], pick, ((1,), (1,)))
            group = low // per
            pieces_ref[turn, half_cols * group : half_cols * group + half_cols] = piece.astype(BF)


def add_cores(count, sums_ref, got_ref, pieces_ref, own_ref, *outs):
    me, core = lax.axis_index("gx"), lax.axis_index("gy") & 1
    part = own_ref.shape[0]
    for turn in range(count):
        mine = pl.ds(pl.multiple_of((core * count + (me ^ turn)) * part, 16), part)
        theirs = pl.ds(pl.multiple_of((me ^ turn) * part, 16), part)
        value = sums_ref[mine, :].astype(F32) + got_ref[theirs, :].astype(F32)
        if turn == 0:
            own_ref[...] = value
        else:
            outs[turn - 1][0:part] = value.astype(BF)
            outs[turn - 1][part:] = pieces_ref[turn]


def add_cols(count, z_count, own_ref, *refs):
    got = refs[: count - 1]
    first_ref, outs, total = refs[count - 1], refs[count:-1], refs[-1]
    z = lax.axis_index("gy") // 2
    part, unit = own_ref.shape[0], first_ref.shape[0]
    value = own_ref[...]
    for ref in got:
        value = value + ref[0:part].astype(F32)
    total[0:part] = value
    if part < total.shape[0]:
        total[part:] = jnp.zeros((total.shape[0] - part, 128), F32)
    for turn in range(z_count):
        value = total[pl.ds(pl.multiple_of((z ^ turn) * unit, 16), unit), :]
        if turn == 0:
            first_ref[...] = value
        else:
            outs[turn - 1][...] = value.astype(BF)


def place_neck(count, part, pieces_ref, *refs):
    got, neck_ref = refs[:-1], refs[-1]
    me = lax.axis_index("gx")
    half_rows, width, cols = neck_ref.shape
    half_cols = cols // count
    for group in range(groups_of(half_rows, width)):
        value = jnp.zeros((128, cols), F32)
        here = slice(half_cols * group, half_cols * group + half_cols)
        for turn in range(count):
            piece = pieces_ref[0, here] if turn == 0 else got[turn - 1][part:][here]
            pick = picking((half_cols, cols), lambda i, j, t=turn: j == i + (me ^ t) * half_cols)
            value = value + dot(piece, pick, ((0,), (0,)))
        per = min(half_rows, 128 // width)
        value = value[: per * width].astype(BF).reshape(per, width, cols)
        neck_ref[group * per : group * per + per] = value


def add_rows(first_ref, *refs):
    value = first_ref[...]
    for ref in refs[:-1]:
        value = value + ref[...].astype(F32)
    refs[-1][...] = value.astype(BF)


def join(z_count, *refs):
    pieces, (out_ref, store) = refs[:z_count], refs[z_count:]
    z = lax.axis_index("gy") // 2
    unit = pieces[0].shape[0]
    for turn in range(z_count):
        store[pl.ds(pl.multiple_of((z ^ turn) * unit, 16), unit), :] = pieces[turn][...]
    out_ref[...] = store[0 : out_ref.shape[0]]


def finish(count, *refs):
    ours, theirs = refs[:count], refs[count : 2 * count]
    level_ref, down_ref, neck_ref, store = refs[2 * count :]
    me, row = lax.axis_index("gx"), lax.axis_index("gy")
    part = ours[0].shape[0]
    for flip, group in ((0, ours), (1, theirs)):
        for turn in range(count):
            place = (((row & 1) ^ flip) * count + (me ^ turn)) * part
            store[pl.ds(pl.multiple_of(place, 16), part), :] = group[turn][...]
    place = 0
    for ref in (neck_ref, down_ref):
        deep = ref.shape[1]
        for i in range(ref.shape[0]):
            for h in range(2):
                ref[i, :, 128 * h : 128 * h + 128] = store[place : place + deep]
                place += deep
    for i in range(level_ref.shape[0]):
        level_ref[i] = store[place : place + 128]
        place += 128


def local(level_in, w_level, w_down, w_neck, cotangent):
    rows, cols, _ = level_in.shape
    half_rows, half_cols = rows // 2, cols // 2
    total = w_neck.shape[3]
    count, gy_count = lax.axis_size("gx"), lax.axis_size("gy")
    z_count = gy_count // 2
    pitch = half_cols + 2 * SIDE
    axes = ("gy", "gx")
    spots = [(y, x) for y in range(gy_count) for x in range(count)]

    def permute(value, target):
        pairs = [(y * count + x, target(y, x)) for y, x in spots]
        return lax.ppermute(value, axes, [(a, b) for a, b in pairs if b is not None])

    def by_col(value, turn):
        return permute(value, lambda y, x: y * count + (x ^ turn))

    def by_z(value, turn):
        return permute(value, lambda y, x: (y ^ (2 * turn)) * count + x)

    def by_core(value):
        return permute(value, lambda y, x: (y ^ 1) * count + x)

    def by_seam(value):
        def target(y, x):
            other = y + 1 if y % 2 else y - 1
            return other * count + x if 0 <= other < gy_count else None

        return permute(value, target)

    strip = jnp.swapaxes(cotangent, 1, 2)
    width = strip.shape[1]
    packed = shape((groups_of(half_rows, width) * pitch + rows * SIDE, 128))
    first = call(begin, shape((16, 128)), (), flops=10**10)
    sent = call(
        functools.partial(pack_cols, count, half_cols), [packed] * (count - 1), (level_in, strip, first)
    )
    got = [by_col(value, turn + 1) for turn, value in enumerate(sent)]
    band = shape((HALO * (cols + 2 * SIDE) + 4 * pitch, 128))
    kept, cross, inner = call(
        functools.partial(pack_rows, count, half_cols),
        [shape((3 * rows * pitch, 128)), band, band],
        (level_in, strip, *got),
    )
    cross, inner = by_seam(cross), by_core(inner)

    wl = w_level.reshape(9, 128, 128)
    wd = w_down.reshape(512, total)
    wn = w_neck.reshape(9 * total, total)
    wfwd, wbwd, wdt, wnt = call(
        turn_weights,
        [shape((1536, 256)), shape((1536, 256)), shape((total, 512)), shape(wn.shape)],
        (wl, wd, wn),
    )
    pixels = rows * cols * count * gy_count
    used = 2 * 9 * total + 4 * 2 * 128 + 9 * 128
    part = -(-used // (2 * count * 16)) * 16
    half = part * count
    unit = -(-part // (z_count * 16)) * 16
    tiles = groups_of(half_rows, width) * half_cols
    sizes = (
        rows, half_rows, half_cols,
        1.0 / math.sqrt(pixels), 1.0 / math.sqrt(pixels // 4),
    )
    far = rows + 2 * HALO
    sums, send, out, grad_input = call(
        functools.partial(main, sizes),
        [shape((2 * half, 128)), shape((half, 128)), shape((half_rows * half_cols, total)), shape(level_in.shape)],
        (kept, cross, inner, wfwd, wbwd, wd, wdt, wn, wnt),
        [
            pltpu.VMEM((far, 2 * pitch, 128), F32),
            pltpu.VMEM((far, pitch, 256), BF),
            pltpu.VMEM((far, pitch, 256), BF),
            pltpu.VMEM((far - 2, pitch, 256), BF),
            pltpu.VMEM((far - 2, pitch, 256), F32),
            pltpu.VMEM((3, half_rows + 6, pitch, total), BF),
            pltpu.VMEM((3, half_rows + 4, pitch, total), BF),
            pltpu.VMEM((half_rows + 4, pitch, total), BF),
            pltpu.VMEM((half_rows + 2, pitch, total), BF),
            pltpu.VMEM((rows + 4, pitch, 256), F32),
            pltpu.VMEM((rows + 4, pitch, 256), BF),
            pltpu.VMEM((rows + 4, pitch, 256), BF),
            pltpu.VMEM((rows, cols, 128), F32),
        ],
        limit=20,
        flops=6 * 10**9,
    )

    pieces = call(
        functools.partial(pack_neck, count, half_rows, width), shape((count, tiles, 128)), (out,)
    )
    own, *sent = call(
        functools.partial(add_cores, count),
        [shape((part, 128), F32)] + [shape((part + tiles, 128))] * (count - 1),
        (sums, by_core(send), pieces),
    )
    got = [by_col(value, turn + 1) for turn, value in enumerate(sent)]
    own, *sent = call(
        functools.partial(add_cols, count, z_count),
        [shape((unit, 128), F32)] + [shape((unit, 128))] * (z_count - 1),
        (own, *got),
        [pltpu.VMEM((unit * z_count, 128), F32)],
    )
    neck_out = call(functools.partial(place_neck, count, part), shape(strip.shape), (pieces, *got))
    got = [by_z(value, turn + 1) for turn, value in enumerate(sent)]
    own = call(add_rows, shape((unit, 128)), (own, *got))
    own = call(
        functools.partial(join, z_count),
        shape((part, 128)),
        [own] + [by_z(own, turn) for turn in range(1, z_count)],
        [pltpu.VMEM((unit * z_count, 128), BF)],
    )
    ours = [own] + [by_col(own, turn) for turn in range(1, count)]
    theirs = [by_core(value) for value in ours]
    grad_level, grad_down, grad_neck = call(
        functools.partial(finish, count),
        [shape((9, 128, 128)), shape((4, 128, total)), shape((9, total, total))],
        (*ours, *theirs),
        [pltpu.VMEM((2 * half, 128), BF)],
    )
    return (
        jnp.swapaxes(neck_out, 1, 2),
        grad_input,
        grad_level.reshape(w_level.shape),
        grad_down.reshape(w_down.shape),
        grad_neck.reshape(w_neck.shape),
    )


def solution(mesh):
    return jax.shard_map(
        local,
        mesh=mesh,
        in_specs=(P("gy", "gx", None), P(), P(), P(), P("gy", None, "gx")),
        out_specs=(P("gy", None, "gx"), P("gy", "gx", None), P(), P(), P()),
        check_vma=False,
    )
```

```python
import functools
import math

import jax
import jax.numpy as jnp
from jax import lax
from jax.experimental import pallas as pl
from jax.experimental.pallas import tpu as pltpu
from jax.sharding import PartitionSpec as P

BF, F32 = jnp.bfloat16, jnp.float32
HALO = 7
SIDE = 8
VMEM = pl.BlockSpec(memory_space=pltpu.VMEM)


def call(body, out_shapes, args, scratch=(), limit=8, flops=10**9):
    return pl.pallas_call(
        body,
        out_shape=out_shapes,
        in_specs=[VMEM] * len(args),
        out_specs=jax.tree.map(lambda _: VMEM, out_shapes),
        scratch_shapes=list(scratch),
        cost_estimate=pl.CostEstimate(flops=flops, bytes_accessed=0, transcendentals=0),
        compiler_params=pltpu.CompilerParams(vmem_limit_bytes=limit * 1024 * 1024),
    )(*args)


def shape(dims, dtype=BF):
    return jax.ShapeDtypeStruct(dims, dtype)


def dot(a, b, dims=((1,), (0,))):
    return lax.dot_general(a, b, (dims, ((), ())), preferred_element_type=F32)


def picking(dims, rule):
    i, j = (lax.broadcasted_iota(jnp.int32, dims, axis) for axis in (0, 1))
    return jnp.where(rule(i, j), 1.0, 0.0).astype(BF)


def groups_of(rows, width):
    return -(-rows * width // 128)


def lanes_to_channels(row, owner, width, total):
    base = row * width % 128
    return picking(
        (128, total),
        lambda lane, channel: (lane >= base)
        & (lane < base + width)
        & (lane - base == channel - owner * width),
    )


def strip_rows(cot_ref):
    half_rows, width, cols = cot_ref.shape
    value = cot_ref[...].reshape(half_rows * width, cols)
    short = 128 * groups_of(half_rows, width) - half_rows * width
    if short:
        value = jnp.concatenate([value, jnp.zeros((short, cols), BF)], axis=0)
    return value


def strip_piece(value, tile, half_cols):
    pitch = half_cols + 2 * SIDE
    pick = picking(
        (pitch, value.shape[1]),
        lambda i, j: j == jnp.where(i < half_cols + SIDE, i, i - pitch) + tile * half_cols,
    )
    parts = [
        dot(pick, value[low : low + 128], ((1,), (1,))) for low in range(0, value.shape[0], 128)
    ]
    return jnp.concatenate(parts, axis=0).astype(BF)


def begin(out_ref):
    out_ref[...] = jnp.zeros(out_ref.shape, BF)


def pack_cols(count, half_cols, level_ref, cot_ref, begin_ref, *outs):
    me = lax.axis_index("gx")
    strip = strip_rows(cot_ref)
    level = level_ref[...].astype(F32)
    first, last = level[:, :SIDE], level[:, level.shape[1] - SIDE :]
    for turn in range(1, count):
        other = me ^ turn
        piece = strip_piece(strip, other, half_cols)
        cut = piece.shape[0]
        outs[turn - 1][0:cut] = piece
        edge = jnp.where(other == me + 1, last, first)
        outs[turn - 1][cut:] = edge.reshape(-1, 128).astype(BF)


def pack_rows(count, half_cols, level_ref, cot_ref, *refs):
    got = refs[: count - 1]
    kept_ref, cross_ref, inner_ref = refs[count - 1 :]
    me, core = lax.axis_index("gx"), lax.axis_index("gy") & 1
    rows, cols = level_ref.shape[0], level_ref.shape[1]
    half_rows, width = cot_ref.shape[0], cot_ref.shape[1]
    total = count * width
    pitch = half_cols + 2 * SIDE
    cut = groups_of(half_rows, width) * pitch
    mine = strip_piece(strip_rows(cot_ref), me, half_cols)
    right = jnp.zeros((rows * SIDE, 128), F32)
    left = jnp.zeros((rows * SIDE, 128), F32)
    for turn in range(1, count):
        edge = got[turn - 1][cut:].astype(F32)
        right = jnp.where(me ^ turn == me + 1, edge, right)
        left = jnp.where(me ^ turn == me - 1, edge, left)
    right, left = right.reshape(rows, SIDE, 128), left.reshape(rows, SIDE, 128)
    level = level_ref[...]
    gap = jnp.zeros((rows, 2 * pitch - cols - 2 * SIDE, 128), F32)
    edges = jnp.concatenate([right, gap, left], axis=1).astype(BF)
    wide = jnp.concatenate([level, edges], axis=1).reshape(2 * rows * pitch, 128)
    kept_ref[0 : 2 * rows * pitch] = wide
    cot = []
    picks = {}
    for row in range(half_rows):
        low = row * width // 128 * pitch
        value = jnp.zeros((pitch, total), F32)
        for turn in range(count):
            part = mine[low : low + pitch] if turn == 0 else got[turn - 1][low : low + pitch]
            key = (row * width % 128, turn)
            if key not in picks:
                picks[key] = lanes_to_channels(row, me ^ turn, width, total)
            value = value + dot(part, picks[key])
        value = value.astype(BF)
        cot.append(value)
        low = 2 * (rows + row) * pitch
        kept_ref[low : low + pitch] = value[:, :128]
        kept_ref[low + pitch : low + 2 * pitch] = value[:, 128:]
    edges = jnp.concatenate([right, left], axis=1).astype(BF)
    band = jnp.concatenate([level, edges], axis=1)
    cells = HALO * (cols + 2 * SIDE)
    for low, neck, is_cross in ((0, 0, core == 0), (rows - HALO, half_rows - 2, core == 1)):
        for ref, here in ((cross_ref, is_cross), (inner_ref, jnp.logical_not(is_cross))):

            @pl.when(here)
            def _(ref=ref, low=low, neck=neck):
                ref[0:cells] = band[low : low + HALO].reshape(cells, 128)
                for i in range(2):
                    spot = cells + 2 * pitch * i
                    ref[spot : spot + pitch] = cot[neck + i][:, :128]
                    ref[spot + pitch : spot + 2 * pitch] = cot[neck + i][:, 128:]


def turn_weights(wl_ref, wd_ref, wn_ref, wfwd_ref, wbwd_ref, wdt_ref, wnt_ref):
    zero = jnp.zeros((128, 128), BF)
    for ky in range(3):
        w = [wl_ref[3 * ky + kx] for kx in range(3)]
        t = [value.T for value in w]
        for ref, blocks in (
            (wfwd_ref, (w[1], w[0], w[2], w[1], w[0], zero, zero, w[2])),
            (wbwd_ref, (t[1], t[2], t[0], t[1], t[2], zero, zero, t[0])),
        ):
            for spot, block in enumerate(blocks):
                low = 512 * ky + 128 * (spot // 2)
                ref[low : low + 128, 128 * (spot % 2) : 128 * (spot % 2) + 128] = block
    for p in range(2):
        wdt_ref[:, 256 * p : 256 * p + 256] = wd_ref[256 * p : 256 * p + 256].T
    for k in range(9):
        total = wn_ref.shape[1]
        wnt_ref[total * k : total * k + total] = wn_ref[total * k : total * k + total].T


def sigmoid_slope(value):
    gate = jax.nn.sigmoid(value)
    return gate, gate + value * gate * (1.0 - gate)


def shifted(value):
    size = value.shape[1]
    return pltpu.roll(value, 1, 1), pltpu.roll(value, size - 1, 1)


def paired(value):
    return jnp.concatenate(
        [pltpu.roll(value[:, :, 128:], 1, 1), pltpu.roll(value[:, :, :128], value.shape[1] - 1, 1)],
        axis=2,
    ).astype(BF)


def dot_rows(a, b, step):
    return jnp.concatenate([dot(a[i : i + step], b) for i in range(0, a.shape[0], step)], axis=0)


def flat(value):
    return value.reshape(-1, value.shape[-1])


def main(
    sizes,
    kept_ref, cross_ref, inner_ref, wfwd, wbwd, wd_ref, wdt_ref, wn_ref, wnt_ref,
    sums_ref, send_ref, out_ref, grad_ref,
    field, pair, side, act, slope, neck, gate, cot_all, ngrad, lback, lgate, lside, spread,
):
    rows, half_rows, half_cols, _, _ = sizes
    cols = 2 * half_cols
    pitch = half_cols + 2 * SIDE
    total = wd_ref.shape[1]
    me, row = lax.axis_index("gx"), lax.axis_index("gy")
    row_end, col_end = lax.axis_size("gy") * half_rows, lax.axis_size("gx") * half_cols
    core = row & 1

    cells = HALO * (cols + 2 * SIDE)

    def take(ref, low, low_neck):
        band = ref[0:cells].reshape(HALO, cols + 2 * SIDE, 128).astype(F32)
        field[low : low + HALO, 0 : cols + SIDE] = band[:, : cols + SIDE]
        field[low : low + HALO, cols + SIDE : 2 * pitch - SIDE] = jnp.zeros(
            (HALO, 2 * pitch - cols - 2 * SIDE, 128), F32
        )
        field[low : low + HALO, 2 * pitch - SIDE :] = band[:, cols + SIDE :]
        for i in range(2):
            spot = cells + 2 * pitch * i
            cot_all[low_neck + i, :, :128] = ref[spot : spot + pitch]
            cot_all[low_neck + i, :, 128:] = ref[spot + pitch : spot + 2 * pitch]

    @pl.when(core == 0)
    def _():
        take(cross_ref, 0, 0)
        take(inner_ref, HALO + rows, 2 + half_rows)

    @pl.when(core == 1)
    def _():
        take(inner_ref, 0, 0)
        take(cross_ref, HALO + rows, 2 + half_rows)

    own = kept_ref[0 : 2 * rows * pitch].reshape(rows, 2 * pitch, 128)
    field[HALO : HALO + rows] = own.astype(F32)
    for row_in in range(half_rows):
        low = 2 * (rows + row_in) * pitch
        cot_all[2 + row_in, :, :128] = kept_ref[low : low + pitch]
        cot_all[2 + row_in, :, 128:] = kept_ref[low + pitch : low + 2 * pitch]
    even = field[:, pl.ds(0, pitch, stride=2), :]
    odd = field[:, pl.ds(1, pitch, stride=2), :]
    both = jnp.concatenate([even, odd], axis=2)
    pair[...] = both.astype(BF)
    side[...] = paired(both)

    act_rows = act.shape[0]
    step = act_rows // 2
    for low in range(0, act_rows, step):
        taken = [
            flat(ref[low + ky : low + ky + step]) for ky in range(3) for ref in (pair, side)
        ]
        pre = dot_rows(jnp.concatenate(taken, axis=1), wfwd[...], step * pitch // 3)
        sig, slp = sigmoid_slope(pre)
        own = flat(pair[low + 1 : low + 1 + step]).astype(F32)
        act[low : low + step] = (own + pre * sig).astype(BF).reshape(step, pitch, 256)
        slope[low : low + step] = slp.reshape(step, pitch, 256)

    def inside(value, first_row):
        r = lax.broadcasted_iota(jnp.int32, value.shape, 0) + (row * half_rows + first_row)
        c = lax.broadcasted_iota(jnp.int32, value.shape, 1)
        c = jnp.where(c < half_cols + SIDE, c, c - pitch) + me * half_cols
        ok = (r >= 0) & (r < row_end) & (c >= 0) & (c < col_end)
        return jnp.where(ok, value, 0.0)

    neck_rows = act_rows // 2
    grid = act[...].reshape(neck_rows, 2, pitch, 256)
    both = jnp.concatenate([flat(grid[:, 0]), flat(grid[:, 1])], axis=1)
    value = dot_rows(both, wd_ref[...], 5 * pitch).reshape(neck_rows, pitch, total)
    value = inside(value, -3).astype(BF)
    before, behind = shifted(value.astype(F32))
    neck[0], neck[1], neck[2] = before.astype(BF), value, behind.astype(BF)

    gate_rows = neck_rows - 2
    taken = [flat(neck[kx, ky : ky + gate_rows]) for ky in range(3) for kx in range(3)]
    pre = dot_rows(jnp.concatenate(taken, axis=1), wn_ref[...], 4 * pitch)
    sig, slp = sigmoid_slope(pre)
    own = flat(neck[1, 1 : 1 + gate_rows]).astype(F32)
    out = (own + pre * sig).astype(BF).reshape(gate_rows, pitch, total)
    out = out[2 : 2 + half_rows, :half_cols].reshape(half_rows * half_cols, total)
    out_ref[...] = out
    value = (flat(cot_all[...]).astype(F32) * slp).astype(BF).reshape(gate_rows, pitch, total)
    before, behind = shifted(value.astype(F32))
    gate[0], gate[1], gate[2] = before.astype(BF), value, behind.astype(BF)

    grad_rows = gate_rows - 2
    taken = [
        flat(gate[2 - kx, 2 - ky : 2 - ky + grad_rows]) for ky in range(3) for kx in range(3)
    ]
    back = dot_rows(jnp.concatenate(taken, axis=1), wnt_ref[...], 3 * pitch)
    value = flat(cot_all[1 : 1 + grad_rows]).astype(F32) + back
    value = inside(value.reshape(grad_rows, pitch, total), -1)
    ngrad[...] = value.astype(BF)

    value = dot_rows(flat(ngrad[...]), wdt_ref[...], 3 * pitch).reshape(grad_rows, pitch, 512)
    for p in range(2):
        for i in range(grad_rows):
            lback[2 * i + p] = value[i, :, 256 * p : 256 * p + 256]
    value = lback[...] * slope[4 : 4 + 2 * grad_rows]
    value = value.astype(BF)
    lgate[...] = value
    lside[...] = paired(value.astype(F32))

    taken = [
        flat(ref[3 - ky : 3 - ky + rows, :half_cols]) for ky in range(3) for ref in (lgate, lside)
    ]
    value = dot_rows(jnp.concatenate(taken, axis=1), wbwd[...], 4 * half_cols).reshape(rows, half_cols, 256)
    value = value + lback[2 : 2 + rows, :half_cols]
    spread[:, pl.ds(0, half_cols, stride=2), :] = value[:, :, :128]
    spread[:, pl.ds(1, half_cols, stride=2), :] = value[:, :, 128:]
    grad_ref[...] = spread[...].astype(BF)

    weight_sums(sizes, sums_ref, neck, gate, act, ngrad, pair, side, lgate)
    half = send_ref.shape[0]
    send_ref[...] = sums_ref[pl.ds(pl.multiple_of((1 - core) * half, 16), half), :]


def weight_sums(sizes, sums_ref, neck, gate, act, ngrad, pair, side, lgate):
    rows, half_rows, half_cols, level_scale, neck_scale = sizes
    pitch = act.shape[1]
    place = 0

    def put(value):
        nonlocal place
        sums_ref[place : place + value.shape[0]] = value
        place += value.shape[0]

    own = flat(gate[1, 2 : 2 + half_rows, :half_cols])
    for ky in range(3):
        for kx in range(3):
            lhs = flat(neck[kx, 2 + ky : 2 + ky + half_rows, :half_cols])
            value = (dot(lhs, own, ((0,), (0,))) * neck_scale).astype(BF)
            put(value[:, :128])
            put(value[:, 128:])
    own = flat(ngrad[1 : 1 + half_rows, :half_cols])
    grid = act[6 : 6 + rows].reshape(half_rows, 2, pitch, 256)
    for p in range(2):
        lhs = flat(grid[:, p, :half_cols])
        value = (dot(lhs, own, ((0,), (0,))) * neck_scale).astype(BF)
        for q in range(2):
            for h in range(2):
                put(value[128 * q : 128 * q + 128, 128 * h : 128 * h + 128])
    own = flat(lgate[2 : 2 + rows, :half_cols])
    for ky in range(3):
        m = dot(flat(pair[6 + ky : 6 + ky + rows, :half_cols]), own, ((0,), (0,)))
        s = dot(flat(side[6 + ky : 6 + ky + rows, :half_cols]), own, ((0,), (0,)))
        for value in (
            m[:128, 128:] + s[:128, :128],
            m[:128, :128] + m[128:, 128:],
            m[128:, :128] + s[128:, 128:],
        ):
            put((value * level_scale).astype(BF))
    if place < sums_ref.shape[0]:
        put(jnp.zeros((sums_ref.shape[0] - place, 128), BF))


def pack_neck(count, half_rows, width, out_ref, pieces_ref):
    me = lax.axis_index("gx")
    cells, total = out_ref.shape
    half_cols, per = cells // half_rows, 128 // width
    for turn in range(count):
        for low in range(0, half_rows, per):
            piece = jnp.zeros((half_cols, 128), F32)
            for r in range(low, min(half_rows, low + per)):
                pick = lanes_to_channels(r, me ^ turn, width, total)
                piece = piece + dot(out_ref[half_cols * r : half_cols * r + half_cols], pick, ((1,), (1,)))
            group = low // per
            pieces_ref[turn, half_cols * group : half_cols * group + half_cols] = piece.astype(BF)


def add_cores(count, cut, sums_ref, got_ref, pieces_ref, own_ref, *outs):
    me, core = lax.axis_index("gx"), lax.axis_index("gy") & 1
    part = own_ref.shape[0]
    early, late = outs[: count - 1], outs[count - 1 :]
    for turn in range(count):
        mine = pl.ds(pl.multiple_of((core * count + (me ^ turn)) * part, 16), part)
        theirs = pl.ds(pl.multiple_of((me ^ turn) * part, 16), part)
        value = sums_ref[mine, :].astype(F32) + got_ref[theirs, :].astype(F32)
        if turn == 0:
            own_ref[...] = value
        else:
            early[turn - 1][...] = value[:cut].astype(BF)
            late[turn - 1][0 : part - cut] = value[cut:].astype(BF)
            late[turn - 1][part - cut :] = pieces_ref[turn]


def row_turns(z_count):
    return [*range(2, z_count), 1] if z_count > 1 else []


def add_cols(count, z_count, low, size, own_ref, *refs):
    got = refs[: count - 1]
    first_ref, outs, total = refs[count - 1], refs[count:-1], refs[-1]
    z = lax.axis_index("gy") // 2
    unit = first_ref.shape[0]
    value = own_ref[low : low + size]
    for ref in got:
        value = value + ref[0:size].astype(F32)
    total[0:size] = value
    if size < total.shape[0]:
        total[size:] = jnp.zeros((total.shape[0] - size, 128), F32)
    for turn in range(z_count):
        value = total[pl.ds(pl.multiple_of((z ^ turn) * unit, 16), unit), :]
        if turn == 0:
            first_ref[...] = value
        else:
            outs[row_turns(z_count).index(turn)][...] = value.astype(BF)


def place_neck(count, part, pieces_ref, *refs):
    got, neck_ref = refs[:-1], refs[-1]
    me = lax.axis_index("gx")
    half_rows, width, cols = neck_ref.shape
    half_cols = cols // count
    for group in range(groups_of(half_rows, width)):
        value = jnp.zeros((128, cols), F32)
        here = slice(half_cols * group, half_cols * group + half_cols)
        for turn in range(count):
            piece = pieces_ref[0, here] if turn == 0 else got[turn - 1][part:][here]
            pick = picking((half_cols, cols), lambda i, j, t=turn: j == i + (me ^ t) * half_cols)
            value = value + dot(piece, pick, ((0,), (0,)))
        per = min(half_rows, 128 // width)
        value = value[: per * width].astype(BF).reshape(per, width, cols)
        neck_ref[group * per : group * per + per] = value


def add_rows(z_count, *refs):
    low = 0
    for group in (refs[:z_count], refs[z_count:-1]):
        value = group[0][...]
        for ref in group[1:]:
            value = value + ref[...].astype(F32)
        refs[-1][low : low + value.shape[0]] = value.astype(BF)
        low += value.shape[0]


def join(z_count, cut, unit, *refs):
    pieces, (out_ref, store) = refs[:z_count], refs[z_count:]
    z = lax.axis_index("gy") // 2
    rest = pieces[0].shape[0] - unit
    for turn in range(z_count):
        here = z ^ turn
        store[pl.ds(pl.multiple_of(here * unit, 16), unit), :] = pieces[turn][0:unit]
        here = unit * z_count + here * rest
        store[pl.ds(pl.multiple_of(here, 16), rest), :] = pieces[turn][unit:]
    out_ref[0:cut] = store[0:cut]
    out_ref[cut:] = store[unit * z_count : unit * z_count + out_ref.shape[0] - cut]


def finish(count, *refs):
    ours, theirs = refs[:count], refs[count : 2 * count]
    level_ref, down_ref, neck_ref, store = refs[2 * count :]
    me, row = lax.axis_index("gx"), lax.axis_index("gy")
    part = ours[0].shape[0]
    for flip, group in ((0, ours), (1, theirs)):
        for turn in range(count):
            place = (((row & 1) ^ flip) * count + (me ^ turn)) * part
            store[pl.ds(pl.multiple_of(place, 16), part), :] = group[turn][...]
    place = 0
    for ref in (neck_ref, down_ref):
        deep = ref.shape[1]
        for i in range(ref.shape[0]):
            for h in range(2):
                ref[i, :, 128 * h : 128 * h + 128] = store[place : place + deep]
                place += deep
    for i in range(level_ref.shape[0]):
        level_ref[i] = store[place : place + 128]
        place += 128


def local(level_in, w_level, w_down, w_neck, cotangent):
    rows, cols, _ = level_in.shape
    half_rows, half_cols = rows // 2, cols // 2
    total = w_neck.shape[3]
    count, gy_count = lax.axis_size("gx"), lax.axis_size("gy")
    z_count = gy_count // 2
    pitch = half_cols + 2 * SIDE
    axes = ("gy", "gx")
    spots = [(y, x) for y in range(gy_count) for x in range(count)]

    def permute(value, target):
        pairs = [(y * count + x, target(y, x)) for y, x in spots]
        return lax.ppermute(value, axes, [(a, b) for a, b in pairs if b is not None])

    def by_col(value, turn):
        return permute(value, lambda y, x: y * count + (x ^ turn))

    def by_z(value, turn):
        return permute(value, lambda y, x: (y ^ (2 * turn)) * count + x)

    def by_core(value):
        return permute(value, lambda y, x: (y ^ 1) * count + x)

    def by_seam(value):
        def target(y, x):
            other = y + 1 if y % 2 else y - 1
            return other * count + x if 0 <= other < gy_count else None

        return permute(value, target)

    strip = jnp.swapaxes(cotangent, 1, 2)
    width = strip.shape[1]
    packed = shape((groups_of(half_rows, width) * pitch + rows * SIDE, 128))
    first = call(begin, shape((16, 128)), (), flops=10**10)
    sent = call(
        functools.partial(pack_cols, count, half_cols), [packed] * (count - 1), (level_in, strip, first)
    )
    got = [by_col(value, turn + 1) for turn, value in enumerate(sent)]
    band = shape((HALO * (cols + 2 * SIDE) + 4 * pitch, 128))
    kept, cross, inner = call(
        functools.partial(pack_rows, count, half_cols),
        [shape((3 * rows * pitch, 128)), band, band],
        (level_in, strip, *got),
    )
    cross, inner = by_seam(cross), by_core(inner)

    wl = w_level.reshape(9, 128, 128)
    wd = w_down.reshape(512, total)
    wn = w_neck.reshape(9 * total, total)
    wfwd, wbwd, wdt, wnt = call(
        turn_weights,
        [shape((1536, 256)), shape((1536, 256)), shape((total, 512)), shape(wn.shape)],
        (wl, wd, wn),
    )
    pixels = rows * cols * count * gy_count
    used = 2 * 9 * total + 4 * 2 * 128 + 9 * 128
    part = -(-used // (2 * count * 16)) * 16
    half = part * count
    tiles = groups_of(half_rows, width) * half_cols
    sizes = (
        rows, half_rows, half_cols,
        1.0 / math.sqrt(pixels), 1.0 / math.sqrt(pixels // 4),
    )
    far = rows + 2 * HALO
    sums, send, out, grad_input = call(
        functools.partial(main, sizes),
        [shape((2 * half, 128)), shape((half, 128)), shape((half_rows * half_cols, total)), shape(level_in.shape)],
        (kept, cross, inner, wfwd, wbwd, wd, wdt, wn, wnt),
        [
            pltpu.VMEM((far, 2 * pitch, 128), F32),
            pltpu.VMEM((far, pitch, 256), BF),
            pltpu.VMEM((far, pitch, 256), BF),
            pltpu.VMEM((far - 2, pitch, 256), BF),
            pltpu.VMEM((far - 2, pitch, 256), F32),
            pltpu.VMEM((3, half_rows + 6, pitch, total), BF),
            pltpu.VMEM((3, half_rows + 4, pitch, total), BF),
            pltpu.VMEM((half_rows + 4, pitch, total), BF),
            pltpu.VMEM((half_rows + 2, pitch, total), BF),
            pltpu.VMEM((rows + 4, pitch, 256), F32),
            pltpu.VMEM((rows + 4, pitch, 256), BF),
            pltpu.VMEM((rows + 4, pitch, 256), BF),
            pltpu.VMEM((rows, cols, 128), F32),
        ],
        limit=20,
        flops=6 * 10**9,
    )

    pieces = call(
        functools.partial(pack_neck, count, half_rows, width), shape((count, tiles, 128)), (out,)
    )
    cut = -(-part // 32) * 16
    rest = part - cut
    units = [-(-size // (z_count * 16)) * 16 for size in (cut, rest)]
    own, *sent = call(
        functools.partial(add_cores, count, cut),
        [shape((part, 128), F32)]
        + [shape((cut, 128))] * (count - 1)
        + [shape((rest + tiles, 128))] * (count - 1),
        (sums, by_core(send), pieces),
    )
    early = [by_col(value, turn + 1) for turn, value in enumerate(sent[: count - 1])]
    late = [by_col(value, turn + 1) for turn, value in enumerate(sent[count - 1 :])]
    terms = []
    for low, size, unit, got in ((0, cut, units[0], early), (cut, rest, units[1], late)):
        first, *sent = call(
            functools.partial(add_cols, count, z_count, low, size),
            [shape((unit, 128), F32)] + [shape((unit, 128))] * (z_count - 1),
            (own, *got),
            [pltpu.VMEM((unit * z_count, 128), F32)],
        )
        terms += [first] + [by_z(value, turn) for turn, value in zip(row_turns(z_count), sent)]
    neck_out = call(
        functools.partial(place_neck, count, rest), shape(strip.shape), (pieces, *late)
    )
    own = call(functools.partial(add_rows, z_count), shape((sum(units), 128)), terms)
    own = call(
        functools.partial(join, z_count, cut, units[0]),
        shape((part, 128)),
        [own] + [by_z(own, turn) for turn in range(1, z_count)],
        [pltpu.VMEM((sum(units) * z_count, 128), BF)],
    )
    ours = [own] + [by_col(own, turn) for turn in range(1, count)]
    theirs = [by_core(value) for value in ours]
    grad_level, grad_down, grad_neck = call(
        functools.partial(finish, count),
        [shape((9, 128, 128)), shape((4, 128, total)), shape((9, total, total))],
        (*ours, *theirs),
        [pltpu.VMEM((2 * half, 128), BF)],
    )
    return (
        jnp.swapaxes(neck_out, 1, 2),
        grad_input,
        grad_level.reshape(w_level.shape),
        grad_down.reshape(w_down.shape),
        grad_neck.reshape(w_neck.shape),
    )


def solution(mesh):
    return jax.shard_map(
        local,
        mesh=mesh,
        in_specs=(P("gy", "gx", None), P(), P(), P(), P("gy", None, "gx")),
        out_specs=(P("gy", None, "gx"), P("gy", "gx", None), P(), P(), P()),
        check_vma=False,
    )
```

```python
import functools
import math

import jax
import jax.numpy as jnp
from jax import lax
from jax.experimental import pallas as pl
from jax.experimental.pallas import tpu as pltpu
from jax.sharding import PartitionSpec as P

BF, F32 = jnp.bfloat16, jnp.float32
HALO = 7
SIDE = 8
VMEM = pl.BlockSpec(memory_space=pltpu.VMEM)


def call(body, out_shapes, args, scratch=(), limit=8, flops=10**9):
    return pl.pallas_call(
        body,
        out_shape=out_shapes,
        in_specs=[VMEM] * len(args),
        out_specs=jax.tree.map(lambda _: VMEM, out_shapes),
        scratch_shapes=list(scratch),
        cost_estimate=pl.CostEstimate(flops=flops, bytes_accessed=0, transcendentals=0),
        compiler_params=pltpu.CompilerParams(vmem_limit_bytes=limit * 1024 * 1024),
    )(*args)


def shape(dims, dtype=BF):
    return jax.ShapeDtypeStruct(dims, dtype)


def dot(a, b, dims=((1,), (0,))):
    return lax.dot_general(a, b, (dims, ((), ())), preferred_element_type=F32)


def picking(dims, rule):
    i, j = (lax.broadcasted_iota(jnp.int32, dims, axis) for axis in (0, 1))
    return jnp.where(rule(i, j), 1.0, 0.0).astype(BF)


def groups_of(rows, width):
    return -(-rows * width // 128)


def lanes_to_channels(row, owner, width, total):
    base = row * width % 128
    return picking(
        (128, total),
        lambda lane, channel: (lane >= base)
        & (lane < base + width)
        & (lane - base == channel - owner * width),
    )


def strip_rows(cot_ref):
    half_rows, width, cols = cot_ref.shape
    value = cot_ref[...].reshape(half_rows * width, cols)
    short = 128 * groups_of(half_rows, width) - half_rows * width
    if short:
        value = jnp.concatenate([value, jnp.zeros((short, cols), BF)], axis=0)
    return value


def strip_piece(value, tile, half_cols):
    pitch = half_cols + 2 * SIDE
    pick = picking(
        (pitch, value.shape[1]),
        lambda i, j: j == jnp.where(i < half_cols + SIDE, i, i - pitch) + tile * half_cols,
    )
    parts = [
        dot(pick, value[low : low + 128], ((1,), (1,))) for low in range(0, value.shape[0], 128)
    ]
    return jnp.concatenate(parts, axis=0).astype(BF)


def begin(out_ref):
    out_ref[...] = jnp.zeros(out_ref.shape, BF)


def pack_cols(count, half_cols, level_ref, cot_ref, begin_ref, *outs):
    me = lax.axis_index("gx")
    strip = strip_rows(cot_ref)
    level = level_ref[...].astype(F32)
    first, last = level[:, :SIDE], level[:, level.shape[1] - SIDE :]
    for turn in range(1, count):
        other = me ^ turn
        piece = strip_piece(strip, other, half_cols)
        cut = piece.shape[0]
        outs[turn - 1][0:cut] = piece
        edge = jnp.where(other == me + 1, last, first)
        outs[turn - 1][cut:] = edge.reshape(-1, 128).astype(BF)


def pack_rows(count, half_cols, level_ref, cot_ref, *refs):
    got = refs[: count - 1]
    kept_ref, cross_ref, inner_ref = refs[count - 1 :]
    me, core = lax.axis_index("gx"), lax.axis_index("gy") & 1
    rows, cols = level_ref.shape[0], level_ref.shape[1]
    half_rows, width = cot_ref.shape[0], cot_ref.shape[1]
    total = count * width
    pitch = half_cols + 2 * SIDE
    cut = groups_of(half_rows, width) * pitch
    mine = strip_piece(strip_rows(cot_ref), me, half_cols)
    right = jnp.zeros((rows * SIDE, 128), F32)
    left = jnp.zeros((rows * SIDE, 128), F32)
    for turn in range(1, count):
        edge = got[turn - 1][cut:].astype(F32)
        right = jnp.where(me ^ turn == me + 1, edge, right)
        left = jnp.where(me ^ turn == me - 1, edge, left)
    right, left = right.reshape(rows, SIDE, 128), left.reshape(rows, SIDE, 128)
    level = level_ref[...]
    gap = jnp.zeros((rows, 2 * pitch - cols - 2 * SIDE, 128), F32)
    edges = jnp.concatenate([right, gap, left], axis=1).astype(BF)
    wide = jnp.concatenate([level, edges], axis=1).reshape(2 * rows * pitch, 128)
    kept_ref[0 : 2 * rows * pitch] = wide
    cot = []
    picks = {}
    for row in range(half_rows):
        low = row * width // 128 * pitch
        value = jnp.zeros((pitch, total), F32)
        for turn in range(count):
            part = mine[low : low + pitch] if turn == 0 else got[turn - 1][low : low + pitch]
            key = (row * width % 128, turn)
            if key not in picks:
                picks[key] = lanes_to_channels(row, me ^ turn, width, total)
            value = value + dot(part, picks[key])
        value = value.astype(BF)
        cot.append(value)
        low = 2 * (rows + row) * pitch
        kept_ref[low : low + pitch] = value[:, :128]
        kept_ref[low + pitch : low + 2 * pitch] = value[:, 128:]
    edges = jnp.concatenate([right, left], axis=1).astype(BF)
    band = jnp.concatenate([level, edges], axis=1)
    cells = HALO * (cols + 2 * SIDE)
    for low, neck, is_cross in ((0, 0, core == 0), (rows - HALO, half_rows - 2, core == 1)):
        for ref, here in ((cross_ref, is_cross), (inner_ref, jnp.logical_not(is_cross))):

            @pl.when(here)
            def _(ref=ref, low=low, neck=neck):
                ref[0:cells] = band[low : low + HALO].reshape(cells, 128)
                for i in range(2):
                    spot = cells + 2 * pitch * i
                    ref[spot : spot + pitch] = cot[neck + i][:, :128]
                    ref[spot + pitch : spot + 2 * pitch] = cot[neck + i][:, 128:]


def turn_weights(wl_ref, wd_ref, wn_ref, wfwd_ref, wbwd_ref, wdt_ref, wnt_ref):
    zero = jnp.zeros((128, 128), BF)
    for ky in range(3):
        w = [wl_ref[3 * ky + kx] for kx in range(3)]
        t = [value.T for value in w]
        for ref, blocks in (
            (wfwd_ref, (w[1], w[0], w[2], w[1], w[0], zero, zero, w[2])),
            (wbwd_ref, (t[1], t[2], t[0], t[1], t[2], zero, zero, t[0])),
        ):
            for spot, block in enumerate(blocks):
                low = 512 * ky + 128 * (spot // 2)
                ref[low : low + 128, 128 * (spot % 2) : 128 * (spot % 2) + 128] = block
    for p in range(2):
        wdt_ref[:, 256 * p : 256 * p + 256] = wd_ref[256 * p : 256 * p + 256].T
    for k in range(9):
        total = wn_ref.shape[1]
        wnt_ref[total * k : total * k + total] = wn_ref[total * k : total * k + total].T


def sigmoid_slope(value):
    gate = jax.nn.sigmoid(value)
    return gate, gate + value * gate * (1.0 - gate)


def shifted(value):
    size = value.shape[1]
    return pltpu.roll(value, 1, 1), pltpu.roll(value, size - 1, 1)


def paired(value):
    return jnp.concatenate(
        [pltpu.roll(value[:, :, 128:], 1, 1), pltpu.roll(value[:, :, :128], value.shape[1] - 1, 1)],
        axis=2,
    ).astype(BF)


def dot_rows(a, b, step):
    return jnp.concatenate([dot(a[i : i + step], b) for i in range(0, a.shape[0], step)], axis=0)


def flat(value):
    return value.reshape(-1, value.shape[-1])


def main(
    sizes,
    kept_ref, cross_ref, inner_ref, wfwd, wbwd, wd_ref, wdt_ref, wn_ref, wnt_ref,
    sums_ref, send_ref, out_ref, grad_ref,
    field, pair, side, act, slope, neck, gate, cot_all, ngrad, lback, lgate, lside, spread,
):
    rows, half_rows, half_cols, _, _ = sizes
    cols = 2 * half_cols
    pitch = half_cols + 2 * SIDE
    total = wd_ref.shape[1]
    me, row = lax.axis_index("gx"), lax.axis_index("gy")
    row_end, col_end = lax.axis_size("gy") * half_rows, lax.axis_size("gx") * half_cols
    core = row & 1

    cells = HALO * (cols + 2 * SIDE)

    def take(ref, low, low_neck):
        band = ref[0:cells].reshape(HALO, cols + 2 * SIDE, 128).astype(F32)
        field[low : low + HALO, 0 : cols + SIDE] = band[:, : cols + SIDE]
        field[low : low + HALO, cols + SIDE : 2 * pitch - SIDE] = jnp.zeros(
            (HALO, 2 * pitch - cols - 2 * SIDE, 128), F32
        )
        field[low : low + HALO, 2 * pitch - SIDE : 2 * pitch] = band[:, cols + SIDE :]
        for i in range(2):
            spot = cells + 2 * pitch * i
            cot_all[low_neck + i, :, :128] = ref[spot : spot + pitch]
            cot_all[low_neck + i, :, 128:] = ref[spot + pitch : spot + 2 * pitch]

    @pl.when(core == 0)
    def _():
        take(cross_ref, 0, 0)
        take(inner_ref, HALO + rows, 2 + half_rows)

    @pl.when(core == 1)
    def _():
        take(inner_ref, 0, 0)
        take(cross_ref, HALO + rows, 2 + half_rows)

    own = kept_ref[0 : 2 * rows * pitch].reshape(rows, 2 * pitch, 128)
    field[HALO : HALO + rows, : 2 * pitch] = own.astype(F32)
    for row_in in range(half_rows):
        low = 2 * (rows + row_in) * pitch
        cot_all[2 + row_in, :, :128] = kept_ref[low : low + pitch]
        cot_all[2 + row_in, :, 128:] = kept_ref[low + pitch : low + 2 * pitch]
    even = field[:, pl.ds(0, pitch, stride=2), :]
    odd = field[:, pl.ds(1, pitch, stride=2), :]
    both = jnp.concatenate([even, odd], axis=2)
    pair[...] = both.astype(BF)
    side[...] = paired(both)

    act_rows = act.shape[0]
    step = act_rows // 2
    for low in range(0, act_rows, step):
        taken = [
            flat(ref[low + ky : low + ky + step]) for ky in range(3) for ref in (pair, side)
        ]
        pre = dot_rows(jnp.concatenate(taken, axis=1), wfwd[...], step * pitch // 3)
        sig, slp = sigmoid_slope(pre)
        own = flat(pair[low + 1 : low + 1 + step]).astype(F32)
        act[low : low + step] = (own + pre * sig).astype(BF).reshape(step, pitch, 256)
        slope[low : low + step] = slp.reshape(step, pitch, 256)

    def inside(value, first_row):
        r = lax.broadcasted_iota(jnp.int32, value.shape, 0) + (row * half_rows + first_row)
        c = lax.broadcasted_iota(jnp.int32, value.shape, 1)
        c = jnp.where(c < half_cols + SIDE, c, c - pitch) + me * half_cols
        ok = (r >= 0) & (r < row_end) & (c >= 0) & (c < col_end)
        return jnp.where(ok, value, 0.0)

    neck_rows = act_rows // 2
    grid = act[...].reshape(neck_rows, 2, pitch, 256)
    both = jnp.concatenate([flat(grid[:, 0]), flat(grid[:, 1])], axis=1)
    value = dot_rows(both, wd_ref[...], 5 * pitch).reshape(neck_rows, pitch, total)
    value = inside(value, -3).astype(BF)
    before, behind = shifted(value.astype(F32))
    neck[0], neck[1], neck[2] = before.astype(BF), value, behind.astype(BF)

    gate_rows = neck_rows - 2
    taken = [flat(neck[kx, ky : ky + gate_rows]) for ky in range(3) for kx in range(3)]
    pre = dot_rows(jnp.concatenate(taken, axis=1), wn_ref[...], 4 * pitch)
    sig, slp = sigmoid_slope(pre)
    own = flat(neck[1, 1 : 1 + gate_rows]).astype(F32)
    out = (own + pre * sig).astype(BF).reshape(gate_rows, pitch, total)
    out = out[2 : 2 + half_rows, :half_cols].reshape(half_rows * half_cols, total)
    out_ref[...] = out
    value = (flat(cot_all[...]).astype(F32) * slp).astype(BF).reshape(gate_rows, pitch, total)
    before, behind = shifted(value.astype(F32))
    gate[0], gate[1], gate[2] = before.astype(BF), value, behind.astype(BF)

    grad_rows = gate_rows - 2
    taken = [
        flat(gate[2 - kx, 2 - ky : 2 - ky + grad_rows]) for ky in range(3) for kx in range(3)
    ]
    back = dot_rows(jnp.concatenate(taken, axis=1), wnt_ref[...], 3 * pitch)
    value = flat(cot_all[1 : 1 + grad_rows]).astype(F32) + back
    value = inside(value.reshape(grad_rows, pitch, total), -1)
    ngrad[...] = value.astype(BF)

    value = dot_rows(flat(ngrad[...]), wdt_ref[...], 3 * pitch).reshape(grad_rows, pitch, 512)
    for p in range(2):
        for i in range(grad_rows):
            lback[2 * i + p] = value[i, :, 256 * p : 256 * p + 256]
    value = lback[...] * slope[4 : 4 + 2 * grad_rows]
    value = value.astype(BF)
    lgate[...] = value
    lside[...] = paired(value.astype(F32))

    taken = [
        flat(ref[3 - ky : 3 - ky + rows, :half_cols]) for ky in range(3) for ref in (lgate, lside)
    ]
    value = dot_rows(jnp.concatenate(taken, axis=1), wbwd[...], 4 * half_cols).reshape(rows, half_cols, 256)
    value = value + lback[2 : 2 + rows, :half_cols]
    spread[:, pl.ds(0, half_cols, stride=2), :] = value[:, :, :128]
    spread[:, pl.ds(1, half_cols, stride=2), :] = value[:, :, 128:]
    grad_ref[...] = spread[:, :cols].astype(BF)

    weight_sums(sizes, sums_ref, neck, gate, act, ngrad, pair, side, lgate)
    half = send_ref.shape[0]
    send_ref[...] = sums_ref[pl.ds(pl.multiple_of((1 - core) * half, 16), half), :]


def weight_sums(sizes, sums_ref, neck, gate, act, ngrad, pair, side, lgate):
    rows, half_rows, half_cols, level_scale, neck_scale = sizes
    pitch = act.shape[1]
    place = 0

    def put(value):
        nonlocal place
        sums_ref[place : place + value.shape[0]] = value
        place += value.shape[0]

    own = flat(gate[1, 2 : 2 + half_rows, :half_cols])
    for ky in range(3):
        for kx in range(3):
            lhs = flat(neck[kx, 2 + ky : 2 + ky + half_rows, :half_cols])
            value = (dot(lhs, own, ((0,), (0,))) * neck_scale).astype(BF)
            put(value[:, :128])
            put(value[:, 128:])
    own = flat(ngrad[1 : 1 + half_rows, :half_cols])
    grid = act[6 : 6 + rows].reshape(half_rows, 2, pitch, 256)
    for p in range(2):
        lhs = flat(grid[:, p, :half_cols])
        value = (dot(lhs, own, ((0,), (0,))) * neck_scale).astype(BF)
        for q in range(2):
            for h in range(2):
                put(value[128 * q : 128 * q + 128, 128 * h : 128 * h + 128])
    own = flat(lgate[2 : 2 + rows, :half_cols])
    for ky in range(3):
        m = dot(flat(pair[6 + ky : 6 + ky + rows, :half_cols]), own, ((0,), (0,)))
        s = dot(flat(side[6 + ky : 6 + ky + rows, :half_cols]), own, ((0,), (0,)))
        for value in (
            m[:128, 128:] + s[:128, :128],
            m[:128, :128] + m[128:, 128:],
            m[128:, :128] + s[128:, 128:],
        ):
            put((value * level_scale).astype(BF))
    if place < sums_ref.shape[0]:
        put(jnp.zeros((sums_ref.shape[0] - place, 128), BF))


def pack_neck(count, half_rows, width, out_ref, pieces_ref):
    me = lax.axis_index("gx")
    cells, total = out_ref.shape
    half_cols, per = cells // half_rows, 128 // width
    for turn in range(count):
        for low in range(0, half_rows, per):
            piece = jnp.zeros((half_cols, 128), F32)
            for r in range(low, min(half_rows, low + per)):
                pick = lanes_to_channels(r, me ^ turn, width, total)
                piece = piece + dot(out_ref[half_cols * r : half_cols * r + half_cols], pick, ((1,), (1,)))
            group = low // per
            pieces_ref[turn, half_cols * group : half_cols * group + half_cols] = piece.astype(BF)


def add_cores(count, cut, sums_ref, got_ref, pieces_ref, own_ref, *outs):
    me, core = lax.axis_index("gx"), lax.axis_index("gy") & 1
    part = own_ref.shape[0]
    early, late = outs[: count - 1], outs[count - 1 :]
    for turn in range(count):
        mine = pl.ds(pl.multiple_of((core * count + (me ^ turn)) * part, 16), part)
        theirs = pl.ds(pl.multiple_of((me ^ turn) * part, 16), part)
        value = sums_ref[mine, :].astype(F32) + got_ref[theirs, :].astype(F32)
        if turn == 0:
            own_ref[...] = value
        else:
            early[turn - 1][...] = value[:cut].astype(BF)
            late[turn - 1][0 : part - cut] = value[cut:].astype(BF)
            late[turn - 1][part - cut :] = pieces_ref[turn]


def row_turns(z_count):
    return [*range(2, z_count), 1] if z_count > 1 else []


def add_cols(count, z_count, low, size, own_ref, *refs):
    got = refs[: count - 1]
    first_ref, outs, total = refs[count - 1], refs[count:-1], refs[-1]
    z = lax.axis_index("gy") // 2
    unit = first_ref.shape[0]
    value = own_ref[low : low + size]
    for ref in got:
        value = value + ref[0:size].astype(F32)
    total[0:size] = value
    if size < total.shape[0]:
        total[size:] = jnp.zeros((total.shape[0] - size, 128), F32)
    for turn in range(z_count):
        value = total[pl.ds(pl.multiple_of((z ^ turn) * unit, 16), unit), :]
        if turn == 0:
            first_ref[...] = value
        else:
            outs[row_turns(z_count).index(turn)][...] = value.astype(BF)


def place_neck(count, part, pieces_ref, *refs):
    got, neck_ref = refs[:-1], refs[-1]
    me = lax.axis_index("gx")
    half_rows, width, cols = neck_ref.shape
    half_cols = cols // count
    for group in range(groups_of(half_rows, width)):
        value = jnp.zeros((128, cols), F32)
        here = slice(half_cols * group, half_cols * group + half_cols)
        for turn in range(count):
            piece = pieces_ref[0, here] if turn == 0 else got[turn - 1][part:][here]
            pick = picking((half_cols, cols), lambda i, j, t=turn: j == i + (me ^ t) * half_cols)
            value = value + dot(piece, pick, ((0,), (0,)))
        per = min(half_rows, 128 // width)
        value = value[: per * width].astype(BF).reshape(per, width, cols)
        neck_ref[group * per : group * per + per] = value


def add_rows(z_count, *refs):
    low = 0
    for group in (refs[:z_count], refs[z_count:-1]):
        value = group[0][...]
        for ref in group[1:]:
            value = value + ref[...].astype(F32)
        refs[-1][low : low + value.shape[0]] = value.astype(BF)
        low += value.shape[0]


def join(z_count, cut, unit, *refs):
    pieces, (out_ref, store) = refs[:z_count], refs[z_count:]
    z = lax.axis_index("gy") // 2
    rest = pieces[0].shape[0] - unit
    for turn in range(z_count):
        here = z ^ turn
        store[pl.ds(pl.multiple_of(here * unit, 16), unit), :] = pieces[turn][0:unit]
        here = unit * z_count + here * rest
        store[pl.ds(pl.multiple_of(here, 16), rest), :] = pieces[turn][unit:]
    out_ref[0:cut] = store[0:cut]
    out_ref[cut:] = store[unit * z_count : unit * z_count + out_ref.shape[0] - cut]


def finish(count, *refs):
    ours, theirs = refs[:count], refs[count : 2 * count]
    level_ref, down_ref, neck_ref, store = refs[2 * count :]
    me, row = lax.axis_index("gx"), lax.axis_index("gy")
    part = ours[0].shape[0]
    for flip, group in ((0, ours), (1, theirs)):
        for turn in range(count):
            place = (((row & 1) ^ flip) * count + (me ^ turn)) * part
            store[pl.ds(pl.multiple_of(place, 16), part), :] = group[turn][...]
    place = 0
    for ref in (neck_ref, down_ref):
        deep = ref.shape[1]
        for i in range(ref.shape[0]):
            for h in range(2):
                ref[i, :, 128 * h : 128 * h + 128] = store[place : place + deep]
                place += deep
    for i in range(level_ref.shape[0]):
        level_ref[i] = store[place : place + 128]
        place += 128


def local(level_in, w_level, w_down, w_neck, cotangent):
    rows, cols, _ = level_in.shape
    half_rows, half_cols = rows // 2, cols // 2
    total = w_neck.shape[3]
    count, gy_count = lax.axis_size("gx"), lax.axis_size("gy")
    z_count = gy_count // 2
    pitch = half_cols + 2 * SIDE
    axes = ("gy", "gx")
    spots = [(y, x) for y in range(gy_count) for x in range(count)]

    def permute(value, target):
        pairs = [(y * count + x, target(y, x)) for y, x in spots]
        return lax.ppermute(value, axes, [(a, b) for a, b in pairs if b is not None])

    def by_col(value, turn):
        return permute(value, lambda y, x: y * count + (x ^ turn))

    def by_z(value, turn):
        return permute(value, lambda y, x: (y ^ (2 * turn)) * count + x)

    def by_core(value):
        return permute(value, lambda y, x: (y ^ 1) * count + x)

    def by_seam(value):
        def target(y, x):
            other = y + 1 if y % 2 else y - 1
            return other * count + x if 0 <= other < gy_count else None

        return permute(value, target)

    strip = jnp.swapaxes(cotangent, 1, 2)
    width = strip.shape[1]
    packed = shape((groups_of(half_rows, width) * pitch + rows * SIDE, 128))
    first = call(begin, shape((16, 128)), (), flops=10**10)
    sent = call(
        functools.partial(pack_cols, count, half_cols), [packed] * (count - 1), (level_in, strip, first)
    )
    got = [by_col(value, turn + 1) for turn, value in enumerate(sent)]
    band = shape((HALO * (cols + 2 * SIDE) + 4 * pitch, 128))
    kept, cross, inner = call(
        functools.partial(pack_rows, count, half_cols),
        [shape((3 * rows * pitch, 128)), band, band],
        (level_in, strip, *got),
    )
    cross, inner = by_seam(cross), by_core(inner)

    wl = w_level.reshape(9, 128, 128)
    wd = w_down.reshape(512, total)
    wn = w_neck.reshape(9 * total, total)
    wfwd, wbwd, wdt, wnt = call(
        turn_weights,
        [shape((1536, 256)), shape((1536, 256)), shape((total, 512)), shape(wn.shape)],
        (wl, wd, wn),
    )
    pixels = rows * cols * count * gy_count
    used = 2 * 9 * total + 4 * 2 * 128 + 9 * 128
    part = -(-used // (2 * count * 16)) * 16
    half = part * count
    tiles = groups_of(half_rows, width) * half_cols
    sizes = (
        rows, half_rows, half_cols,
        1.0 / math.sqrt(pixels), 1.0 / math.sqrt(pixels // 4),
    )
    far = rows + 2 * HALO
    sums, send, out, grad_input = call(
        functools.partial(main, sizes),
        [shape((2 * half, 128)), shape((half, 128)), shape((half_rows * half_cols, total)), shape(level_in.shape)],
        (kept, cross, inner, wfwd, wbwd, wd, wdt, wn, wnt),
        [
            pltpu.VMEM((far, 2 * pitch + 8, 128), F32),
            pltpu.VMEM((far, pitch, 256), BF),
            pltpu.VMEM((far, pitch, 256), BF),
            pltpu.VMEM((far - 2, pitch, 256), BF),
            pltpu.VMEM((far - 2, pitch, 256), F32),
            pltpu.VMEM((3, half_rows + 6, pitch, total), BF),
            pltpu.VMEM((3, half_rows + 4, pitch, total), BF),
            pltpu.VMEM((half_rows + 4, pitch, total), BF),
            pltpu.VMEM((half_rows + 2, pitch, total), BF),
            pltpu.VMEM((rows + 4, pitch, 256), F32),
            pltpu.VMEM((rows + 4, pitch, 256), BF),
            pltpu.VMEM((rows + 4, pitch, 256), BF),
            pltpu.VMEM((rows, cols + 8, 128), F32),
        ],
        limit=20,
        flops=6 * 10**9,
    )

    pieces = call(
        functools.partial(pack_neck, count, half_rows, width), shape((count, tiles, 128)), (out,)
    )
    cut = -(-part // 32) * 16
    rest = part - cut
    units = [-(-size // (z_count * 16)) * 16 for size in (cut, rest)]
    own, *sent = call(
        functools.partial(add_cores, count, cut),
        [shape((part, 128), F32)]
        + [shape((cut, 128))] * (count - 1)
        + [shape((rest + tiles, 128))] * (count - 1),
        (sums, by_core(send), pieces),
    )
    early = [by_col(value, turn + 1) for turn, value in enumerate(sent[: count - 1])]
    late = [by_col(value, turn + 1) for turn, value in enumerate(sent[count - 1 :])]
    terms = []
    for low, size, unit, got in ((0, cut, units[0], early), (cut, rest, units[1], late)):
        first, *sent = call(
            functools.partial(add_cols, count, z_count, low, size),
            [shape((unit, 128), F32)] + [shape((unit, 128))] * (z_count - 1),
            (own, *got),
            [pltpu.VMEM((unit * z_count, 128), F32)],
        )
        terms += [first] + [by_z(value, turn) for turn, value in zip(row_turns(z_count), sent)]
    neck_out = call(
        functools.partial(place_neck, count, rest), shape(strip.shape), (pieces, *late)
    )
    own = call(functools.partial(add_rows, z_count), shape((sum(units), 128)), terms)
    own = call(
        functools.partial(join, z_count, cut, units[0]),
        shape((part, 128)),
        [own] + [by_z(own, turn) for turn in range(1, z_count)],
        [pltpu.VMEM((sum(units) * z_count, 128), BF)],
    )
    ours = [own] + [by_col(own, turn) for turn in range(1, count)]
    theirs = [by_core(value) for value in ours]
    grad_level, grad_down, grad_neck = call(
        functools.partial(finish, count),
        [shape((9, 128, 128)), shape((4, 128, total)), shape((9, total, total))],
        (*ours, *theirs),
        [pltpu.VMEM((2 * half, 128), BF)],
    )
    return (
        jnp.swapaxes(neck_out, 1, 2),
        grad_input,
        grad_level.reshape(w_level.shape),
        grad_down.reshape(w_down.shape),
        grad_neck.reshape(w_neck.shape),
    )


def solution(mesh):
    return jax.shard_map(
        local,
        mesh=mesh,
        in_specs=(P("gy", "gx", None), P(), P(), P(), P("gy", None, "gx")),
        out_specs=(P("gy", None, "gx"), P("gy", "gx", None), P(), P(), P()),
        check_vma=False,
    )
```

```python
import functools
import math

import jax
import jax.numpy as jnp
from jax import lax
from jax.experimental import pallas as pl
from jax.experimental.pallas import tpu as pltpu
from jax.sharding import PartitionSpec as P

BF, F32 = jnp.bfloat16, jnp.float32
HALO = 7
SIDE = 8
VMEM = pl.BlockSpec(memory_space=pltpu.VMEM)


def call(body, out_shapes, args, scratch=(), limit=8, flops=10**9):
    return pl.pallas_call(
        body,
        out_shape=out_shapes,
        in_specs=[VMEM] * len(args),
        out_specs=jax.tree.map(lambda _: VMEM, out_shapes),
        scratch_shapes=list(scratch),
        cost_estimate=pl.CostEstimate(flops=flops, bytes_accessed=0, transcendentals=0),
        compiler_params=pltpu.CompilerParams(vmem_limit_bytes=limit * 1024 * 1024),
    )(*args)


def shape(dims, dtype=BF):
    return jax.ShapeDtypeStruct(dims, dtype)


def dot(a, b, dims=((1,), (0,))):
    return lax.dot_general(a, b, (dims, ((), ())), preferred_element_type=F32)


def picking(dims, rule):
    i, j = (lax.broadcasted_iota(jnp.int32, dims, axis) for axis in (0, 1))
    return jnp.where(rule(i, j), 1.0, 0.0).astype(BF)


def groups_of(rows, width):
    return -(-rows * width // 128)


def lanes_to_channels(row, owner, width, total):
    base = row * width % 128
    return picking(
        (128, total),
        lambda lane, channel: (lane >= base)
        & (lane < base + width)
        & (lane - base == channel - owner * width),
    )


def strip_rows(cot_ref):
    half_rows, width, cols = cot_ref.shape
    value = cot_ref[...].reshape(half_rows * width, cols)
    short = 128 * groups_of(half_rows, width) - half_rows * width
    if short:
        value = jnp.concatenate([value, jnp.zeros((short, cols), BF)], axis=0)
    return value


def span_of(half_cols):
    return half_cols + SIDE


def cut_of(half_rows, width, half_cols):
    return -(-groups_of(half_rows, width) * span_of(half_cols) // 16) * 16


def strip_piece(value, tile, half_cols, cut):
    span = span_of(half_cols)
    pick = picking(
        (span, value.shape[1]),
        lambda i, j: j == jnp.where(i < half_cols + SIDE // 2, i, i - span) + tile * half_cols,
    )
    parts = [
        dot(pick, value[low : low + 128], ((1,), (1,))) for low in range(0, value.shape[0], 128)
    ]
    short = cut - span * len(parts)
    if short:
        parts.append(jnp.zeros((short, 128), F32))
    return jnp.concatenate(parts, axis=0).astype(BF)


def spread_out(value):
    return jnp.concatenate([value, value[value.shape[0] - SIDE :]], axis=0)


def has_edge(turn):
    return turn & (turn + 1) == 0


def begin(out_ref):
    out_ref[...] = jnp.zeros(out_ref.shape, BF)


def pack_cols(count, half_cols, level_ref, cot_ref, begin_ref, *outs):
    me = lax.axis_index("gx")
    strip = strip_rows(cot_ref)
    level = level_ref[...].astype(F32)
    first, last = level[:, :SIDE], level[:, level.shape[1] - SIDE :]
    for turn in range(1, count):
        other = me ^ turn
        cut = cut_of(cot_ref.shape[0], cot_ref.shape[1], half_cols)
        outs[turn - 1][0:cut] = strip_piece(strip, other, half_cols, cut)
        if has_edge(turn):
            edge = jnp.where(other == me + 1, last, first)
            outs[turn - 1][cut:] = edge.reshape(-1, 128).astype(BF)


def pack_rows(count, half_cols, level_ref, cot_ref, *refs):
    got = refs[: count - 1]
    kept_ref, cross_ref, inner_ref, held = refs[count - 1 :]
    me, core = lax.axis_index("gx"), lax.axis_index("gy") & 1
    rows, cols = level_ref.shape[0], level_ref.shape[1]
    half_rows, width = cot_ref.shape[0], cot_ref.shape[1]
    total = count * width
    pitch = half_cols + 2 * SIDE
    span, cut = span_of(half_cols), cut_of(half_rows, width, half_cols)
    mine = strip_piece(strip_rows(cot_ref), me, half_cols, cut)
    right = jnp.zeros((rows * SIDE, 128), F32)
    left = jnp.zeros((rows * SIDE, 128), F32)
    for turn in filter(has_edge, range(1, count)):
        edge = got[turn - 1][cut:].astype(F32)
        right = jnp.where(me ^ turn == me + 1, edge, right)
        left = jnp.where(me ^ turn == me - 1, edge, left)
    right, left = right.reshape(rows, SIDE, 128), left.reshape(rows, SIDE, 128)
    level = level_ref[...]
    gap = jnp.zeros((rows, 2 * pitch - cols - 2 * SIDE, 128), F32)
    edges = jnp.concatenate([right, gap, left], axis=1).astype(BF)
    wide = jnp.concatenate([level, edges], axis=1).reshape(2 * rows * pitch, 128)
    kept_ref[0 : 2 * rows * pitch] = wide
    cot, picks = [], {}
    halves = 2 * width == 128 and count % 2 == 0
    if halves:
        for turn in range(count):
            held[me ^ turn] = (mine if turn == 0 else got[turn - 1][0:cut]).astype(F32)
        left_half = lax.broadcasted_iota(jnp.int32, (span, 128), 1) < width
    for row in range(half_rows):
        low = row * width // 128 * span
        if halves:
            tiles = []
            for owner in range(0, count, 2):
                a, b = (held[owner + i, low : low + span] for i in range(2))
                if row % 2:
                    a = pltpu.roll(a, width, 1)
                else:
                    b = pltpu.roll(b, width, 1)
                tiles.append(jnp.where(left_half, a, b))
            value = jnp.concatenate(tiles, axis=1)
        else:
            value = jnp.zeros((span, total), F32)
            for turn in range(count):
                part = mine[low : low + span] if turn == 0 else got[turn - 1][low : low + span]
                key = (row * width % 128, turn)
                if key not in picks:
                    picks[key] = lanes_to_channels(row, me ^ turn, width, total)
                value = value + dot(part, picks[key])
        cot.append(value)
        value = spread_out(value)
        value = value.astype(BF)
        low = 2 * (rows + row) * pitch
        kept_ref[low : low + pitch] = value[:, :128]
        kept_ref[low + pitch : low + 2 * pitch] = value[:, 128:]
    edges = jnp.concatenate([right, left], axis=1).astype(BF)
    band = jnp.concatenate([level, edges], axis=1)
    cells = HALO * (cols + 2 * SIDE)
    for low, neck, is_cross in ((0, 0, core == 0), (rows - HALO, half_rows - 2, core == 1)):
        for ref, here in ((cross_ref, is_cross), (inner_ref, jnp.logical_not(is_cross))):

            @pl.when(here)
            def _(ref=ref, low=low, neck=neck):
                ref[0:cells] = band[low : low + HALO].reshape(cells, 128)
                for i in range(2):
                    spot = cells + 2 * span * i
                    both = jnp.concatenate([cot[neck + i][:, :128], cot[neck + i][:, 128:]], axis=0)
                    ref[spot : spot + 2 * span] = both.astype(BF)


def turn_weights(wl_ref, wd_ref, wn_ref, wfwd_ref, wbwd_ref, wdt_ref, wnt_ref):
    zero = jnp.zeros((128, 128), BF)
    for ky in range(3):
        w = [wl_ref[3 * ky + kx] for kx in range(3)]
        t = [value.T for value in w]
        for ref, blocks in (
            (wfwd_ref, (w[1], w[0], w[2], w[1], w[0], zero, zero, w[2])),
            (wbwd_ref, (t[1], t[2], t[0], t[1], t[2], zero, zero, t[0])),
        ):
            for spot, block in enumerate(blocks):
                low = 512 * ky + 128 * (spot // 2)
                ref[low : low + 128, 128 * (spot % 2) : 128 * (spot % 2) + 128] = block
    for p in range(2):
        wdt_ref[:, 256 * p : 256 * p + 256] = wd_ref[256 * p : 256 * p + 256].T
    for k in range(9):
        total = wn_ref.shape[1]
        wnt_ref[total * k : total * k + total] = wn_ref[total * k : total * k + total].T


def sigmoid_slope(value):
    gate = jax.nn.sigmoid(value)
    return gate, gate + value * gate * (1.0 - gate)


def shifted(value):
    size = value.shape[1]
    return pltpu.roll(value, 1, 1), pltpu.roll(value, size - 1, 1)


def paired(value):
    return jnp.concatenate(
        [pltpu.roll(value[:, :, 128:], 1, 1), pltpu.roll(value[:, :, :128], value.shape[1] - 1, 1)],
        axis=2,
    ).astype(BF)


def dot_rows(a, b, step):
    return jnp.concatenate([dot(a[i : i + step], b) for i in range(0, a.shape[0], step)], axis=0)


def flat(value):
    return value.reshape(-1, value.shape[-1])


def main(
    sizes,
    kept_ref, cross_ref, inner_ref, wfwd, wbwd, wd_ref, wdt_ref, wn_ref, wnt_ref,
    sums_ref, send_ref, out_ref, grad_ref,
    field, pair, side, act, slope, neck, gate, cot_all, ngrad, lback, lgate, lside, spread,
):
    rows, half_rows, half_cols, _, _ = sizes
    cols = 2 * half_cols
    pitch = half_cols + 2 * SIDE
    total = wd_ref.shape[1]
    me, row = lax.axis_index("gx"), lax.axis_index("gy")
    row_end, col_end = lax.axis_size("gy") * half_rows, lax.axis_size("gx") * half_cols
    core = row & 1

    cells = HALO * (cols + 2 * SIDE)

    def take(ref, low, low_neck):
        band = ref[0:cells].reshape(HALO, cols + 2 * SIDE, 128).astype(F32)
        field[low : low + HALO, 0 : cols + SIDE] = band[:, : cols + SIDE]
        field[low : low + HALO, cols + SIDE : 2 * pitch - SIDE] = jnp.zeros(
            (HALO, 2 * pitch - cols - 2 * SIDE, 128), F32
        )
        field[low : low + HALO, 2 * pitch - SIDE : 2 * pitch] = band[:, cols + SIDE :]
        for i in range(2):
            span = span_of(half_cols)
            spot = cells + 2 * span * i
            both = ref[spot : spot + 2 * span].astype(F32)
            both = jnp.concatenate([spread_out(both[:span]), spread_out(both[span:])], axis=1)
            cot_all[low_neck + i] = both.astype(BF)

    @pl.when(core == 0)
    def _():
        take(cross_ref, 0, 0)
        take(inner_ref, HALO + rows, 2 + half_rows)

    @pl.when(core == 1)
    def _():
        take(inner_ref, 0, 0)
        take(cross_ref, HALO + rows, 2 + half_rows)

    own = kept_ref[0 : 2 * rows * pitch].reshape(rows, 2 * pitch, 128)
    field[HALO : HALO + rows, : 2 * pitch] = own.astype(F32)
    for row_in in range(half_rows):
        low = 2 * (rows + row_in) * pitch
        cot_all[2 + row_in, :, :128] = kept_ref[low : low + pitch]
        cot_all[2 + row_in, :, 128:] = kept_ref[low + pitch : low + 2 * pitch]
    even = field[:, pl.ds(0, pitch, stride=2), :]
    odd = field[:, pl.ds(1, pitch, stride=2), :]
    both = jnp.concatenate([even, odd], axis=2)
    pair[...] = both.astype(BF)
    side[...] = paired(both)

    act_rows = act.shape[0]
    step = act_rows // 2
    for low in range(0, act_rows, step):
        taken = [
            flat(ref[low + ky : low + ky + step]) for ky in range(3) for ref in (pair, side)
        ]
        pre = dot_rows(jnp.concatenate(taken, axis=1), wfwd[...], step * pitch // 3)
        sig, slp = sigmoid_slope(pre)
        own = flat(pair[low + 1 : low + 1 + step]).astype(F32)
        act[low : low + step] = (own + pre * sig).astype(BF).reshape(step, pitch, 256)
        slope[low : low + step] = slp.reshape(step, pitch, 256)

    def inside(value, first_row):
        r = lax.broadcasted_iota(jnp.int32, value.shape, 0) + (row * half_rows + first_row)
        c = lax.broadcasted_iota(jnp.int32, value.shape, 1)
        c = jnp.where(c < half_cols + SIDE, c, c - pitch) + me * half_cols
        ok = (r >= 0) & (r < row_end) & (c >= 0) & (c < col_end)
        return jnp.where(ok, value, 0.0)

    neck_rows = act_rows // 2
    grid = act[...].reshape(neck_rows, 2, pitch, 256)
    both = jnp.concatenate([flat(grid[:, 0]), flat(grid[:, 1])], axis=1)
    value = dot_rows(both, wd_ref[...], 5 * pitch).reshape(neck_rows, pitch, total)
    value = inside(value, -3).astype(BF)
    before, behind = shifted(value.astype(F32))
    neck[0], neck[1], neck[2] = before.astype(BF), value, behind.astype(BF)

    gate_rows = neck_rows - 2
    taken = [flat(neck[kx, ky : ky + gate_rows]) for ky in range(3) for kx in range(3)]
    pre = dot_rows(jnp.concatenate(taken, axis=1), wn_ref[...], 4 * pitch)
    sig, slp = sigmoid_slope(pre)
    own = flat(neck[1, 1 : 1 + gate_rows]).astype(F32)
    out = (own + pre * sig).astype(BF).reshape(gate_rows, pitch, total)
    out = out[2 : 2 + half_rows, :half_cols].reshape(half_rows * half_cols, total)
    out_ref[...] = out
    value = (flat(cot_all[...]).astype(F32) * slp).astype(BF).reshape(gate_rows, pitch, total)
    before, behind = shifted(value.astype(F32))
    gate[0], gate[1], gate[2] = before.astype(BF), value, behind.astype(BF)

    grad_rows = gate_rows - 2
    taken = [
        flat(gate[2 - kx, 2 - ky : 2 - ky + grad_rows]) for ky in range(3) for kx in range(3)
    ]
    back = dot_rows(jnp.concatenate(taken, axis=1), wnt_ref[...], 3 * pitch)
    value = flat(cot_all[1 : 1 + grad_rows]).astype(F32) + back
    value = inside(value.reshape(grad_rows, pitch, total), -1)
    ngrad[...] = value.astype(BF)

    value = dot_rows(flat(ngrad[...]), wdt_ref[...], 3 * pitch).reshape(grad_rows, pitch, 512)
    for p in range(2):
        for i in range(grad_rows):
            lback[2 * i + p] = value[i, :, 256 * p : 256 * p + 256]
    value = lback[...] * slope[4 : 4 + 2 * grad_rows]
    value = value.astype(BF)
    lgate[...] = value
    lside[...] = paired(value.astype(F32))

    taken = [
        flat(ref[3 - ky : 3 - ky + rows, :half_cols]) for ky in range(3) for ref in (lgate, lside)
    ]
    value = dot_rows(jnp.concatenate(taken, axis=1), wbwd[...], 4 * half_cols).reshape(rows, half_cols, 256)
    value = value + lback[2 : 2 + rows, :half_cols]
    spread[:, pl.ds(0, half_cols, stride=2), :] = value[:, :, :128]
    spread[:, pl.ds(1, half_cols, stride=2), :] = value[:, :, 128:]
    grad_ref[...] = spread[:, :cols].astype(BF)

    weight_sums(sizes, sums_ref, neck, gate, act, ngrad, pair, side, lgate)
    half = send_ref.shape[0]
    send_ref[...] = sums_ref[pl.ds(pl.multiple_of((1 - core) * half, 16), half), :]


def weight_sums(sizes, sums_ref, neck, gate, act, ngrad, pair, side, lgate):
    rows, half_rows, half_cols, level_scale, neck_scale = sizes
    pitch = act.shape[1]
    place = 0

    def put(value):
        nonlocal place
        sums_ref[place : place + value.shape[0]] = value
        place += value.shape[0]

    own = flat(gate[1, 2 : 2 + half_rows, :half_cols])
    for ky in range(3):
        for kx in range(3):
            lhs = flat(neck[kx, 2 + ky : 2 + ky + half_rows, :half_cols])
            value = (dot(lhs, own, ((0,), (0,))) * neck_scale).astype(BF)
            put(value[:, :128])
            put(value[:, 128:])
    own = flat(ngrad[1 : 1 + half_rows, :half_cols])
    grid = act[6 : 6 + rows].reshape(half_rows, 2, pitch, 256)
    for p in range(2):
        lhs = flat(grid[:, p, :half_cols])
        value = (dot(lhs, own, ((0,), (0,))) * neck_scale).astype(BF)
        for q in range(2):
            for h in range(2):
                put(value[128 * q : 128 * q + 128, 128 * h : 128 * h + 128])
    own = flat(lgate[2 : 2 + rows, :half_cols])
    for ky in range(3):
        m = dot(flat(pair[6 + ky : 6 + ky + rows, :half_cols]), own, ((0,), (0,)))
        s = dot(flat(side[6 + ky : 6 + ky + rows, :half_cols]), own, ((0,), (0,)))
        for value in (
            m[:128, 128:] + s[:128, :128],
            m[:128, :128] + m[128:, 128:],
            m[128:, :128] + s[128:, 128:],
        ):
            put((value * level_scale).astype(BF))
    if place < sums_ref.shape[0]:
        put(jnp.zeros((sums_ref.shape[0] - place, 128), BF))


def pack_neck(count, half_rows, width, out_ref, pieces_ref):
    me = lax.axis_index("gx")
    cells, total = out_ref.shape
    half_cols, per = cells // half_rows, 128 // width
    for turn in range(count):
        for low in range(0, half_rows, per):
            piece = jnp.zeros((half_cols, 128), F32)
            for r in range(low, min(half_rows, low + per)):
                pick = lanes_to_channels(r, me ^ turn, width, total)
                piece = piece + dot(out_ref[half_cols * r : half_cols * r + half_cols], pick, ((1,), (1,)))
            group = low // per
            pieces_ref[turn, half_cols * group : half_cols * group + half_cols] = piece.astype(BF)


def add_cores(count, cut, sums_ref, got_ref, pieces_ref, own_ref, *outs):
    me, core = lax.axis_index("gx"), lax.axis_index("gy") & 1
    part = own_ref.shape[0]
    early, late = outs[: count - 1], outs[count - 1 :]
    for turn in range(count):
        mine = pl.ds(pl.multiple_of((core * count + (me ^ turn)) * part, 16), part)
        theirs = pl.ds(pl.multiple_of((me ^ turn) * part, 16), part)
        value = sums_ref[mine, :].astype(F32) + got_ref[theirs, :].astype(F32)
        if turn == 0:
            own_ref[...] = value
        else:
            early[turn - 1][...] = value[:cut].astype(BF)
            late[turn - 1][0 : part - cut] = value[cut:].astype(BF)
            late[turn - 1][part - cut :] = pieces_ref[turn]


def row_turns(z_count):
    return [*range(2, z_count), 1] if z_count > 1 else []


def add_cols(count, z_count, low, size, own_ref, *refs):
    got = refs[: count - 1]
    first_ref, outs, total = refs[count - 1], refs[count:-1], refs[-1]
    z = lax.axis_index("gy") // 2
    unit = first_ref.shape[0]
    value = own_ref[low : low + size]
    for ref in got:
        value = value + ref[0:size].astype(F32)
    total[0:size] = value
    if size < total.shape[0]:
        total[size:] = jnp.zeros((total.shape[0] - size, 128), F32)
    for turn in range(z_count):
        value = total[pl.ds(pl.multiple_of((z ^ turn) * unit, 16), unit), :]
        if turn == 0:
            first_ref[...] = value
        else:
            outs[row_turns(z_count).index(turn)][...] = value.astype(BF)


def place_neck(count, part, pieces_ref, *refs):
    got, neck_ref = refs[:-1], refs[-1]
    me = lax.axis_index("gx")
    half_rows, width, cols = neck_ref.shape
    half_cols = cols // count
    for group in range(groups_of(half_rows, width)):
        value = jnp.zeros((128, cols), F32)
        here = slice(half_cols * group, half_cols * group + half_cols)
        for turn in range(count):
            piece = pieces_ref[0, here] if turn == 0 else got[turn - 1][part:][here]
            pick = picking((half_cols, cols), lambda i, j, t=turn: j == i + (me ^ t) * half_cols)
            value = value + dot(piece, pick, ((0,), (0,)))
        per = min(half_rows, 128 // width)
        value = value[: per * width].astype(BF).reshape(per, width, cols)
        neck_ref[group * per : group * per + per] = value


def add_rows(z_count, *refs):
    low = 0
    for group in (refs[:z_count], refs[z_count:-1]):
        value = group[0][...]
        for ref in group[1:]:
            value = value + ref[...].astype(F32)
        refs[-1][low : low + value.shape[0]] = value.astype(BF)
        low += value.shape[0]


def join(z_count, cut, unit, *refs):
    pieces, (out_ref, store) = refs[:z_count], refs[z_count:]
    z = lax.axis_index("gy") // 2
    rest = pieces[0].shape[0] - unit
    for turn in range(z_count):
        here = z ^ turn
        store[pl.ds(pl.multiple_of(here * unit, 16), unit), :] = pieces[turn][0:unit]
        here = unit * z_count + here * rest
        store[pl.ds(pl.multiple_of(here, 16), rest), :] = pieces[turn][unit:]
    out_ref[0:cut] = store[0:cut]
    out_ref[cut:] = store[unit * z_count : unit * z_count + out_ref.shape[0] - cut]


def finish(count, *refs):
    ours, theirs = refs[:count], refs[count : 2 * count]
    level_ref, down_ref, neck_ref, store = refs[2 * count :]
    me, row = lax.axis_index("gx"), lax.axis_index("gy")
    part = ours[0].shape[0]
    for flip, group in ((0, ours), (1, theirs)):
        for turn in range(count):
            place = (((row & 1) ^ flip) * count + (me ^ turn)) * part
            store[pl.ds(pl.multiple_of(place, 16), part), :] = group[turn][...]
    place = 0
    for ref in (neck_ref, down_ref):
        deep = ref.shape[1]
        for i in range(ref.shape[0]):
            for h in range(2):
                ref[i, :, 128 * h : 128 * h + 128] = store[place : place + deep]
                place += deep
    for i in range(level_ref.shape[0]):
        level_ref[i] = store[place : place + 128]
        place += 128


def local(level_in, w_level, w_down, w_neck, cotangent):
    rows, cols, _ = level_in.shape
    half_rows, half_cols = rows // 2, cols // 2
    total = w_neck.shape[3]
    count, gy_count = lax.axis_size("gx"), lax.axis_size("gy")
    z_count = gy_count // 2
    pitch = half_cols + 2 * SIDE
    axes = ("gy", "gx")
    spots = [(y, x) for y in range(gy_count) for x in range(count)]

    def permute(value, target):
        pairs = [(y * count + x, target(y, x)) for y, x in spots]
        return lax.ppermute(value, axes, [(a, b) for a, b in pairs if b is not None])

    def by_col(value, turn):
        return permute(value, lambda y, x: y * count + (x ^ turn))

    def by_z(value, turn):
        return permute(value, lambda y, x: (y ^ (2 * turn)) * count + x)

    def by_core(value):
        return permute(value, lambda y, x: (y ^ 1) * count + x)

    def by_seam(value):
        def target(y, x):
            other = y + 1 if y % 2 else y - 1
            return other * count + x if 0 <= other < gy_count else None

        return permute(value, target)

    strip = jnp.swapaxes(cotangent, 1, 2)
    width = strip.shape[1]
    cut = cut_of(half_rows, width, half_cols)
    packed = [shape((cut + rows * SIDE * has_edge(turn), 128)) for turn in range(1, count)]
    first = call(begin, shape((16, 128)), (), flops=10**10)
    sent = call(
        functools.partial(pack_cols, count, half_cols), packed, (level_in, strip, first)
    )
    got = [by_col(value, turn + 1) for turn, value in enumerate(sent)]
    band = shape((HALO * (cols + 2 * SIDE) + 4 * span_of(half_cols), 128))
    kept, cross, inner = call(
        functools.partial(pack_rows, count, half_cols),
        [shape((3 * rows * pitch, 128)), band, band],
        (level_in, strip, *got),
        [pltpu.VMEM((count, cut, 128), F32)],
    )
    cross, inner = by_seam(cross), by_core(inner)

    wl = w_level.reshape(9, 128, 128)
    wd = w_down.reshape(512, total)
    wn = w_neck.reshape(9 * total, total)
    wfwd, wbwd, wdt, wnt = call(
        turn_weights,
        [shape((1536, 256)), shape((1536, 256)), shape((total, 512)), shape(wn.shape)],
        (wl, wd, wn),
    )
    pixels = rows * cols * count * gy_count
    used = 2 * 9 * total + 4 * 2 * 128 + 9 * 128
    part = -(-used // (2 * count * 16)) * 16
    half = part * count
    tiles = groups_of(half_rows, width) * half_cols
    sizes = (
        rows, half_rows, half_cols,
        1.0 / math.sqrt(pixels), 1.0 / math.sqrt(pixels // 4),
    )
    far = rows + 2 * HALO
    sums, send, out, grad_input = call(
        functools.partial(main, sizes),
        [shape((2 * half, 128)), shape((half, 128)), shape((half_rows * half_cols, total)), shape(level_in.shape)],
        (kept, cross, inner, wfwd, wbwd, wd, wdt, wn, wnt),
        [
            pltpu.VMEM((far, 2 * pitch + 8, 128), F32),
            pltpu.VMEM((far, pitch, 256), BF),
            pltpu.VMEM((far, pitch, 256), BF),
            pltpu.VMEM((far - 2, pitch, 256), BF),
            pltpu.VMEM((far - 2, pitch, 256), F32),
            pltpu.VMEM((3, half_rows + 6, pitch, total), BF),
            pltpu.VMEM((3, half_rows + 4, pitch, total), BF),
            pltpu.VMEM((half_rows + 4, pitch, total), BF),
            pltpu.VMEM((half_rows + 2, pitch, total), BF),
            pltpu.VMEM((rows + 4, pitch, 256), F32),
            pltpu.VMEM((rows + 4, pitch, 256), BF),
            pltpu.VMEM((rows + 4, pitch, 256), BF),
            pltpu.VMEM((rows, cols + 8, 128), F32),
        ],
        limit=20,
        flops=6 * 10**9,
    )

    pieces = call(
        functools.partial(pack_neck, count, half_rows, width), shape((count, tiles, 128)), (out,)
    )
    cut = -(-part // 32) * 16
    rest = part - cut
    units = [-(-size // (z_count * 16)) * 16 for size in (cut, rest)]
    own, *sent = call(
        functools.partial(add_cores, count, cut),
        [shape((part, 128), F32)]
        + [shape((cut, 128))] * (count - 1)
        + [shape((rest + tiles, 128))] * (count - 1),
        (sums, by_core(send), pieces),
    )
    early = [by_col(value, turn + 1) for turn, value in enumerate(sent[: count - 1])]
    late = [by_col(value, turn + 1) for turn, value in enumerate(sent[count - 1 :])]
    terms = []
    for low, size, unit, got in ((0, cut, units[0], early), (cut, rest, units[1], late)):
        first, *sent = call(
            functools.partial(add_cols, count, z_count, low, size),
            [shape((unit, 128), F32)] + [shape((unit, 128))] * (z_count - 1),
            (own, *got),
            [pltpu.VMEM((unit * z_count, 128), F32)],
        )
        terms += [first] + [by_z(value, turn) for turn, value in zip(row_turns(z_count), sent)]
    neck_out = call(
        functools.partial(place_neck, count, rest), shape(strip.shape), (pieces, *late)
    )
    own = call(functools.partial(add_rows, z_count), shape((sum(units), 128)), terms)
    own = call(
        functools.partial(join, z_count, cut, units[0]),
        shape((part, 128)),
        [own] + [by_z(own, turn) for turn in range(1, z_count)],
        [pltpu.VMEM((sum(units) * z_count, 128), BF)],
    )
    ours = [own] + [by_col(own, turn) for turn in range(1, count)]
    theirs = [by_core(value) for value in ours]
    grad_level, grad_down, grad_neck = call(
        functools.partial(finish, count),
        [shape((9, 128, 128)), shape((4, 128, total)), shape((9, total, total))],
        (*ours, *theirs),
        [pltpu.VMEM((2 * half, 128), BF)],
    )
    return (
        jnp.swapaxes(neck_out, 1, 2),
        grad_input,
        grad_level.reshape(w_level.shape),
        grad_down.reshape(w_down.shape),
        grad_neck.reshape(w_neck.shape),
    )


def solution(mesh):
    return jax.shard_map(
        local,
        mesh=mesh,
        in_specs=(P("gy", "gx", None), P(), P(), P(), P("gy", None, "gx")),
        out_specs=(P("gy", None, "gx"), P("gy", "gx", None), P(), P(), P()),
        check_vma=False,
    )
```

```python
import functools
import math

import jax
import jax.numpy as jnp
from jax import lax
from jax.experimental import pallas as pl
from jax.experimental.pallas import tpu as pltpu
from jax.sharding import PartitionSpec as P

BF, F32 = jnp.bfloat16, jnp.float32
HALO = 7
SIDE = 8
VMEM = pl.BlockSpec(memory_space=pltpu.VMEM)


def call(body, out_shapes, args, scratch=(), limit=8, flops=10**9):
    return pl.pallas_call(
        body,
        out_shape=out_shapes,
        in_specs=[VMEM] * len(args),
        out_specs=jax.tree.map(lambda _: VMEM, out_shapes),
        scratch_shapes=list(scratch),
        cost_estimate=pl.CostEstimate(flops=flops, bytes_accessed=0, transcendentals=0),
        compiler_params=pltpu.CompilerParams(vmem_limit_bytes=limit * 1024 * 1024),
    )(*args)


def shape(dims, dtype=BF):
    return jax.ShapeDtypeStruct(dims, dtype)


def dot(a, b, dims=((1,), (0,))):
    return lax.dot_general(a, b, (dims, ((), ())), preferred_element_type=F32)


def picking(dims, rule):
    i, j = (lax.broadcasted_iota(jnp.int32, dims, axis) for axis in (0, 1))
    return jnp.where(rule(i, j), 1.0, 0.0).astype(BF)


def groups_of(rows, width):
    return -(-rows * width // 128)


def lanes_to_channels(row, owner, width, total):
    base = row * width % 128
    return picking(
        (128, total),
        lambda lane, channel: (lane >= base)
        & (lane < base + width)
        & (lane - base == channel - owner * width),
    )


def strip_rows(cot_ref):
    half_rows, width, cols = cot_ref.shape
    value = cot_ref[...].reshape(half_rows * width, cols)
    short = 128 * groups_of(half_rows, width) - half_rows * width
    if short:
        value = jnp.concatenate([value, jnp.zeros((short, cols), BF)], axis=0)
    return value


def span_of(half_cols):
    return half_cols + SIDE


def cut_of(half_rows, width, half_cols):
    return -(-groups_of(half_rows, width) * span_of(half_cols) // 16) * 16


def strip_piece(value, tile, half_cols, cut):
    span = span_of(half_cols)
    pick = picking(
        (span, value.shape[1]),
        lambda i, j: j == jnp.where(i < half_cols + SIDE // 2, i, i - span) + tile * half_cols,
    )
    parts = [
        dot(pick, value[low : low + 128], ((1,), (1,))) for low in range(0, value.shape[0], 128)
    ]
    short = cut - span * len(parts)
    if short:
        parts.append(jnp.zeros((short, 128), F32))
    return jnp.concatenate(parts, axis=0).astype(BF)


def spread_out(value):
    return jnp.concatenate([value, value[value.shape[0] - SIDE :]], axis=0)


def has_edge(turn):
    return turn & (turn + 1) == 0


def begin(out_ref):
    out_ref[...] = jnp.zeros(out_ref.shape, BF)


def pack_cols(count, half_cols, level_ref, cot_ref, begin_ref, *outs):
    me = lax.axis_index("gx")
    strip = strip_rows(cot_ref)
    level = level_ref[...].astype(F32)
    first, last = level[:, :SIDE], level[:, level.shape[1] - SIDE :]
    for turn in range(1, count):
        other = me ^ turn
        cut = cut_of(cot_ref.shape[0], cot_ref.shape[1], half_cols)
        outs[turn - 1][0:cut] = strip_piece(strip, other, half_cols, cut)
        if has_edge(turn):
            edge = jnp.where(other == me + 1, last, first)
            outs[turn - 1][cut:] = edge.reshape(-1, 128).astype(BF)


def pack_rows(count, half_cols, level_ref, cot_ref, *refs):
    got = refs[: count - 1]
    kept_ref, cross_ref, inner_ref, held = refs[count - 1 :]
    me, core = lax.axis_index("gx"), lax.axis_index("gy") & 1
    rows, cols = level_ref.shape[0], level_ref.shape[1]
    half_rows, width = cot_ref.shape[0], cot_ref.shape[1]
    total = count * width
    pitch = half_cols + 2 * SIDE
    span, cut = span_of(half_cols), cut_of(half_rows, width, half_cols)
    mine = strip_piece(strip_rows(cot_ref), me, half_cols, cut)
    right = jnp.zeros((rows * SIDE, 128), F32)
    left = jnp.zeros((rows * SIDE, 128), F32)
    for turn in filter(has_edge, range(1, count)):
        edge = got[turn - 1][cut:].astype(F32)
        right = jnp.where(me ^ turn == me + 1, edge, right)
        left = jnp.where(me ^ turn == me - 1, edge, left)
    right, left = right.reshape(rows, SIDE, 128), left.reshape(rows, SIDE, 128)
    level = level_ref[...]
    gap = jnp.zeros((rows, 2 * pitch - cols - 2 * SIDE, 128), F32)
    edges = jnp.concatenate([right, gap, left], axis=1).astype(BF)
    wide = jnp.concatenate([level, edges], axis=1).reshape(2 * rows * pitch, 128)
    kept_ref[0 : 2 * rows * pitch] = wide
    cot, picks = [], {}
    halves = 2 * width == 128 and count % 2 == 0
    if halves:
        for turn in range(count):
            held[me ^ turn] = (mine if turn == 0 else got[turn - 1][0:cut]).astype(F32)
        left_half = lax.broadcasted_iota(jnp.int32, (span, 128), 1) < width
    for row in range(half_rows):
        low = row * width // 128 * span
        if halves:
            tiles = []
            for owner in range(0, count, 2):
                a, b = (held[owner + i, low : low + span] for i in range(2))
                if row % 2:
                    a = pltpu.roll(a, width, 1)
                else:
                    b = pltpu.roll(b, width, 1)
                tiles.append(jnp.where(left_half, a, b))
            value = jnp.concatenate(tiles, axis=1)
        else:
            value = jnp.zeros((span, total), F32)
            for turn in range(count):
                part = mine[low : low + span] if turn == 0 else got[turn - 1][low : low + span]
                key = (row * width % 128, turn)
                if key not in picks:
                    picks[key] = lanes_to_channels(row, me ^ turn, width, total)
                value = value + dot(part, picks[key])
        cot.append(value)
        value = spread_out(value)
        value = value.astype(BF)
        low = 2 * (rows + row) * pitch
        kept_ref[low : low + pitch] = value[:, :128]
        kept_ref[low + pitch : low + 2 * pitch] = value[:, 128:]
    edges = jnp.concatenate([right, left], axis=1).astype(BF)
    band = jnp.concatenate([level, edges], axis=1)
    cells = HALO * (cols + 2 * SIDE)
    for low, neck, is_cross in ((0, 0, core == 0), (rows - HALO, half_rows - 2, core == 1)):
        for ref, here in ((cross_ref, is_cross), (inner_ref, jnp.logical_not(is_cross))):

            @pl.when(here)
            def _(ref=ref, low=low, neck=neck):
                ref[0:cells] = band[low : low + HALO].reshape(cells, 128)
                for i in range(2):
                    spot = cells + 2 * span * i
                    both = jnp.concatenate([cot[neck + i][:, :128], cot[neck + i][:, 128:]], axis=0)
                    ref[spot : spot + 2 * span] = both.astype(BF)


def turn_weights(wl_ref, wd_ref, wn_ref, wfwd_ref, wbwd_ref, wdt_ref, wnt_ref):
    zero = jnp.zeros((128, 128), BF)
    for ky in range(3):
        w = [wl_ref[3 * ky + kx] for kx in range(3)]
        t = [value.T for value in w]
        for ref, blocks in (
            (wfwd_ref, (w[1], w[0], w[2], w[1], w[0], zero, zero, w[2])),
            (wbwd_ref, (t[1], t[2], t[0], t[1], t[2], zero, zero, t[0])),
        ):
            for spot, block in enumerate(blocks):
                low = 512 * ky + 128 * (spot // 2)
                ref[low : low + 128, 128 * (spot % 2) : 128 * (spot % 2) + 128] = block
    for p in range(2):
        wdt_ref[:, 256 * p : 256 * p + 256] = wd_ref[256 * p : 256 * p + 256].T
    for k in range(9):
        total = wn_ref.shape[1]
        wnt_ref[total * k : total * k + total] = wn_ref[total * k : total * k + total].T


def slope_at(value, gate):
    return gate + value * gate * (1.0 - gate)


def shifted(value):
    size = value.shape[1]
    return pltpu.roll(value, 1, 1), pltpu.roll(value, size - 1, 1)


def paired(value):
    return jnp.concatenate(
        [pltpu.roll(value[:, :, 128:], 1, 1), pltpu.roll(value[:, :, :128], value.shape[1] - 1, 1)],
        axis=2,
    ).astype(BF)


def dot_rows(a, b, step):
    return jnp.concatenate([dot(a[i : i + step], b) for i in range(0, a.shape[0], step)], axis=0)


def flat(value):
    return value.reshape(-1, value.shape[-1])


def main(
    sizes,
    kept_ref, cross_ref, inner_ref, wfwd, wbwd, wd_ref, wdt_ref, wn_ref, wnt_ref,
    sums_ref, send_ref, out_ref, grad_ref,
    field, pair, side, act, slope, neck, gate, cot_all, ngrad, lback, lgate, lside, spread,
):
    rows, half_rows, half_cols, _, _ = sizes
    cols = 2 * half_cols
    pitch = half_cols + 2 * SIDE
    total = wd_ref.shape[1]
    me, row = lax.axis_index("gx"), lax.axis_index("gy")
    row_end, col_end = lax.axis_size("gy") * half_rows, lax.axis_size("gx") * half_cols
    core = row & 1

    cells = HALO * (cols + 2 * SIDE)

    def take(ref, low, low_neck):
        band = ref[0:cells].reshape(HALO, cols + 2 * SIDE, 128).astype(F32)
        field[low : low + HALO, 0 : cols + SIDE] = band[:, : cols + SIDE]
        field[low : low + HALO, cols + SIDE : 2 * pitch - SIDE] = jnp.zeros(
            (HALO, 2 * pitch - cols - 2 * SIDE, 128), F32
        )
        field[low : low + HALO, 2 * pitch - SIDE : 2 * pitch] = band[:, cols + SIDE :]
        for i in range(2):
            span = span_of(half_cols)
            spot = cells + 2 * span * i
            both = ref[spot : spot + 2 * span].astype(F32)
            both = jnp.concatenate([spread_out(both[:span]), spread_out(both[span:])], axis=1)
            cot_all[low_neck + i] = both.astype(BF)

    @pl.when(core == 0)
    def _():
        take(cross_ref, 0, 0)
        take(inner_ref, HALO + rows, 2 + half_rows)

    @pl.when(core == 1)
    def _():
        take(inner_ref, 0, 0)
        take(cross_ref, HALO + rows, 2 + half_rows)

    own = kept_ref[0 : 2 * rows * pitch].reshape(rows, 2 * pitch, 128)
    field[HALO : HALO + rows, : 2 * pitch] = own.astype(F32)
    for row_in in range(half_rows):
        low = 2 * (rows + row_in) * pitch
        cot_all[2 + row_in, :, :128] = kept_ref[low : low + pitch]
        cot_all[2 + row_in, :, 128:] = kept_ref[low + pitch : low + 2 * pitch]
    even = field[:, pl.ds(0, pitch, stride=2), :]
    odd = field[:, pl.ds(1, pitch, stride=2), :]
    both = jnp.concatenate([even, odd], axis=2)
    pair[...] = both.astype(BF)
    side[...] = paired(both)

    act_rows = act.shape[0]
    step = act_rows // 2
    for low in range(0, act_rows, step):
        taken = [
            flat(ref[low + ky : low + ky + step]) for ky in range(3) for ref in (pair, side)
        ]
        pre = dot_rows(jnp.concatenate(taken, axis=1), wfwd[...], step * pitch // 3)
        sig = jax.nn.sigmoid(pre)
        own = flat(pair[low + 1 : low + 1 + step]).astype(F32)
        act[low : low + step] = (own + pre * sig).astype(BF).reshape(step, pitch, 256)
        first, last = max(low, 4), min(low + step, act_rows - 4)
        here = slice((first - low) * pitch, (last - low) * pitch)
        slope[first:last] = slope_at(pre[here], sig[here]).reshape(last - first, pitch, 256)

    def inside(value, first_row):
        r = lax.broadcasted_iota(jnp.int32, value.shape, 0) + (row * half_rows + first_row)
        c = lax.broadcasted_iota(jnp.int32, value.shape, 1)
        c = jnp.where(c < half_cols + SIDE, c, c - pitch) + me * half_cols
        ok = (r >= 0) & (r < row_end) & (c >= 0) & (c < col_end)
        return jnp.where(ok, value, 0.0)

    neck_rows = act_rows // 2
    grid = act[...].reshape(neck_rows, 2, pitch, 256)
    both = jnp.concatenate([flat(grid[:, 0]), flat(grid[:, 1])], axis=1)
    value = dot_rows(both, wd_ref[...], 5 * pitch).reshape(neck_rows, pitch, total)
    value = inside(value, -3).astype(BF)
    before, behind = shifted(value.astype(F32))
    neck[0], neck[1], neck[2] = before.astype(BF), value, behind.astype(BF)

    gate_rows = neck_rows - 2
    taken = [flat(neck[kx, ky : ky + gate_rows]) for ky in range(3) for kx in range(3)]
    pre = dot_rows(jnp.concatenate(taken, axis=1), wn_ref[...], 4 * pitch)
    sig = jax.nn.sigmoid(pre)
    slp = slope_at(pre, sig)
    own = flat(neck[1, 3 : 3 + half_rows]).astype(F32)
    here = slice(2 * pitch, (2 + half_rows) * pitch)
    out = (own + pre[here] * sig[here]).astype(BF).reshape(half_rows, pitch, total)
    out = out[:, :half_cols].reshape(half_rows * half_cols, total)
    out_ref[...] = out
    value = (flat(cot_all[...]).astype(F32) * slp).astype(BF).reshape(gate_rows, pitch, total)
    before, behind = shifted(value.astype(F32))
    gate[0], gate[1], gate[2] = before.astype(BF), value, behind.astype(BF)

    grad_rows = gate_rows - 2
    taken = [
        flat(gate[2 - kx, 2 - ky : 2 - ky + grad_rows]) for ky in range(3) for kx in range(3)
    ]
    back = dot_rows(jnp.concatenate(taken, axis=1), wnt_ref[...], 3 * pitch)
    value = flat(cot_all[1 : 1 + grad_rows]).astype(F32) + back
    value = inside(value.reshape(grad_rows, pitch, total), -1)
    ngrad[...] = value.astype(BF)

    value = dot_rows(flat(ngrad[...]), wdt_ref[...], 3 * pitch).reshape(grad_rows, pitch, 512)
    for p in range(2):
        for i in range(grad_rows):
            lback[2 * i + p] = value[i, :, 256 * p : 256 * p + 256]
    value = lback[...] * slope[4 : 4 + 2 * grad_rows]
    value = value.astype(BF)
    lgate[...] = value
    lside[...] = paired(value.astype(F32))

    taken = [
        flat(ref[3 - ky : 3 - ky + rows, :half_cols]) for ky in range(3) for ref in (lgate, lside)
    ]
    value = dot_rows(jnp.concatenate(taken, axis=1), wbwd[...], 4 * half_cols).reshape(rows, half_cols, 256)
    value = value + lback[2 : 2 + rows, :half_cols]
    spread[:, pl.ds(0, half_cols, stride=2), :] = value[:, :, :128]
    spread[:, pl.ds(1, half_cols, stride=2), :] = value[:, :, 128:]
    grad_ref[...] = spread[:, :cols].astype(BF)

    weight_sums(sizes, sums_ref, neck, gate, act, ngrad, pair, side, lgate)
    half = send_ref.shape[0]
    send_ref[...] = sums_ref[pl.ds(pl.multiple_of((1 - core) * half, 16), half), :]


def weight_sums(sizes, sums_ref, neck, gate, act, ngrad, pair, side, lgate):
    rows, half_rows, half_cols, level_scale, neck_scale = sizes
    pitch = act.shape[1]
    place = 0

    def put(value):
        nonlocal place
        sums_ref[place : place + value.shape[0]] = value
        place += value.shape[0]

    own = flat(gate[1, 2 : 2 + half_rows, :half_cols])
    for ky in range(3):
        for kx in range(3):
            lhs = flat(neck[kx, 2 + ky : 2 + ky + half_rows, :half_cols])
            value = (dot(lhs, own, ((0,), (0,))) * neck_scale).astype(BF)
            put(value[:, :128])
            put(value[:, 128:])
    own = flat(ngrad[1 : 1 + half_rows, :half_cols])
    grid = act[6 : 6 + rows].reshape(half_rows, 2, pitch, 256)
    for p in range(2):
        lhs = flat(grid[:, p, :half_cols])
        value = (dot(lhs, own, ((0,), (0,))) * neck_scale).astype(BF)
        for q in range(2):
            for h in range(2):
                put(value[128 * q : 128 * q + 128, 128 * h : 128 * h + 128])
    own = flat(lgate[2 : 2 + rows, :half_cols])
    for ky in range(3):
        m = dot(flat(pair[6 + ky : 6 + ky + rows, :half_cols]), own, ((0,), (0,)))
        s = dot(flat(side[6 + ky : 6 + ky + rows, :half_cols]), own, ((0,), (0,)))
        for value in (
            m[:128, 128:] + s[:128, :128],
            m[:128, :128] + m[128:, 128:],
            m[128:, :128] + s[128:, 128:],
        ):
            put((value * level_scale).astype(BF))
    if place < sums_ref.shape[0]:
        put(jnp.zeros((sums_ref.shape[0] - place, 128), BF))


def pack_neck(count, half_rows, width, out_ref, pieces_ref):
    me = lax.axis_index("gx")
    cells, total = out_ref.shape
    half_cols, per = cells // half_rows, 128 // width
    for turn in range(count):
        for low in range(0, half_rows, per):
            piece = jnp.zeros((half_cols, 128), F32)
            for r in range(low, min(half_rows, low + per)):
                pick = lanes_to_channels(r, me ^ turn, width, total)
                piece = piece + dot(out_ref[half_cols * r : half_cols * r + half_cols], pick, ((1,), (1,)))
            group = low // per
            pieces_ref[turn, half_cols * group : half_cols * group + half_cols] = piece.astype(BF)


def add_cores(count, cut, sums_ref, got_ref, pieces_ref, own_ref, *outs):
    me, core = lax.axis_index("gx"), lax.axis_index("gy") & 1
    part = own_ref.shape[0]
    early, late = outs[: count - 1], outs[count - 1 :]
    for turn in range(count):
        mine = pl.ds(pl.multiple_of((core * count + (me ^ turn)) * part, 16), part)
        theirs = pl.ds(pl.multiple_of((me ^ turn) * part, 16), part)
        value = sums_ref[mine, :].astype(F32) + got_ref[theirs, :].astype(F32)
        if turn == 0:
            own_ref[...] = value
        else:
            early[turn - 1][...] = value[:cut].astype(BF)
            late[turn - 1][0 : part - cut] = value[cut:].astype(BF)
            late[turn - 1][part - cut :] = pieces_ref[turn]


def row_turns(z_count):
    return [*range(2, z_count), 1] if z_count > 1 else []


def add_cols(count, z_count, low, size, own_ref, *refs):
    got = refs[: count - 1]
    first_ref, outs, total = refs[count - 1], refs[count:-1], refs[-1]
    z = lax.axis_index("gy") // 2
    unit = first_ref.shape[0]
    value = own_ref[low : low + size]
    for ref in got:
        value = value + ref[0:size].astype(F32)
    total[0:size] = value
    if size < total.shape[0]:
        total[size:] = jnp.zeros((total.shape[0] - size, 128), F32)
    for turn in range(z_count):
        value = total[pl.ds(pl.multiple_of((z ^ turn) * unit, 16), unit), :]
        if turn == 0:
            first_ref[...] = value
        else:
            outs[row_turns(z_count).index(turn)][...] = value.astype(BF)


def place_neck(count, part, pieces_ref, *refs):
    got, neck_ref = refs[:-1], refs[-1]
    me = lax.axis_index("gx")
    half_rows, width, cols = neck_ref.shape
    half_cols = cols // count
    for group in range(groups_of(half_rows, width)):
        value = jnp.zeros((128, cols), F32)
        here = slice(half_cols * group, half_cols * group + half_cols)
        for turn in range(count):
            piece = pieces_ref[0, here] if turn == 0 else got[turn - 1][part:][here]
            pick = picking((half_cols, cols), lambda i, j, t=turn: j == i + (me ^ t) * half_cols)
            value = value + dot(piece, pick, ((0,), (0,)))
        per = min(half_rows, 128 // width)
        value = value[: per * width].astype(BF).reshape(per, width, cols)
        neck_ref[group * per : group * per + per] = value


def add_rows(z_count, *refs):
    low = 0
    for group in (refs[:z_count], refs[z_count:-1]):
        value = group[0][...]
        for ref in group[1:]:
            value = value + ref[...].astype(F32)
        refs[-1][low : low + value.shape[0]] = value.astype(BF)
        low += value.shape[0]


def join(z_count, cut, unit, *refs):
    pieces, (out_ref, store) = refs[:z_count], refs[z_count:]
    z = lax.axis_index("gy") // 2
    rest = pieces[0].shape[0] - unit
    for turn in range(z_count):
        here = z ^ turn
        store[pl.ds(pl.multiple_of(here * unit, 16), unit), :] = pieces[turn][0:unit]
        here = unit * z_count + here * rest
        store[pl.ds(pl.multiple_of(here, 16), rest), :] = pieces[turn][unit:]
    out_ref[0:cut] = store[0:cut]
    out_ref[cut:] = store[unit * z_count : unit * z_count + out_ref.shape[0] - cut]


def finish(count, *refs):
    ours, theirs = refs[:count], refs[count : 2 * count]
    level_ref, down_ref, neck_ref, store = refs[2 * count :]
    me, row = lax.axis_index("gx"), lax.axis_index("gy")
    part = ours[0].shape[0]
    for flip, group in ((0, ours), (1, theirs)):
        for turn in range(count):
            place = (((row & 1) ^ flip) * count + (me ^ turn)) * part
            store[pl.ds(pl.multiple_of(place, 16), part), :] = group[turn][...]
    place = 0
    for ref in (neck_ref, down_ref):
        deep = ref.shape[1]
        for i in range(ref.shape[0]):
            for h in range(2):
                ref[i, :, 128 * h : 128 * h + 128] = store[place : place + deep]
                place += deep
    for i in range(level_ref.shape[0]):
        level_ref[i] = store[place : place + 128]
        place += 128


def local(level_in, w_level, w_down, w_neck, cotangent):
    rows, cols, _ = level_in.shape
    half_rows, half_cols = rows // 2, cols // 2
    total = w_neck.shape[3]
    count, gy_count = lax.axis_size("gx"), lax.axis_size("gy")
    z_count = gy_count // 2
    pitch = half_cols + 2 * SIDE
    axes = ("gy", "gx")
    spots = [(y, x) for y in range(gy_count) for x in range(count)]

    def permute(value, target):
        pairs = [(y * count + x, target(y, x)) for y, x in spots]
        return lax.ppermute(value, axes, [(a, b) for a, b in pairs if b is not None])

    def by_col(value, turn):
        return permute(value, lambda y, x: y * count + (x ^ turn))

    def by_z(value, turn):
        return permute(value, lambda y, x: (y ^ (2 * turn)) * count + x)

    def by_core(value):
        return permute(value, lambda y, x: (y ^ 1) * count + x)

    def by_seam(value):
        def target(y, x):
            other = y + 1 if y % 2 else y - 1
            return other * count + x if 0 <= other < gy_count else None

        return permute(value, target)

    strip = jnp.swapaxes(cotangent, 1, 2)
    width = strip.shape[1]
    cut = cut_of(half_rows, width, half_cols)
    packed = [shape((cut + rows * SIDE * has_edge(turn), 128)) for turn in range(1, count)]
    first = call(begin, shape((16, 128)), (), flops=10**10)
    sent = call(
        functools.partial(pack_cols, count, half_cols), packed, (level_in, strip, first)
    )
    got = [by_col(value, turn + 1) for turn, value in enumerate(sent)]
    band = shape((HALO * (cols + 2 * SIDE) + 4 * span_of(half_cols), 128))
    kept, cross, inner = call(
        functools.partial(pack_rows, count, half_cols),
        [shape((3 * rows * pitch, 128)), band, band],
        (level_in, strip, *got),
        [pltpu.VMEM((count, cut, 128), F32)],
    )
    cross, inner = by_seam(cross), by_core(inner)

    wl = w_level.reshape(9, 128, 128)
    wd = w_down.reshape(512, total)
    wn = w_neck.reshape(9 * total, total)
    wfwd, wbwd, wdt, wnt = call(
        turn_weights,
        [shape((1536, 256)), shape((1536, 256)), shape((total, 512)), shape(wn.shape)],
        (wl, wd, wn),
    )
    pixels = rows * cols * count * gy_count
    used = 2 * 9 * total + 4 * 2 * 128 + 9 * 128
    part = -(-used // (2 * count * 16)) * 16
    half = part * count
    tiles = groups_of(half_rows, width) * half_cols
    sizes = (
        rows, half_rows, half_cols,
        1.0 / math.sqrt(pixels), 1.0 / math.sqrt(pixels // 4),
    )
    far = rows + 2 * HALO
    sums, send, out, grad_input = call(
        functools.partial(main, sizes),
        [shape((2 * half, 128)), shape((half, 128)), shape((half_rows * half_cols, total)), shape(level_in.shape)],
        (kept, cross, inner, wfwd, wbwd, wd, wdt, wn, wnt),
        [
            pltpu.VMEM((far, 2 * pitch + 8, 128), F32),
            pltpu.VMEM((far, pitch, 256), BF),
            pltpu.VMEM((far, pitch, 256), BF),
            pltpu.VMEM((far - 2, pitch, 256), BF),
            pltpu.VMEM((far - 2, pitch, 256), F32),
            pltpu.VMEM((3, half_rows + 6, pitch, total), BF),
            pltpu.VMEM((3, half_rows + 4, pitch, total), BF),
            pltpu.VMEM((half_rows + 4, pitch, total), BF),
            pltpu.VMEM((half_rows + 2, pitch, total), BF),
            pltpu.VMEM((rows + 4, pitch, 256), F32),
            pltpu.VMEM((rows + 4, pitch, 256), BF),
            pltpu.VMEM((rows + 4, pitch, 256), BF),
            pltpu.VMEM((rows, cols + 8, 128), F32),
        ],
        limit=20,
        flops=6 * 10**9,
    )

    pieces = call(
        functools.partial(pack_neck, count, half_rows, width), shape((count, tiles, 128)), (out,)
    )
    cut = -(-part // 32) * 16
    rest = part - cut
    units = [-(-size // (z_count * 16)) * 16 for size in (cut, rest)]
    own, *sent = call(
        functools.partial(add_cores, count, cut),
        [shape((part, 128), F32)]
        + [shape((cut, 128))] * (count - 1)
        + [shape((rest + tiles, 128))] * (count - 1),
        (sums, by_core(send), pieces),
    )
    early = [by_col(value, turn + 1) for turn, value in enumerate(sent[: count - 1])]
    late = [by_col(value, turn + 1) for turn, value in enumerate(sent[count - 1 :])]
    terms = []
    for low, size, unit, got in ((0, cut, units[0], early), (cut, rest, units[1], late)):
        first, *sent = call(
            functools.partial(add_cols, count, z_count, low, size),
            [shape((unit, 128), F32)] + [shape((unit, 128))] * (z_count - 1),
            (own, *got),
            [pltpu.VMEM((unit * z_count, 128), F32)],
        )
        terms += [first] + [by_z(value, turn) for turn, value in zip(row_turns(z_count), sent)]
    neck_out = call(
        functools.partial(place_neck, count, rest), shape(strip.shape), (pieces, *late)
    )
    own = call(functools.partial(add_rows, z_count), shape((sum(units), 128)), terms)
    own = call(
        functools.partial(join, z_count, cut, units[0]),
        shape((part, 128)),
        [own] + [by_z(own, turn) for turn in range(1, z_count)],
        [pltpu.VMEM((sum(units) * z_count, 128), BF)],
    )
    ours = [own] + [by_col(own, turn) for turn in range(1, count)]
    theirs = [by_core(value) for value in ours]
    grad_level, grad_down, grad_neck = call(
        functools.partial(finish, count),
        [shape((9, 128, 128)), shape((4, 128, total)), shape((9, total, total))],
        (*ours, *theirs),
        [pltpu.VMEM((2 * half, 128), BF)],
    )
    return (
        jnp.swapaxes(neck_out, 1, 2),
        grad_input,
        grad_level.reshape(w_level.shape),
        grad_down.reshape(w_down.shape),
        grad_neck.reshape(w_neck.shape),
    )


def solution(mesh):
    return jax.shard_map(
        local,
        mesh=mesh,
        in_specs=(P("gy", "gx", None), P(), P(), P(), P("gy", None, "gx")),
        out_specs=(P("gy", None, "gx"), P("gy", "gx", None), P(), P(), P()),
        check_vma=False,
    )
```
